512 devices in a mesh: wide: 64 (over z, x), hot: 8 (over y, core).
Axes of the slice: x: 4, y: 4, z: 16, core: 2. Of those that a mesh axis runs over, the one named last changes fastest.
Arguments:
- paper_features: bfloat16 [524288, 768], P(('wide', 'hot')), may hold values from -24 to 24
- self_weight: bfloat16 [768, 256], replicated, may hold values from -0.21875 to 0.21875
- cite_weight: bfloat16 [768, 256], replicated, may hold values from -0.21875 to 0.21875
- hot_embed: float32 [1024, 256], P('hot'), may hold values from -6 to 6
- hot_ids: int32 [524288, 8], P(('wide', 'hot')), may hold values from 0 to 1023
- tile_values: bfloat16 [16384, 128, 128], P(('wide', 'hot')), may hold values from 0 to 1, as said below
- tile_rows: int32 [16384], P(('wide', 'hot')), may hold values from 0 to 128
- tile_target_block: int32 [16384], P(('wide', 'hot')), may hold values from 0 to 7
- tile_block: int32 [16384], P(('wide', 'hot')), may hold values from 0 to 7
- tile_owner: int32 [16384], P(('wide', 'hot')), may hold values from 0 to 63, as said below
- cotangent: bfloat16 [524288, 256], P(('wide', 'hot')), may hold values from -6 to 6
Outputs:
- hidden: bfloat16 [524288, 256], P(('wide', 'hot'))
- self_grad: float32 [768, 256], P('wide')
- cite_grad: float32 [768, 256], P('wide')
- author_grad: float32 [1024, 256], P('hot')
The draws below stay inside these ranges and needn't reach their ends.
Inputs may be any that keep to these rules, and one draw needn't show every extreme that they name: Within each device's 32 tiles no value of tile_owner appears more than 1 times, and one value appears exactly 1 times. Tile rows at or past tile_rows are padding. `tile_values`: edge weights lie in [0, 1]; most entries are zero.
All inputs are finite; a program needn't handle non-finite values.
Results may differ from the reference program's by a relative error of at most 0.0059.
Values may be sent and summed in bfloat16 or wider, within the bound.
A program may use at most 128 MiB of HBM per device.

```python
import math
import jax
import jax.numpy as jnp
import numpy as np
from jax import lax

DIN = 768
FEAT = 256
TILE = 128
B_DEV = 8
HK = 8
TILES_DEV = 32
SLOT = 1
HOT = 1024
PAPERS = 524288
TILES = 16384
N_WIDE = 64
N_HOT = 8


def draw_tile_owner(key, part):
    key = jax.random.fold_in(key, 7)
    device_keys = jax.random.split(key, N_WIDE * N_HOT)

    def one_device(device_key):
        first_key, second_key, third_key = jax.random.split(device_key, 3)
        leading = jax.random.randint(first_key, (), 0, N_WIDE, dtype=jnp.int32)
        others = jnp.repeat(jnp.arange(N_WIDE - 1, dtype=jnp.int32), SLOT)
        others = others + (others >= leading).astype(jnp.int32)
        others = jax.random.permutation(second_key, others)
        kept = jnp.concatenate([jnp.full((SLOT,), leading, jnp.int32), others])[:TILES_DEV]
        return jax.random.permutation(third_key, kept)
    return jax.vmap(one_device)(device_keys).reshape(-1)


def draw_tile_values(key, part):
    key = jax.random.fold_in(key, 11)
    weight_key, keep_key = jax.random.split(key)
    shape = (TILES, TILE, TILE)
    uniform_part = jax.random.uniform(weight_key, shape, jnp.float32)
    keep = (jax.random.uniform(keep_key, shape, jnp.float32) < 0.1).astype(jnp.float32)
    weights = uniform_part
    return (keep * weights).astype(jnp.bfloat16)


def place_ends(values, rng, low, top_value):
    longest = values.shape.index(max(values.shape))
    spots = []
    for shift in (0, 1):
        where = [jax.random.randint(jax.random.fold_in(rng, axis), (), 0, length) for axis, length in enumerate(values.shape)]
        where[longest] = (where[longest] + shift) % values.shape[longest]
        spots.append(tuple(where))
    return values.at[spots[0]].set(low).at[spots[1]].set(top_value)


def spiked(drawn, stream_key, source, target, blocks, factor):
    owner, partner = [(jnp.arange(drawn.shape[dim]) // (drawn.shape[dim] // blocks)).reshape([-1 if axis == dim else 1 for axis in range(drawn.ndim)]) for dim in (source, target)]
    chosen = jax.random.permutation(stream_key, blocks)[partner]
    strong = (owner == chosen) | (owner == (partner + blocks // 2) % blocks)
    return jnp.where(strong, factor * drawn, drawn)


def level_of(own_key, extent, shards, least, top_value):
    def one(axis_at, shards_of):
        draws = jax.random.uniform(jax.random.fold_in(jax.random.fold_in(own_key, 6), axis_at), (shards_of,), jnp.float32, least / len(shards), top_value / len(shards))
        return jnp.repeat(jnp.exp(draws), extent[axis_at] // shards_of).reshape((-1,) + (1,) * (len(extent) - axis_at - 1))

    factor_of = one(*shards[0])
    for cut in shards[1:]:
        factor_of = factor_of * one(*cut)
    return factor_of


def rank_bounds(amount, skew):
    weights = [(1 << 20) // math.isqrt(grade ** skew) + 1 for grade in range(1, amount + 1)]
    width = 1 + sum(weights) // (1 << 30)
    return np.cumsum(np.array([max(1, weight // width) for weight in weights]))


def skewed_ids(rng, dims, amount, slope):
    grid = rank_bounds(amount, slope)
    ticket = jax.random.randint(jax.random.fold_in(rng, 1), dims, 0, int(grid[amount - 1]))
    standing = jnp.searchsorted(jnp.asarray(grid, jnp.int32), ticket, side="right")
    return jax.random.permutation(jax.random.fold_in(rng, 2), amount)[standing].astype(jnp.int32)


def normal_values(key, dims, width, bound, cuts=(), kind=jnp.bfloat16):
    entries = width * jax.random.normal(key, dims, jnp.float32)
    if cuts:
        entries = entries * level_of(key, dims, cuts, -0.22, 0.18)
    return jnp.clip(entries, -bound, bound).astype(kind)


def noise_with(key, extent, deviation, bound, cuts, heavy, held_as=jnp.bfloat16):
    result = deviation * jax.random.normal(key, extent, jnp.float32)
    if cuts:
        result = result * level_of(key, extent, cuts, -0.22, 0.18)
    return jnp.clip(spiked(result, jax.random.fold_in(key, 3), *heavy), -bound, bound).astype(held_as)


def setup_inputs(seed: int = 0) -> dict:
    keys = jax.random.split(jax.random.key(seed), 12)
    paper_features = noise_with(keys[0], (PAPERS, DIN), 1.0, 24.0, ((0, 512),), (0, 1, 256, 6.0))
    self_weight = normal_values(keys[1], (DIN, FEAT), DIN ** -0.5, 0.21875)
    cite_weight = normal_values(keys[2], (DIN, FEAT), DIN ** -0.5, 0.21875)
    hot_embed = normal_values(keys[3], (HOT, FEAT), 1.0, 6.0, ((0, 8),), jnp.float32)
    hot_ids = place_ends(skewed_ids(keys[4], (PAPERS, HK), HOT, 2), jax.random.fold_in(keys[4], 3), 0, HOT - 1).astype(jnp.int32)
    tile_values = draw_tile_values(jax.random.fold_in(keys[11], 71), 0)
    tile_rows = place_ends(jax.random.randint(keys[6], (TILES,), 0, TILE + 1), jax.random.fold_in(keys[6], 1), 0, TILE).astype(jnp.int32)
    tile_target_block = place_ends(jax.random.randint(keys[7], (TILES,), 0, B_DEV), jax.random.fold_in(keys[7], 1), 0, B_DEV - 1).astype(jnp.int32)
    tile_block = place_ends(jax.random.randint(keys[8], (TILES,), 0, B_DEV), jax.random.fold_in(keys[8], 1), 0, B_DEV - 1).astype(jnp.int32)
    tile_owner = draw_tile_owner(jax.random.fold_in(keys[11], 71), 0)
    cotangent = normal_values(keys[10], (PAPERS, FEAT), 1.0, 6.0, ((0, 512),))
    return {"paper_features": paper_features, "self_weight": self_weight, "cite_weight": cite_weight, "hot_embed": hot_embed, "hot_ids": hot_ids, "tile_values": tile_values, "tile_rows": tile_rows, "tile_target_block": tile_target_block, "tile_block": tile_block, "tile_owner": tile_owner, "cotangent": cotangent}


def reference(paper_features, self_weight, cite_weight, hot_embed, hot_ids, tile_values, tile_rows, tile_target_block, tile_block, tile_owner, cotangent):
    row_total = B_DEV * TILE
    self_rows = jnp.dot(paper_features, self_weight, preferred_element_type=jnp.float32)
    cite_rows = jnp.dot(paper_features, cite_weight, preferred_element_type=jnp.float32).astype(jnp.bfloat16)
    cite_blocks = cite_rows.reshape(-1, TILE, FEAT)
    feature_blocks = paper_features.reshape(-1, TILE, DIN)
    hot_table = hot_embed.astype(jnp.bfloat16).astype(jnp.float32)
    author_mix = jnp.zeros((paper_features.shape[0], FEAT), jnp.float32)
    for author_slot in range(HK):
        author_mix = author_mix + hot_table[hot_ids[:, author_slot]]
    author_mix = author_mix / HK
    positions = jnp.arange(TILE, dtype=jnp.int32)
    block_ids = jnp.arange(B_DEV, dtype=jnp.int32)

    def device_step(carry, device):
        first_tile = (device * TILES_DEV).astype(jnp.int32)
        first_row = (device * row_total).astype(jnp.int32)
        values = lax.dynamic_slice_in_dim(tile_values, first_tile, TILES_DEV, 0).astype(jnp.float32)
        used = lax.dynamic_slice_in_dim(tile_rows, first_tile, TILES_DEV, 0)
        target_block = lax.dynamic_slice_in_dim(tile_target_block, first_tile, TILES_DEV, 0)
        block = lax.dynamic_slice_in_dim(tile_block, first_tile, TILES_DEV, 0)
        owner = lax.dynamic_slice_in_dim(tile_owner, first_tile, TILES_DEV, 0)
        masked_values = jnp.where(positions[None, :, None] < used[:, None, None], values, jnp.float32(0.0))
        hot_index = device % N_HOT
        source = ((owner * N_HOT + hot_index) * B_DEV + block).astype(jnp.int32)
        sender_rows = cite_blocks[source].astype(jnp.float32)
        message_product = jnp.einsum('hpb,hbo->hpo', masked_values, sender_rows)
        target_hot_flags = (target_block[:, None] == block_ids[None, :]).astype(jnp.float32)
        summed_messages = jnp.einsum('yq,ycg->qcg', target_hot_flags, message_product)
        degree = jnp.einsum('tb,tr->br', target_hot_flags, jnp.sum(masked_values, axis=2))
        inverse = 1.0 / jnp.maximum(degree, 1.0)
        cite_mix = (summed_messages * inverse[..., None]).reshape(row_total, FEAT)
        preact = lax.dynamic_slice_in_dim(self_rows, first_row, row_total, 0) + cite_mix + lax.dynamic_slice_in_dim(author_mix, first_row, row_total, 0)
        sigmoid_pre = jax.nn.sigmoid(preact)
        hidden = (preact * sigmoid_pre).astype(jnp.bfloat16)
        cot_rows = lax.dynamic_slice_in_dim(cotangent, first_row, row_total, 0).astype(jnp.float32)
        pre_grad = (cot_rows * sigmoid_pre * (1.0 + preact * (1.0 - sigmoid_pre))).astype(jnp.bfloat16)
        scaled_messages = (pre_grad.astype(jnp.float32).reshape(B_DEV, TILE, FEAT) * inverse[..., None]).astype(jnp.bfloat16)
        backward_product = jnp.einsum('yvs,yvo->yso', masked_values, scaled_messages[target_block].astype(jnp.float32)).astype(jnp.bfloat16)
        source_feats = feature_blocks[source].astype(jnp.float32)
        carry = carry + jnp.einsum('tcd,tcf->df', source_feats, backward_product.astype(jnp.float32))
        return carry, (hidden, pre_grad)

    devices = jnp.arange(N_WIDE * N_HOT, dtype=jnp.int32)
    cite_grad, outputs = lax.scan(device_step, jnp.zeros((DIN, FEAT), jnp.float32), devices)
    hidden = outputs[0].reshape(-1, FEAT)
    pre_grad = outputs[1].reshape(-1, FEAT)
    self_grad = lax.dot_general(paper_features, pre_grad, (((0,), (0,)), ((), ())), preferred_element_type=jnp.float32)
    grad_rows = pre_grad.astype(jnp.float32)
    author_grad = jnp.zeros((HOT, FEAT), jnp.float32)
    for author_slot in range(HK):
        author_grad = author_grad + jax.ops.segment_sum(grad_rows, hot_ids[:, author_slot], num_segments=HOT)
    author_grad = author_grad / HK
    return hidden, self_grad, cite_grad, author_grad
```

```python
import functools

import jax
import jax.numpy as jnp
from jax import lax
from jax.experimental import pallas as pl
from jax.experimental.pallas import tpu as pltpu
from jax.sharding import PartitionSpec as P

HK = 8
BLOCKS = 8
NX = 4
SUBS = 4
PAD = 16
MESH = pl.DeviceIdType.MESH
F32 = jnp.float32
BF16 = jnp.bfloat16
VMEM_LIMIT = 58 * 1024 * 1024


def place(nz):
    w = lax.axis_index("wide")
    h = lax.axis_index("hot")
    return w // NX, w % NX, w, h


def greet(partners):
    barrier = pltpu.get_barrier_semaphore()
    for partner in partners:
        pl.semaphore_signal(barrier, inc=1, device_id=partner, device_id_type=MESH)
    return lambda: pl.semaphore_wait(barrier, len(partners))


def remote(src, dst, send, recv, target):
    return pltpu.make_async_remote_copy(
        src_ref=src, dst_ref=dst, send_sem=send, recv_sem=recv, device_id=target, device_id_type=MESH
    )


def forward_kernel(nz, nh, *refs):
    half = nz // 2
    (feat, w_cite, w_self, hot, ids, req) = refs[:6]
    (arrived, base, counts, table_out) = refs[6:10]
    refs = refs[10:]
    own, packed, table, asked = refs[:4]
    right = [own] + list(refs[4 : 4 + half])
    left = [own] + list(refs[4 + half : 3 + 2 * half]) + [right[half]]
    (r_send, r_recv, l_send, l_recv, x_send, x_recv, h_send, h_recv, q_send, q_recv, q_local) = refs[
        3 + 2 * half :
    ]
    z, x, w, h = place(nz)
    blocks, size, width = own.shape
    hot_rows = hot.shape[0]
    hot_total = table.shape[0]
    per = blocks // SUBS
    to_right = (lax.rem(z + 1, nz) * NX + x, h)
    to_left = (lax.rem(z + nz - 1, nz) * NX + x, h)
    x_peers = [(z * NX + lax.rem(x + d, NX), h) for d in range(1, NX)]
    h_peers = [(w, lax.rem(h + d, nh)) for d in range(1, nh)]
    wait_all = greet([to_right, to_left] + x_peers + h_peers)

    own[...] = (
        jnp.dot(feat[...], w_cite[...], preferred_element_type=F32)
        .astype(BF16)
        .reshape(blocks, size, width)
    )
    my_rows = pl.ds(pl.multiple_of(h * hot_rows, hot_rows), hot_rows)
    table[my_rows] = hot[...].astype(BF16)
    table_out[0] = req[...]
    wait_all()

    def ring(side, k, s):
        part = pl.ds(s * per, per)
        if side == "r":
            return remote(
                right[k - 1].at[part], right[k].at[part], r_send.at[k - 1, s], r_recv.at[k - 1, s], to_right
            )
        return remote(
            left[k - 1].at[part], left[k].at[part], l_send.at[k - 1, s], l_recv.at[k - 1, s], to_left
        )

    def goes(side, k, s):
        if k > half:
            return False
        return k < half or (s < SUBS // 2) == (side == "r")

    for s in range(SUBS):
        for side in "rl":
            if goes(side, 1, s):
                ring(side, 1, s).start()
    asks = []
    for d in range(1, NX):
        asks.append(
            remote(
                table_out.at[0], table_out.at[NX - d], q_send.at[d - 1], q_recv.at[NX - d - 1], x_peers[d - 1]
            )
        )
    for copy in asks:
        copy.start()
    hots = []
    for d in range(1, nh):
        hots.append(
            remote(
                table.at[my_rows], table.at[my_rows], h_send.at[d - 1], h_recv.at[nh - d - 1], h_peers[d - 1]
            )
        )
    for copy in hots:
        copy.start()
    for d in range(1, NX):
        remote(
            table_out.at[0], table_out.at[d], q_send.at[d - 1], q_recv.at[d - 1], x_peers[d - 1]
        ).wait_recv()
    local = pltpu.make_async_copy(table_out, asked, q_local)
    local.start()
    local.wait()

    def exchange(zoff, source):
        owner = lax.rem(z + zoff, nz) * NX + x
        for d in range(1, NX):
            packed[d - 1, zoff] = source[jnp.maximum(asked[d, 0, owner], 0)]
            remote(
                packed.at[d - 1, zoff],
                arrived.at[NX - d, zoff],
                x_send.at[d - 1, zoff],
                x_recv.at[NX - d - 1, zoff],
                x_peers[d - 1],
            ).start()
        arrived[0, zoff] = source[jnp.maximum(asked[0, 0, owner], 0)]

    def rows_of(i):
        rows = pl.ds(i * size, size)
        authors = lax.broadcasted_iota(jnp.int32, (size, hot_total), 1)
        many = jnp.zeros((size, hot_total), F32)
        for k in range(HK):
            many = many + jnp.where(ids[rows, k : k + 1] == authors, 1.0, 0.0)
        many = many.astype(BF16)
        counts[rows] = many
        base[rows] = jnp.dot(feat[rows], w_self[...], preferred_element_type=F32) + jnp.dot(
            many, table[...], preferred_element_type=F32
        ) * (1.0 / HK)

    exchange(0, own)
    for k in range(1, half + 1):
        for s in range(SUBS):
            for side in "rl":
                if goes(side, k, s):
                    ring(side, k, s).wait_recv()
                if goes(side, k + 1, s):
                    ring(side, k + 1, s).start()
        exchange(nz - k, right[k])
        if k < half:
            exchange(k, left[k])
        if k == 1:
            for d in range(1, nh):
                there = pl.ds(pl.multiple_of(lax.rem(h + d, nh) * hot_rows, hot_rows), hot_rows)
                remote(
                    table.at[there], table.at[there], h_send.at[d - 1], h_recv.at[d - 1], h_peers[d - 1]
                ).wait_recv()
        for i in range(blocks):
            if i * half // blocks == k - 1:
                rows_of(i)
    for zoff in range(nz):
        for d in range(1, NX):
            copy = remote(
                packed.at[d - 1, zoff],
                arrived.at[d, zoff],
                x_send.at[d - 1, zoff],
                x_recv.at[d - 1, zoff],
                x_peers[d - 1],
            )
            copy.wait_recv()
            copy.wait_send()
    for copy in asks + hots:
        copy.wait_send()
    for k in range(1, half + 1):
        for s in range(SUBS):
            for side in "rl":
                if goes(side, k, s):
                    ring(side, k, s).wait_send()


def forward(nz, nh, feat, w_cite, w_self, hot, ids, req):
    half = nz // 2
    rows, width = feat.shape[0], w_self.shape[1]
    size = rows // BLOCKS
    blocks = rows // size
    hot_total = hot.shape[0] * nh
    vmem = pl.BlockSpec(memory_space=pltpu.VMEM)
    chunk = (blocks, size, width)
    dma = pltpu.SemaphoreType.DMA
    return pl.pallas_call(
        functools.partial(forward_kernel, nz, nh),
        out_shape=(
            jax.ShapeDtypeStruct((NX, nz, size, width), BF16),
            jax.ShapeDtypeStruct((rows, width), F32),
            jax.ShapeDtypeStruct((rows, hot_total), BF16),
            jax.ShapeDtypeStruct((NX, 8, req.shape[1]), jnp.int32),
        ),
        in_specs=[vmem] * 6,
        out_specs=(vmem,) * 4,
        scratch_shapes=[
            pltpu.VMEM(chunk, BF16),
            pltpu.VMEM((NX - 1, nz, size, width), BF16),
            pltpu.VMEM((hot_total, width), BF16),
            pltpu.SMEM((NX, 8, req.shape[1]), jnp.int32),
        ]
        + [pltpu.VMEM(chunk, BF16)] * (2 * half - 1)
        + [
            dma((half, SUBS)),
            dma((half, SUBS)),
            dma((half, SUBS)),
            dma((half, SUBS)),
            dma((NX - 1, nz)),
            dma((NX - 1, nz)),
            dma((nh - 1,)),
            dma((nh - 1,)),
            dma((NX - 1,)),
            dma((NX - 1,)),
            dma,
        ],
        compiler_params=pltpu.CompilerParams(
            collective_id=1, has_side_effects=True, vmem_limit_bytes=VMEM_LIMIT
        ),
    )(feat, w_cite, w_self, hot, ids, req)


def local_kernel(
    slots, used, target, arrived, values, base, cotangent, hidden, grad, back, total, masked, scaled, inverse
):
    tiles, size, _ = values.shape
    width = base.shape[1]
    blocks = total.shape[0]
    total[...] = jnp.zeros_like(total)
    ones = jnp.ones((size, size), BF16)
    row = lax.broadcasted_iota(jnp.int32, (size, size), 0)

    def message(t, carry):
        m = jnp.where(row < used[t], values[t].astype(F32), 0.0).astype(BF16)
        masked[t] = m
        there = target[t]
        total[there, :, :width] += jnp.dot(m, arrived[slots[t]], preferred_element_type=F32)
        total[there, :, width:] += jnp.dot(m, ones, preferred_element_type=F32)
        return carry

    lax.fori_loop(0, tiles, message, 0)

    def finish(j, carry):
        rows = pl.ds(pl.multiple_of(j * size, size), size)
        inv = 1.0 / jnp.maximum(total[j, :, width : width + 1], 1.0)
        pre = base[rows] + total[j, :, :width] * inv
        s = jax.nn.sigmoid(pre)
        hidden[rows] = (pre * s).astype(BF16)
        g = (cotangent[rows].astype(F32) * s * (1.0 + pre * (1.0 - s))).astype(BF16)
        grad[rows] = g
        scaled[j] = (g.astype(F32) * inv).astype(BF16)
        return carry

    lax.fori_loop(0, blocks, finish, 0)

    def backward(t, carry):
        back[t] = lax.dot_general(
            masked[t], scaled[target[t]], (((0,), (0,)), ((), ())), preferred_element_type=F32
        ).astype(BF16)
        return carry

    lax.fori_loop(0, tiles, backward, 0)


def local_part(slots, used, target, arrived, values, base, cotangent):
    tiles, size, _ = values.shape
    rows, width = base.shape
    blocks = rows // size
    vmem = pl.BlockSpec(memory_space=pltpu.VMEM)
    smem = pl.BlockSpec(memory_space=pltpu.SMEM)
    return pl.pallas_call(
        local_kernel,
        out_shape=(
            jax.ShapeDtypeStruct((rows, width), BF16),
            jax.ShapeDtypeStruct((rows, width), BF16),
            jax.ShapeDtypeStruct((tiles, size, width), BF16),
        ),
        in_specs=[smem] * 3 + [vmem] * 4,
        out_specs=(vmem,) * 3,
        scratch_shapes=[
            pltpu.VMEM((blocks, size, width + size), F32),
            pltpu.VMEM((tiles, size, size), BF16),
            pltpu.VMEM((blocks, size, width), BF16),
            pltpu.VMEM((8, 128), F32),
        ],
        compiler_params=pltpu.CompilerParams(vmem_limit_bytes=VMEM_LIMIT),
    )(slots, used, target, arrived, values, base, cotangent)


class WeightSum:
    def __init__(self, where, nz, nh, refs):
        self.z, self.x, self.w, self.h = where
        self.nz, self.nh = nz, nh
        (self.mine, self.got1, self.mid, self.got2, self.last, self.got3, self.done) = refs[:7]
        (self.s1, self.r1, self.s2, self.r2, self.s3, self.r3, self.s4, self.r4) = refs[7:15]
        self.share = self.mine.shape[1] // NX

    @staticmethod
    def scratch(nz, nh, share, width, kind):
        dma = pltpu.SemaphoreType.DMA
        two = nz // nh
        return [
            pltpu.VMEM((nz, NX * share, width), kind),
            pltpu.VMEM((nh - 1, two, NX * share, width), kind),
            pltpu.VMEM((NX, two, PAD, width), F32),
            pltpu.VMEM((NX - 1, two, PAD, width), F32),
            pltpu.VMEM((two, PAD, width), F32),
            pltpu.VMEM((nz - 1, PAD, width), F32),
            pltpu.VMEM((PAD, width), F32),
            dma((nh - 1, two)),
            dma((nh - 1, two)),
            dma((NX - 1,)),
            dma((NX - 1,)),
            dma((two,)),
            dma((nz - 1,)),
            dma((nh - 1,)),
            dma,
        ]

    def copies1(self):
        out = []
        for d in range(1, self.nh):
            peer = lax.rem(self.h + d, self.nh)
            for i in range(self.nz // self.nh):
                e = self.nh - d - 1
                out.append(
                    remote(
                        self.mine.at[peer + i * self.nh],
                        self.got1.at[e, i],
                        self.s1.at[d - 1, i],
                        self.r1.at[e, i],
                        (self.w, peer),
                    )
                )
        return out

    def copies2(self):
        out = []
        for d in range(1, NX):
            peer = lax.rem(self.x + d, NX)
            e = NX - d - 1
            out.append(
                remote(
                    self.mid.at[peer],
                    self.got2.at[e],
                    self.s2.at[d - 1],
                    self.r2.at[e],
                    (self.z * NX + peer, self.h),
                )
            )
        return out

    def each3(self, act):
        for i in range(self.nz // self.nh):
            there = self.h + i * self.nh
            off = lax.rem(self.z - there + self.nz, self.nz)

            @pl.when(off != 0)
            def _():
                act(
                    remote(
                        self.last.at[i],
                        self.got3.at[off - 1],
                        self.s3.at[i],
                        self.r3.at[off - 1],
                        (there * NX + self.x, self.h),
                    )
                )

    def copies4(self):
        return [
            remote(
                self.done, self.done, self.s4.at[d - 1], self.r4, (self.w, lax.rem(self.h + d, self.nh))
            )
            for d in range(1, self.nh)
        ]

    def stage1(self):
        for copy in self.copies1():
            copy.start()

    def stage2(self):
        self.mid[...] = jnp.zeros_like(self.mid)
        for copy in self.copies1():
            copy.wait_recv()
        for i in range(self.nz // self.nh):
            sums = self.mine[self.h + i * self.nh].astype(F32)
            for e in range(self.nh - 1):
                sums = sums + self.got1[e, i].astype(F32)
            for peer in range(NX):
                self.mid[peer, i, : self.share] = sums[peer * self.share : (peer + 1) * self.share]
        for copy in self.copies2():
            copy.start()

    def stage3(self):
        for copy in self.copies2():
            copy.wait_recv()
        sums = self.mid[self.x]
        for e in range(NX - 1):
            sums = sums + self.got2[e]
        self.last[...] = sums
        self.each3(lambda copy: copy.start())

    def stage4(self):
        @pl.when(lax.rem(self.z, self.nh) == self.h)
        def _():
            for o in range(self.nz - 1):
                remote(
                    self.last.at[0], self.got3.at[o], self.s3.at[0], self.r3.at[o], (self.w, self.h)
                ).wait_recv()
            sums = self.last[self.z // self.nh]
            for o in range(self.nz - 1):
                sums = sums + self.got3[o]
            self.done[...] = sums
            for copy in self.copies4():
                copy.start()

    def finish(self, out):
        @pl.when(lax.rem(self.z, self.nh) != self.h)
        def _():
            self.copies4()[0].wait_recv()

        out[...] = self.done[: self.share]

    def drain(self):
        for copy in self.copies1() + self.copies2():
            copy.wait_send()
        self.each3(lambda copy: copy.wait_send())

        @pl.when(lax.rem(self.z, self.nh) == self.h)
        def _():
            for copy in self.copies4():
                copy.wait_send()


class AuthorSum:
    def __init__(self, where, nz, nh, refs):
        self.z, self.x, self.w, self.h = where
        self.nz, self.nh, self.np = nz, nh, nz // 2
        (self.mine, self.got1, self.mid, self.got2, self.cut, self.got3, self.sums4, self.rows5) = refs[:8]
        (self.s1, self.r1, self.s2, self.r2, self.s3, self.r3, self.s4, self.r4, self.s5, self.r5) = refs[8:18]

    @staticmethod
    def scratch(nz, nh, rows, width):
        dma = pltpu.SemaphoreType.DMA
        part = rows // NX
        pieces = nz // 2
        return [
            pltpu.VMEM((nh, rows, width), F32),
            pltpu.VMEM((nh - 1, rows, width), F32),
            pltpu.VMEM((NX, part, width), F32),
            pltpu.VMEM((NX - 1, part, width), F32),
            pltpu.VMEM((pieces, 8, width // 2), F32),
            pltpu.VMEM((nz - 1, 8, width // 2), F32),
            pltpu.VMEM((pieces, 8, width // 2), F32),
            pltpu.VMEM((NX, part, width), F32),
            dma((nh - 1,)),
            dma((nh - 1,)),
            dma((NX - 1,)),
            dma((NX - 1,)),
            dma((nz - 1,)),
            dma((nz - 1,)),
            dma((pieces - 1,)),
            dma((pieces - 1,)),
            dma((NX - 1,)),
            dma((NX - 1,)),
        ]

    def copies1(self):
        out = []
        for d in range(1, self.nh):
            peer = lax.rem(self.h + d, self.nh)
            e = self.nh - d - 1
            out.append(
                remote(self.mine.at[peer], self.got1.at[e], self.s1.at[d - 1], self.r1.at[e], (self.w, peer))
            )
        return out

    def copies2(self):
        out = []
        for d in range(1, NX):
            peer = lax.rem(self.x + d, NX)
            e = NX - d - 1
            to = (self.z * NX + peer, self.h)
            out.append(remote(self.mid.at[peer], self.got2.at[e], self.s2.at[d - 1], self.r2.at[e], to))
        return out

    def copies3(self):
        out = []
        for d in range(1, self.nz):
            peer = lax.rem(self.z + d, self.nz)
            e = self.nz - d - 1
            to = (peer * NX + self.x, self.h)
            out.append(
                remote(
                    self.cut.at[lax.rem(peer, self.np)], self.got3.at[e], self.s3.at[d - 1], self.r3.at[e], to
                )
            )
        return out

    def copies4(self, coming=False):
        out = []
        p = lax.rem(self.z, self.np)
        for d in range(1, self.np):
            other = lax.rem(p + d, self.np)
            to = ((self.z - p + other) * NX + self.x, self.h)
            e = d - 1 if coming else self.np - d - 1
            piece = self.sums4.at[other if coming else p]
            out.append(remote(piece, piece, self.s4.at[d - 1], self.r4.at[e], to))
        return out

    def copies5(self, coming=False):
        out = []
        for d in range(1, NX):
            peer = lax.rem(self.x + d, NX)
            e = d - 1 if coming else NX - d - 1
            rows = self.rows5.at[peer if coming else self.x]
            out.append(remote(rows, rows, self.s5.at[d - 1], self.r5.at[e], (self.z * NX + peer, self.h)))
        return out

    def stage1(self):
        for copy in self.copies1():
            copy.start()

    def stage2(self):
        for copy in self.copies1():
            copy.wait_recv()
        sums = self.mine[self.h]
        for e in range(self.nh - 1):
            sums = sums + self.got1[e]
        self.mid[...] = sums.reshape(self.mid.shape)
        for copy in self.copies2():
            copy.start()

    def stage3(self):
        for copy in self.copies2():
            copy.wait_recv()
        sums = self.mid[self.x]
        for e in range(NX - 1):
            sums = sums + self.got2[e]
        lanes = self.cut.shape[2]
        for p in range(self.np):
            g, c = p // 2, p % 2
            self.cut[p] = sums[g * 8 : (g + 1) * 8, c * lanes : (c + 1) * lanes]
        for copy in self.copies3():
            copy.start()

    def stage4(self):
        for copy in self.copies3():
            copy.wait_recv()
        p = lax.rem(self.z, self.np)
        sums = self.cut[p]
        for e in range(self.nz - 1):
            sums = sums + self.got3[e]
        self.sums4[p] = sums
        for copy in self.copies4():
            copy.start()

    def stage5(self):
        for copy in self.copies4(True):
            copy.wait_recv()
        lanes = self.cut.shape[2]
        for p in range(self.np):
            g, c = p // 2, p % 2
            self.rows5[self.x, g * 8 : (g + 1) * 8, c * lanes : (c + 1) * lanes] = self.sums4[p]
        for copy in self.copies5():
            copy.start()

    def finish(self, out):
        for copy in self.copies5(True):
            copy.wait_recv()
        out[...] = self.rows5[...].reshape(out.shape)

    def drain(self):
        for copy in self.copies1() + self.copies2() + self.copies3() + self.copies4() + self.copies5():
            copy.wait_send()


def backward_kernel(nz, nh, *refs):
    half = nz // 2
    (tile_at, asked, back, feat, counts, grad) = refs[:6]
    (self_out, cite_out, author_out) = refs[6:9]
    refs = list(refs[9:])
    packed, came, far, near = refs[:4]
    refs = refs[4:]
    right, left = refs[:half], refs[half : 2 * half]
    (r_send, r_recv, l_send, l_recv, x_send, x_recv) = refs[2 * half : 2 * half + 6]
    refs = refs[2 * half + 6 :]
    where = place(nz)
    z, x, w, h = where
    selfs = WeightSum(where, nz, nh, refs[:15])
    cites = WeightSum(where, nz, nh, refs[15:30])
    authors = AuthorSum(where, nz, nh, refs[30:48])
    blocks, size, width = far.shape
    per = blocks // SUBS
    to_right = (lax.rem(z + 1, nz) * NX + x, h)
    to_left = (lax.rem(z + nz - 1, nz) * NX + x, h)
    z_peers = [(lax.rem(z + d, nz) * NX + x, h) for d in range(1, nz)]
    x_peers = [(z * NX + lax.rem(x + d, NX), h) for d in range(1, NX)]
    h_peers = [(w, lax.rem(h + d, nh)) for d in range(1, nh)]
    greet(z_peers + x_peers + h_peers)()

    def exchange(zoff):
        there = lax.rem(z + zoff, nz) * NX
        out = []
        for d in range(1, NX):
            packed[d - 1, zoff] = back[tile_at[there + lax.rem(x + d, NX)]]
            remote(
                packed.at[d - 1, zoff],
                came.at[NX - d - 1, zoff],
                x_send.at[d - 1, zoff],
                x_recv.at[NX - d - 1, zoff],
                x_peers[d - 1],
            ).start()

    def exchanged(zoff, what):
        for d in range(1, NX):
            copy = remote(
                packed.at[d - 1, zoff],
                came.at[d - 1, zoff],
                x_send.at[d - 1, zoff],
                x_recv.at[d - 1, zoff],
                x_peers[d - 1],
            )
            what(copy)

    step_rows = min(size, 32)

    def add_local(dst, sources, s, zoff):
        owner = lax.rem(z + zoff, nz) * NX + x
        wanted = [asked[d, 0, owner] for d in range(NX)]
        mine = tile_at[owner]

        def body(i, carry):
            rows = pl.ds(pl.multiple_of(i * step_rows, step_rows), step_rows)
            terms = [back[mine, rows].astype(F32)]
            for d in range(1, NX):
                terms.append(came[d - 1, zoff, rows].astype(F32))
            for j in range(s * per, (s + 1) * per):
                total = None
                for d in range(NX):
                    term = jnp.where(wanted[d] == j, terms[d], 0.0)
                    total = term if total is None else total + term
                for source in sources:
                    total = total + source[j, rows].astype(F32)
                dst[j, rows] = total.astype(BF16)
            return carry

        lax.fori_loop(0, size // step_rows, body, 0)

    def ring(side, k, s):
        part = pl.ds(s * per, per)
        bufs, send, recv, to = (
            (right, r_send, r_recv, to_right) if side == "r" else (left, l_send, l_recv, to_left)
        )
        src = far if k == half else bufs[k]
        return remote(src.at[part], bufs[k - 1].at[part], send.at[k - 1, s], recv.at[k - 1, s], to)

    def goes(side, k, s):
        return k < half or (s < SUBS // 2) == (side == "r")

    def product(lhs, rhs, put, step):
        def body(i, carry):
            at = pl.multiple_of(i * step, step)
            put(
                at,
                lax.dot_general(
                    lhs[:, pl.ds(at, step)], rhs[...], (((0,), (0,)), ((), ())), preferred_element_type=F32
                ),
            )
            return carry

        lax.fori_loop(0, lhs.shape[1] // step, body, 0)

    def put_weight(dest):
        group = dest.mine.shape[1]

        def put(at, value):
            first = at // group
            for i in range(value.shape[0] // group):
                dest.mine[first + i] = value[i * group : (i + 1) * group].astype(dest.mine.dtype)

        return put

    group = selfs.mine.shape[1]
    weight_step = group * 8 if feat.shape[1] % 128 == 0 else feat.shape[1]

    def put_author(at, value):
        rows = authors.mine.shape[1]
        for i in range(value.shape[0] // rows):
            authors.mine[at // rows + i] = value[i * rows : (i + 1) * rows] * (1.0 / HK)

    author_step = min(counts.shape[1], 256)

    def self_start():
        product(feat, grad, put_weight(selfs), weight_step)
        selfs.stage1()

    def author_start():
        product(counts, grad, put_author, author_step)
        authors.stage1()

    extras = [
        self_start,
        author_start,
        selfs.stage2,
        authors.stage2,
        selfs.stage3,
        authors.stage3,
        selfs.stage4,
        authors.stage4,
        authors.stage5,
        lambda: selfs.finish(self_out),
        lambda: authors.finish(author_out),
    ]

    exchange(half)
    exchange(half - 1)
    exchange(half + 1)
    for k in range(half, 0, -1):
        exchanged(k, lambda copy: copy.wait_recv())
        if k < half:
            exchanged(nz - k, lambda copy: copy.wait_recv())
        for s in range(SUBS):
            for side in "rl":
                if not goes(side, k, s):
                    continue
                bufs = right if side == "r" else left
                zoff = k if side == "r" else nz - k
                sources = []
                if k < half and goes(side, k + 1, s):
                    ring(side, k + 1, s).wait_recv()
                    sources = [bufs[k]]
                add_local(far if k == half else bufs[k], sources, s, zoff)
                ring(side, k, s).start()
        if k >= 2:
            exchange(k - 2)
            if k - 2 > 0:
                exchange(nz - k + 2)
        first = (half - k) * len(extras) // half
        last = (half - k + 1) * len(extras) // half
        for extra in extras[first:last]:
            extra()
    exchanged(0, lambda copy: copy.wait_recv())
    for s in range(SUBS):
        ring("r", 1, s).wait_recv()
        ring("l", 1, s).wait_recv()
        add_local(near, [right[0], left[0]], s, 0)

    def near_rows(at, step):
        return feat[:, pl.ds(at, step)]

    flat = near[...].reshape(blocks * size, width)

    def cite_body(i, carry):
        at = pl.multiple_of(i * weight_step, weight_step)
        put_weight(cites)(
            at,
            lax.dot_general(
                feat[:, pl.ds(at, weight_step)], flat, (((0,), (0,)), ((), ())), preferred_element_type=F32
            ),
        )
        return carry

    lax.fori_loop(0, feat.shape[1] // weight_step, cite_body, 0)
    cites.stage1()
    cites.stage2()
    cites.stage3()
    cites.stage4()
    for zoff in range(nz):
        exchanged(zoff, lambda copy: copy.wait_send())
    for k in range(half, 0, -1):
        for s in range(SUBS):
            for side in "rl":
                if goes(side, k, s):
                    ring(side, k, s).wait_send()
    selfs.drain()
    authors.drain()
    cites.finish(cite_out)
    cites.drain()


def backward(nz, nh, tile_at, asked, back, feat, counts, grad, share, hot_rows):
    half = nz // 2
    _, size, width = back.shape
    rows = feat.shape[0]
    chunk = (rows // size, size, width)
    vmem = pl.BlockSpec(memory_space=pltpu.VMEM)
    smem = pl.BlockSpec(memory_space=pltpu.SMEM)
    dma = pltpu.SemaphoreType.DMA
    return pl.pallas_call(
        functools.partial(backward_kernel, nz, nh),
        out_shape=(
            jax.ShapeDtypeStruct((share, width), F32),
            jax.ShapeDtypeStruct((share, width), F32),
            jax.ShapeDtypeStruct((hot_rows, width), F32),
        ),
        in_specs=[smem] * 2 + [vmem] * 4,
        out_specs=(vmem,) * 3,
        scratch_shapes=[
            pltpu.VMEM((NX - 1, nz, size, width), BF16),
            pltpu.VMEM((NX - 1, nz, size, width), BF16),
            pltpu.VMEM(chunk, BF16),
            pltpu.VMEM(chunk, BF16),
        ]
        + [pltpu.VMEM(chunk, BF16)] * (2 * half)
        + [
            dma((half, SUBS)),
            dma((half, SUBS)),
            dma((half, SUBS)),
            dma((half, SUBS)),
            dma((NX - 1, nz)),
            dma((NX - 1, nz)),
        ]
        + WeightSum.scratch(nz, nh, share, width, F32)
        + WeightSum.scratch(nz, nh, share, width, BF16)
        + AuthorSum.scratch(nz, nh, hot_rows, width),
        compiler_params=pltpu.CompilerParams(
            collective_id=2, has_side_effects=True, vmem_limit_bytes=VMEM_LIMIT
        ),
    )(tile_at, asked, back, feat, counts, grad)


def on_device(
    paper_features,
    self_weight,
    cite_weight,
    hot_embed,
    hot_ids,
    tile_values,
    tile_rows,
    tile_target_block,
    tile_block,
    tile_owner,
    cotangent,
):
    wide = lax.axis_size("wide")
    nh = lax.axis_size("hot")
    nz = wide // NX
    tiles = tile_values.shape[0]
    z, x, _, _ = place(nz)
    lanes = max(128, wide)
    owners = jnp.arange(lanes, dtype=jnp.int32)
    owned = tile_owner[:, None] == owners[None, :]
    numbers = jnp.arange(tiles, dtype=jnp.int32)
    wanted = jnp.max(jnp.where(owned, tile_block[:, None], -1), axis=0)
    tile_at = jnp.max(jnp.where(owned, numbers[:, None], 0), axis=0)
    req = jnp.broadcast_to(wanted[None, :], (8, lanes))
    slots = ((tile_owner % NX - x) % NX) * nz + (tile_owner // NX - z) % nz
    arrived, base, counts, asked = forward(
        nz, nh, paper_features, cite_weight, self_weight, hot_embed, hot_ids, req
    )
    _, _, size, width = arrived.shape
    hidden, grad, back = local_part(
        slots,
        tile_rows,
        tile_target_block,
        arrived.reshape(NX * nz, size, width),
        tile_values,
        base,
        cotangent,
    )
    self_grad, cite_grad, author_grad = backward(
        nz,
        nh,
        tile_at,
        asked,
        back,
        paper_features,
        counts,
        grad,
        self_weight.shape[0] // wide,
        hot_embed.shape[0],
    )
    return hidden, self_grad, cite_grad, author_grad


def solution(mesh):
    return jax.shard_map(
        on_device,
        mesh=mesh,
        in_specs=(
            P(("wide", "hot"), None),
            P(),
            P(),
            P("hot", None),
            P(("wide", "hot"), None),
            P(("wide", "hot"), None, None),
            P(("wide", "hot")),
            P(("wide", "hot")),
            P(("wide", "hot")),
            P(("wide", "hot")),
            P(("wide", "hot"), None),
        ),
        out_specs=(P(("wide", "hot"), None), P("wide", None), P("wide", None), P("hot", None)),
        check_vma=False,
    )
```

```python
import functools

import jax
import jax.numpy as jnp
from jax import lax
from jax.experimental import pallas as pl
from jax.experimental.pallas import tpu as pltpu
from jax.sharding import PartitionSpec as P

HK = 8
NX = 4
SUBS = 4
PAD = 16
MESH = pl.DeviceIdType.MESH
F32 = jnp.float32
BF16 = jnp.bfloat16
VMEM_LIMIT = 58 * 1024 * 1024


def place(nz):
    w = lax.axis_index("wide")
    h = lax.axis_index("hot")
    return w // NX, w % NX, w, h


def greet(partners):
    barrier = pltpu.get_barrier_semaphore()
    for partner in partners:
        pl.semaphore_signal(barrier, inc=1, device_id=partner, device_id_type=MESH)
    return lambda: pl.semaphore_wait(barrier, len(partners))


def remote(src, dst, send, recv, target):
    return pltpu.make_async_remote_copy(
        src_ref=src, dst_ref=dst, send_sem=send, recv_sem=recv, device_id=target, device_id_type=MESH
    )


class WeightSum:
    def __init__(self, where, nz, nh, refs):
        self.z, self.x, self.w, self.h = where
        self.nz, self.nh = nz, nh
        (self.mine, self.got1, self.mid, self.got2, self.last, self.got3, self.done) = refs[:7]
        (self.s1, self.r1, self.s2, self.r2, self.s3, self.r3, self.s4, self.r4) = refs[7:15]
        self.share = self.mine.shape[1] // NX

    @staticmethod
    def scratch(nz, nh, share, width, kind):
        dma = pltpu.SemaphoreType.DMA
        two = nz // nh
        return [
            pltpu.VMEM((nz, NX * share, width), kind),
            pltpu.VMEM((nh - 1, two, NX * share, width), kind),
            pltpu.VMEM((NX, two, PAD, width), F32),
            pltpu.VMEM((NX - 1, two, PAD, width), F32),
            pltpu.VMEM((two, PAD, width), F32),
            pltpu.VMEM((nz - 1, PAD, width), F32),
            pltpu.VMEM((PAD, width), F32),
            dma((nh - 1, two)),
            dma((nh - 1, two)),
            dma((NX - 1,)),
            dma((NX - 1,)),
            dma((two,)),
            dma((nz - 1,)),
            dma((nh - 1,)),
            dma,
        ]

    def copies1(self):
        out = []
        for d in range(1, self.nh):
            peer = lax.rem(self.h + d, self.nh)
            for i in range(self.nz // self.nh):
                e = self.nh - d - 1
                out.append(
                    remote(
                        self.mine.at[peer + i * self.nh],
                        self.got1.at[e, i],
                        self.s1.at[d - 1, i],
                        self.r1.at[e, i],
                        (self.w, peer),
                    )
                )
        return out

    def copies2(self):
        out = []
        for d in range(1, NX):
            peer = lax.rem(self.x + d, NX)
            e = NX - d - 1
            out.append(
                remote(
                    self.mid.at[peer],
                    self.got2.at[e],
                    self.s2.at[d - 1],
                    self.r2.at[e],
                    (self.z * NX + peer, self.h),
                )
            )
        return out

    def each3(self, act):
        for i in range(self.nz // self.nh):
            there = self.h + i * self.nh
            off = lax.rem(self.z - there + self.nz, self.nz)

            @pl.when(off != 0)
            def _():
                act(
                    remote(
                        self.last.at[i],
                        self.got3.at[off - 1],
                        self.s3.at[i],
                        self.r3.at[off - 1],
                        (there * NX + self.x, self.h),
                    )
                )

    def copies4(self):
        return [
            remote(
                self.done, self.done, self.s4.at[d - 1], self.r4, (self.w, lax.rem(self.h + d, self.nh))
            )
            for d in range(1, self.nh)
        ]

    def stage1(self):
        for copy in self.copies1():
            copy.start()

    def stage2(self):
        self.mid[...] = jnp.zeros_like(self.mid)
        for copy in self.copies1():
            copy.wait_recv()
        for i in range(self.nz // self.nh):
            sums = self.mine[self.h + i * self.nh].astype(F32)
            for e in range(self.nh - 1):
                sums = sums + self.got1[e, i].astype(F32)
            for peer in range(NX):
                self.mid[peer, i, : self.share] = sums[peer * self.share : (peer + 1) * self.share]
        for copy in self.copies2():
            copy.start()

    def stage3(self):
        for copy in self.copies2():
            copy.wait_recv()
        sums = self.mid[self.x]
        for e in range(NX - 1):
            sums = sums + self.got2[e]
        self.last[...] = sums
        self.each3(lambda copy: copy.start())

    def stage4(self):
        @pl.when(lax.rem(self.z, self.nh) == self.h)
        def _():
            for o in range(self.nz - 1):
                remote(
                    self.last.at[0], self.got3.at[o], self.s3.at[0], self.r3.at[o], (self.w, self.h)
                ).wait_recv()
            sums = self.last[self.z // self.nh]
            for o in range(self.nz - 1):
                sums = sums + self.got3[o]
            self.done[...] = sums
            for copy in self.copies4():
                copy.start()

    def finish(self, out):
        @pl.when(lax.rem(self.z, self.nh) != self.h)
        def _():
            self.copies4()[0].wait_recv()

        out[...] = self.done[: self.share]

    def drain(self):
        for copy in self.copies1() + self.copies2():
            copy.wait_send()
        self.each3(lambda copy: copy.wait_send())

        @pl.when(lax.rem(self.z, self.nh) == self.h)
        def _():
            for copy in self.copies4():
                copy.wait_send()


class AuthorSum:
    def __init__(self, where, nz, nh, refs):
        self.z, self.x, self.w, self.h = where
        self.nz, self.nh, self.np = nz, nh, nz // 2
        (self.mine, self.got1, self.mid, self.got2, self.cut, self.got3, self.sums4, self.rows5) = refs[:8]
        (self.s1, self.r1, self.s2, self.r2, self.s3, self.r3, self.s4, self.r4, self.s5, self.r5) = refs[8:18]

    @staticmethod
    def scratch(nz, nh, rows, width):
        dma = pltpu.SemaphoreType.DMA
        part = rows // NX
        pieces = nz // 2
        return [
            pltpu.VMEM((nh, rows, width), F32),
            pltpu.VMEM((nh - 1, rows, width), F32),
            pltpu.VMEM((NX, part, width), F32),
            pltpu.VMEM((NX - 1, part, width), F32),
            pltpu.VMEM((pieces, 8, width // 2), F32),
            pltpu.VMEM((nz - 1, 8, width // 2), F32),
            pltpu.VMEM((pieces, 8, width // 2), F32),
            pltpu.VMEM((NX, part, width), F32),
            dma((nh - 1,)),
            dma((nh - 1,)),
            dma((NX - 1,)),
            dma((NX - 1,)),
            dma((nz - 1,)),
            dma((nz - 1,)),
            dma((pieces - 1,)),
            dma((pieces - 1,)),
            dma((NX - 1,)),
            dma((NX - 1,)),
        ]

    def copies1(self):
        out = []
        for d in range(1, self.nh):
            peer = lax.rem(self.h + d, self.nh)
            e = self.nh - d - 1
            out.append(
                remote(self.mine.at[peer], self.got1.at[e], self.s1.at[d - 1], self.r1.at[e], (self.w, peer))
            )
        return out

    def copies2(self):
        out = []
        for d in range(1, NX):
            peer = lax.rem(self.x + d, NX)
            e = NX - d - 1
            to = (self.z * NX + peer, self.h)
            out.append(remote(self.mid.at[peer], self.got2.at[e], self.s2.at[d - 1], self.r2.at[e], to))
        return out

    def copies3(self):
        out = []
        for d in range(1, self.nz):
            peer = lax.rem(self.z + d, self.nz)
            e = self.nz - d - 1
            to = (peer * NX + self.x, self.h)
            out.append(
                remote(
                    self.cut.at[lax.rem(peer, self.np)], self.got3.at[e], self.s3.at[d - 1], self.r3.at[e], to
                )
            )
        return out

    def copies4(self, coming=False):
        out = []
        p = lax.rem(self.z, self.np)
        for d in range(1, self.np):
            other = lax.rem(p + d, self.np)
            to = ((self.z - p + other) * NX + self.x, self.h)
            e = d - 1 if coming else self.np - d - 1
            piece = self.sums4.at[other if coming else p]
            out.append(remote(piece, piece, self.s4.at[d - 1], self.r4.at[e], to))
        return out

    def copies5(self, coming=False):
        out = []
        for d in range(1, NX):
            peer = lax.rem(self.x + d, NX)
            e = d - 1 if coming else NX - d - 1
            rows = self.rows5.at[peer if coming else self.x]
            out.append(remote(rows, rows, self.s5.at[d - 1], self.r5.at[e], (self.z * NX + peer, self.h)))
        return out

    def stage1(self):
        for copy in self.copies1():
            copy.start()

    def stage2(self):
        for copy in self.copies1():
            copy.wait_recv()
        sums = self.mine[self.h]
        for e in range(self.nh - 1):
            sums = sums + self.got1[e]
        self.mid[...] = sums.reshape(self.mid.shape)
        for copy in self.copies2():
            copy.start()

    def stage3(self):
        for copy in self.copies2():
            copy.wait_recv()
        sums = self.mid[self.x]
        for e in range(NX - 1):
            sums = sums + self.got2[e]
        lanes = self.cut.shape[2]
        for p in range(self.np):
            g, c = p // 2, p % 2
            self.cut[p] = sums[g * 8 : (g + 1) * 8, c * lanes : (c + 1) * lanes]
        for copy in self.copies3():
            copy.start()

    def stage4(self):
        for copy in self.copies3():
            copy.wait_recv()
        p = lax.rem(self.z, self.np)
        sums = self.cut[p]
        for e in range(self.nz - 1):
            sums = sums + self.got3[e]
        self.sums4[p] = sums
        for copy in self.copies4():
            copy.start()

    def stage5(self):
        for copy in self.copies4(True):
            copy.wait_recv()
        lanes = self.cut.shape[2]
        for p in range(self.np):
            g, c = p // 2, p % 2
            self.rows5[self.x, g * 8 : (g + 1) * 8, c * lanes : (c + 1) * lanes] = self.sums4[p]
        for copy in self.copies5():
            copy.start()

    def finish(self, out):
        for copy in self.copies5(True):
            copy.wait_recv()
        out[...] = self.rows5[...].reshape(out.shape)

    def drain(self):
        for copy in self.copies1() + self.copies2() + self.copies3() + self.copies4() + self.copies5():
            copy.wait_send()


def layer_kernel(names, nz, nh, *refs):
    r = dict(zip(names, refs))
    half = nz // 2
    feat, w_cite, w_self, hot, ids, req, values, cotangent, used, target = refs[:10]
    hidden, self_out, cite_out, author_out = refs[10:14]
    own, packed, table, asks, asked, arrived = (
        r[n] for n in ("own", "packed", "table", "asks", "asked", "arrived")
    )
    spread, turned, counts, feat_t, base, total, grad, scaled = (
        r[n] for n in ("spread", "turned", "counts", "feat_t", "base", "total", "grad", "scaled")
    )
    where = place(nz)
    z, x, w, h = where
    selfs = WeightSum(where, nz, nh, [r["self%d" % i] for i in range(15)])
    cites = WeightSum(where, nz, nh, [r["cite%d" % i] for i in range(15)])
    authors = AuthorSum(where, nz, nh, [r["author%d" % i] for i in range(18)])
    blocks, size, width = own.shape
    hot_rows = hot.shape[0]
    hot_total = table.shape[0]
    per = blocks // SUBS
    to_right = (lax.rem(z + 1, nz) * NX + x, h)
    to_left = (lax.rem(z + nz - 1, nz) * NX + x, h)
    z_peers = [(lax.rem(z + d, nz) * NX + x, h) for d in range(1, nz)]
    x_peers = [(z * NX + lax.rem(x + d, NX), h) for d in range(1, NX)]
    h_peers = [(w, lax.rem(h + d, nh)) for d in range(1, nh)]
    wait_all = greet(z_peers + x_peers + h_peers)

    my_rows = pl.ds(pl.multiple_of(h * hot_rows, hot_rows), hot_rows)
    table[my_rows] = hot[...].astype(BF16)
    asks[0] = req[...]

    def spot(zoff):
        if zoff == 0:
            return 0
        return 2 * zoff if zoff < half else 2 * (nz - zoff) - 1

    def offsets(k):
        return [0] if k == 0 else [half] if k == half else [nz - k, k]

    f_right = [own] + [r["f_right%d" % k] for k in range(1, half + 1)]
    f_left = [own] + [r["f_left%d" % k] for k in range(1, half)] + [f_right[half]]
    rows_f32 = lax.broadcasted_iota(jnp.int32, (size, size), 0)

    def goes(side, k, s):
        if k > half:
            return False
        return k < half or (s < SUBS // 2) == (side == "r")

    def f_ring(side, k, s):
        part = pl.ds(s * per, per)
        bufs, to = (f_right, to_right) if side == "r" else (f_left, to_left)
        return remote(
            bufs[k - 1].at[part],
            bufs[k].at[part],
            r["fs_" + side].at[k - 1, s],
            r["fr_" + side].at[k - 1, s],
            to,
        )

    wait_all()
    for s in range(SUBS):
        rows = pl.ds(s * per * size, per * size)
        own[s * per : (s + 1) * per] = (
            jnp.dot(feat[rows], w_cite[...], preferred_element_type=F32)
            .astype(BF16)
            .reshape(per, size, width)
        )
        for side in "rl":
            if goes(side, 1, s):
                f_ring(side, 1, s).start()

    def ask_copies(coming):
        return [
            remote(
                asks.at[0],
                asks.at[d if coming else NX - d],
                r["q_send"].at[d - 1],
                r["q_recv"].at[d - 1 if coming else NX - d - 1],
                x_peers[d - 1],
            )
            for d in range(1, NX)
        ]

    def hot_copies(coming):
        out = []
        for d in range(1, nh):
            peer = lax.rem(h + d, nh) if coming else h
            rows = table.at[pl.ds(pl.multiple_of(peer * hot_rows, hot_rows), hot_rows)]
            e = d - 1 if coming else nh - d - 1
            out.append(remote(rows, rows, r["h_send"].at[d - 1], r["h_recv"].at[e], h_peers[d - 1]))
        return out

    for copy in ask_copies(False) + hot_copies(False):
        copy.start()
    for copy in ask_copies(True):
        copy.wait_recv()
    local = pltpu.make_async_copy(asks, asked, r["q_local"])
    local.start()
    local.wait()

    def owner_at(zoff, d):
        return lax.rem(z + zoff, nz) * NX + lax.rem(x + d, NX)

    def f_copy(zoff, d, coming):
        return remote(
            packed.at[d - 1, zoff],
            arrived.at[spot(zoff), d if coming else NX - d],
            r["fx_send"].at[d - 1, zoff],
            r["fx_recv"].at[d - 1 if coming else NX - d - 1, zoff],
            x_peers[d - 1],
        )

    def f_exchange(zoff, source):
        owner = owner_at(zoff, 0)
        for d in range(1, NX):
            packed[d - 1, zoff] = source[jnp.maximum(asked[d, 0, owner], 0)]
            f_copy(zoff, d, False).start()
        arrived[spot(zoff), 0] = source[jnp.maximum(asked[0, 0, owner], 0)]

    def tile_of(zoff, d):
        t = asked[0, 1, owner_at(zoff, d)]
        number = jnp.maximum(t, 0)
        return values[number].astype(F32), jnp.where(t < 0, 0, used[number]), target[number]

    def prepare(k):
        held = spread.at[k % 2]
        n = 0
        for zoff in offsets(k):
            for d in range(NX):
                m, live, block = tile_of(zoff, d)
                turned[spot(zoff), d] = jnp.where(rows_f32 < live, m, 0.0).T.astype(BF16)

                def lay(j, carry, m=m, live=live, block=block, n=n):
                    there = jnp.where(block == j, live, 0)
                    rows = pl.ds(pl.multiple_of(j * size, size), size)
                    held[rows, n * size : (n + 1) * size] = jnp.where(rows_f32 < there, m, 0.0).astype(BF16)
                    return carry

                lax.fori_loop(0, blocks, lay, 0)
                n += 1
        ones = jnp.ones((n * size, size), BF16)

        def degrees(j, carry):
            rows = pl.ds(pl.multiple_of(j * size, size), size)
            more = jnp.dot(held[rows, : n * size], ones, preferred_element_type=F32)
            total[rows, width:] = more if k == 0 else total[rows, width:] + more
            return carry

        lax.fori_loop(0, blocks, degrees, 0)

    def messages(k):
        for zoff in offsets(k):
            for d in range(1, NX):
                f_copy(zoff, d, True).wait_recv()
        first = spot(offsets(k)[0])
        count = len(offsets(k))
        span = count * NX * size

        def gather(j, carry):
            rows = pl.ds(pl.multiple_of(j * size, size), size)
            more = jnp.dot(
                spread[k % 2, rows, :span],
                arrived[first : first + count].reshape(span, width),
                preferred_element_type=F32,
            )
            total[rows, :width] = more if k == 0 else total[rows, :width] + more
            return carry

        lax.fori_loop(0, blocks, gather, 0)

    def rows_of(i):
        rows = pl.ds(i * size, size)
        names = lax.broadcasted_iota(jnp.int32, (hot_total, size), 0)
        many = jnp.zeros((hot_total, size), F32)
        for k in range(HK):
            many = many + jnp.where(ids[k : k + 1, rows] == names, 1.0, 0.0)
        many = many.astype(BF16)
        counts[:, rows] = many
        mix = lax.dot_general(many, table[...], (((0,), (0,)), ((), ())), preferred_element_type=F32)
        base[rows] = jnp.dot(feat[rows], w_self[...], preferred_element_type=F32) + mix * (1.0 / HK)
        feat_t[:, rows] = feat[rows].astype(F32).T.astype(BF16)

    f_exchange(0, own)
    prepare(0)
    prepare(1)
    for k in range(1, half + 1):
        for s in range(SUBS):
            for side in "rl":
                if goes(side, k, s):
                    f_ring(side, k, s).wait_recv()
                if goes(side, k + 1, s):
                    f_ring(side, k + 1, s).start()
        f_exchange(nz - k, f_right[k])
        if k < half:
            f_exchange(k, f_left[k])
        messages(k - 1)
        if k < half:
            prepare(k + 1)
        if k == 1:
            for copy in hot_copies(True):
                copy.wait_recv()
        for i in range(blocks):
            if i * (half - 1) // blocks == k - 1:
                rows_of(i)
    messages(half)

    def finish(j, carry):
        rows = pl.ds(pl.multiple_of(j * size, size), size)
        inv = 1.0 / jnp.maximum(total[rows, width : width + 1], 1.0)
        pre = base[rows] + total[rows, :width] * inv
        s = jax.nn.sigmoid(pre)
        hidden[rows] = (pre * s).astype(BF16)
        g = (cotangent[rows].astype(F32) * s * (1.0 + pre * (1.0 - s))).astype(BF16)
        grad[rows] = g
        scaled[j] = (g.astype(F32) * inv).astype(BF16)
        return carry

    lax.fori_loop(0, blocks, finish, 0)

    back, came, mine, far, near = (r[n] for n in ("back", "came", "mine", "far", "near"))
    b_right = [r["b_right%d" % k] for k in range(half)]
    b_left = [r["b_left%d" % k] for k in range(half)]

    def b_copy(zoff, d, coming):
        return remote(
            back.at[d - 1, zoff],
            came.at[d - 1 if coming else NX - d - 1, zoff],
            r["bx_send"].at[d - 1, zoff],
            r["bx_recv"].at[d - 1 if coming else NX - d - 1, zoff],
            x_peers[d - 1],
        )

    def b_exchange(zoff):
        for d in [*range(1, NX), 0]:
            block = target[jnp.maximum(asked[0, 1, owner_at(zoff, d)], 0)]
            value = jnp.dot(turned[spot(zoff), d], scaled[block], preferred_element_type=F32).astype(BF16)
            if d == 0:
                mine[zoff] = value
            else:
                back[d - 1, zoff] = value
                b_copy(zoff, d, False).start()

    def b_arrive(zoff):
        for d in range(1, NX):
            b_copy(zoff, d, True).wait_recv()

    step_rows = min(size, 32)

    def add_local(dst, sources, s, zoff):
        wanted = [asked[d, 0, owner_at(zoff, 0)] for d in range(NX)]

        def body(i, carry):
            rows = pl.ds(pl.multiple_of(i * step_rows, step_rows), step_rows)
            terms = [mine[zoff, rows].astype(F32)]
            for d in range(1, NX):
                terms.append(came[d - 1, zoff, rows].astype(F32))
            for j in range(s * per, (s + 1) * per):
                sums = None
                for d in range(NX):
                    term = jnp.where(wanted[d] == j, terms[d], 0.0)
                    sums = term if sums is None else sums + term
                for source in sources:
                    sums = sums + source[j, rows].astype(F32)
                dst[j, rows] = sums.astype(BF16)
            return carry

        lax.fori_loop(0, size // step_rows, body, 0)

    def b_ring(side, k, s):
        part = pl.ds(s * per, per)
        bufs, to = (b_right, to_right) if side == "r" else (b_left, to_left)
        src = far if k == half else bufs[k]
        return remote(
            src.at[part], bufs[k - 1].at[part], r["bs_" + side].at[k - 1, s], r["br_" + side].at[k - 1, s], to
        )

    group = selfs.mine.shape[1]

    def weight_product(rhs, dest):
        def body(i, carry):
            rows = pl.ds(pl.multiple_of(i * 4 * group, 4 * group), 4 * group)
            value = jnp.dot(feat_t[rows], rhs, preferred_element_type=F32)
            for q in range(4):
                dest.mine[i * 4 + q] = value[q * group : (q + 1) * group].astype(dest.mine.dtype)
            return carry

        lax.fori_loop(0, nz // 4, body, 0)

    def self_start():
        weight_product(grad[...], selfs)
        selfs.stage1()

    def author_start():
        def body(i, carry):
            rows = pl.ds(pl.multiple_of(i * hot_rows, hot_rows), hot_rows)
            authors.mine[i] = jnp.dot(counts[rows], grad[...], preferred_element_type=F32) * (1.0 / HK)
            return carry

        lax.fori_loop(0, nh, body, 0)
        authors.stage1()

    extras = [
        self_start,
        author_start,
        selfs.stage2,
        authors.stage2,
        selfs.stage3,
        authors.stage3,
        selfs.stage4,
        authors.stage4,
        authors.stage5,
        lambda: selfs.finish(self_out),
        lambda: authors.finish(author_out),
    ]
    b_exchange(half)
    for zoff in offsets(half - 1):
        b_exchange(zoff)
    for k in range(half, 0, -1):
        for zoff in offsets(k):
            b_arrive(zoff)
        for s in range(SUBS):
            for side in "rl":
                if not goes(side, k, s):
                    continue
                bufs = b_right if side == "r" else b_left
                sources = []
                if k < half and goes(side, k + 1, s):
                    b_ring(side, k + 1, s).wait_recv()
                    sources = [bufs[k]]
                add_local(far if k == half else bufs[k], sources, s, k if side == "r" else nz - k)
                b_ring(side, k, s).start()
        if k >= 2:
            for zoff in offsets(k - 2):
                b_exchange(zoff)
        first = (half - k) * len(extras) // half
        last = (half - k + 1) * len(extras) // half
        for extra in extras[first:last]:
            extra()
    b_arrive(0)
    for s in range(SUBS):
        b_ring("r", 1, s).wait_recv()
        b_ring("l", 1, s).wait_recv()
        add_local(near, [b_right[0], b_left[0]], s, 0)
    weight_product(near[...].reshape(blocks * size, width), cites)
    cites.stage1()
    for copy in ask_copies(False) + hot_copies(False):
        copy.wait_send()
    for zoff in range(nz):
        for d in range(1, NX):
            f_copy(zoff, d, False).wait_send()
            b_copy(zoff, d, False).wait_send()
    for k in range(1, half + 1):
        for s in range(SUBS):
            for side in "rl":
                if goes(side, k, s):
                    f_ring(side, k, s).wait_send()
                    b_ring(side, k, s).wait_send()
    selfs.drain()
    authors.drain()
    cites.stage2()
    cites.stage3()
    cites.stage4()
    cites.finish(cite_out)
    cites.drain()


def layer(nz, nh, feat, w_cite, w_self, hot, ids, req, values, cotangent, used, target):
    half = nz // 2
    rows, din = feat.shape
    width = w_self.shape[1]
    size = values.shape[1]
    blocks = rows // size
    hot_total = hot.shape[0] * nh
    share = din // (nz * NX)
    vmem = pl.BlockSpec(memory_space=pltpu.VMEM)
    smem = pl.BlockSpec(memory_space=pltpu.SMEM)
    dma = pltpu.SemaphoreType.DMA
    chunk = pltpu.VMEM((blocks, size, width), BF16)
    column = pltpu.VMEM((NX - 1, nz, size, width), BF16)
    scratch = {
        "own": chunk,
        "packed": column,
        "table": pltpu.VMEM((hot_total, width), BF16),
        "asks": pltpu.VMEM((NX,) + req.shape, jnp.int32),
        "asked": pltpu.SMEM((NX,) + req.shape, jnp.int32),
        "arrived": pltpu.VMEM((nz, NX, size, width), BF16),
        "spread": pltpu.VMEM((2, rows, 2 * NX * size), BF16),
        "turned": pltpu.VMEM((nz, NX, size, size), BF16),
        "counts": pltpu.VMEM((hot_total, rows), BF16),
        "feat_t": pltpu.VMEM((din, rows), BF16),
        "base": pltpu.VMEM((rows, width), F32),
        "total": pltpu.VMEM((rows, width + size), F32),
        "grad": pltpu.VMEM((rows, width), BF16),
        "scaled": chunk,
        "back": column,
        "came": column,
        "mine": pltpu.VMEM((nz, size, width), BF16),
        "far": chunk,
        "near": chunk,
        "h_send": dma((nh - 1,)),
        "h_recv": dma((nh - 1,)),
        "q_send": dma((NX - 1,)),
        "q_recv": dma((NX - 1,)),
        "q_local": dma,
    }
    for k in range(1, half + 1):
        scratch["f_right%d" % k] = chunk
    for k in range(1, half):
        scratch["f_left%d" % k] = chunk
    for k in range(half):
        scratch["b_right%d" % k] = chunk
        scratch["b_left%d" % k] = chunk
    for name in ("fs_r", "fr_r", "fs_l", "fr_l", "bs_r", "br_r", "bs_l", "br_l"):
        scratch[name] = dma((half, SUBS))
    for name in ("fx_send", "fx_recv", "bx_send", "bx_recv"):
        scratch[name] = dma((NX - 1, nz))
    for name, parts in (
        ("self", WeightSum.scratch(nz, nh, share, width, F32)),
        ("cite", WeightSum.scratch(nz, nh, share, width, BF16)),
        ("author", AuthorSum.scratch(nz, nh, hot.shape[0], width)),
    ):
        for i, part in enumerate(parts):
            scratch[name + str(i)] = part
    names = ["in%d" % i for i in range(10)] + ["out%d" % i for i in range(4)] + list(scratch)
    return pl.pallas_call(
        functools.partial(layer_kernel, names, nz, nh),
        out_shape=(
            jax.ShapeDtypeStruct((rows, width), BF16),
            jax.ShapeDtypeStruct((share, width), F32),
            jax.ShapeDtypeStruct((share, width), F32),
            jax.ShapeDtypeStruct(hot.shape, F32),
        ),
        in_specs=[vmem] * 8 + [smem] * 2,
        out_specs=(vmem,) * 4,
        scratch_shapes=list(scratch.values()),
        compiler_params=pltpu.CompilerParams(
            collective_id=1, has_side_effects=True, vmem_limit_bytes=VMEM_LIMIT
        ),
    )(feat, w_cite, w_self, hot, ids, req, values, cotangent, used, target)


def hand_over_kernel(*refs):
    half = len(refs) // 2
    for src, dst in zip(refs[:half], refs[half:]):
        dst[...] = src[...]


def hand_over(arrays):
    vmem = pl.BlockSpec(memory_space=pltpu.VMEM)
    return pl.pallas_call(
        hand_over_kernel,
        out_shape=tuple(jax.ShapeDtypeStruct(a.shape, a.dtype) for a in arrays),
        in_specs=[vmem] * len(arrays),
        out_specs=(vmem,) * len(arrays),
    )(*arrays)


def on_device(
    paper_features,
    self_weight,
    cite_weight,
    hot_embed,
    hot_ids,
    tile_values,
    tile_rows,
    tile_target_block,
    tile_block,
    tile_owner,
    cotangent,
):
    wide = lax.axis_size("wide")
    nh = lax.axis_size("hot")
    nz = wide // NX
    tiles = tile_values.shape[0]
    shape = (8, tiles, max(128, wide))
    what = jnp.where(
        lax.broadcasted_iota(jnp.int32, shape, 0) == 0,
        tile_block[None, :, None],
        lax.broadcasted_iota(jnp.int32, shape, 1),
    )
    owned = tile_owner[None, :, None] == lax.broadcasted_iota(jnp.int32, shape, 2)
    req = jnp.max(jnp.where(owned, what, -1), axis=1)
    return hand_over(
        layer(
            nz,
            nh,
            paper_features,
            cite_weight,
            self_weight,
            hot_embed,
            hot_ids.T,
            req,
            tile_values,
            cotangent,
            tile_rows,
            tile_target_block,
        )
    )


def solution(mesh):
    return jax.shard_map(
        on_device,
        mesh=mesh,
        in_specs=(
            P(("wide", "hot"), None),
            P(),
            P(),
            P("hot", None),
            P(("wide", "hot"), None),
            P(("wide", "hot"), None, None),
            P(("wide", "hot")),
            P(("wide", "hot")),
            P(("wide", "hot")),
            P(("wide", "hot")),
            P(("wide", "hot"), None),
        ),
        out_specs=(P(("wide", "hot"), None), P("wide", None), P("wide", None), P("hot", None)),
        check_vma=False,
    )
```

```python
import functools

import jax
import jax.numpy as jnp
from jax import lax
from jax.experimental import pallas as pl
from jax.experimental.pallas import tpu as pltpu
from jax.sharding import PartitionSpec as P

HK = 8
NX = 4
SUBS = 8
PAD = 16
MESH = pl.DeviceIdType.MESH
F32 = jnp.float32
BF16 = jnp.bfloat16
VMEM_LIMIT = 58 * 1024 * 1024


def place(nz):
    w = lax.axis_index("wide")
    h = lax.axis_index("hot")
    return w // NX, w % NX, w, h


def greet(partners):
    barrier = pltpu.get_barrier_semaphore()
    for partner in partners:
        pl.semaphore_signal(barrier, inc=1, device_id=partner, device_id_type=MESH)
    return lambda: pl.semaphore_wait(barrier, len(partners))


def remote(src, dst, send, recv, target):
    return pltpu.make_async_remote_copy(
        src_ref=src, dst_ref=dst, send_sem=send, recv_sem=recv, device_id=target, device_id_type=MESH
    )


class WeightSum:
    def __init__(self, where, nz, nh, refs):
        self.z, self.x, self.w, self.h = where
        self.nz, self.nh = nz, nh
        (self.mine, self.got1, self.mid, self.got2, self.last, self.got3, self.done) = refs[:7]
        (self.wide, self.s1, self.r1, self.s2, self.r2, self.s3, self.r3, self.s4, self.r4) = refs[7:16]
        self.share = self.mine.shape[1] // NX

    @staticmethod
    def scratch(nz, nh, share, width, kind):
        dma = pltpu.SemaphoreType.DMA
        two = nz // nh
        return [
            pltpu.VMEM((nz, NX * share, width), kind),
            pltpu.VMEM((nh - 1, two, NX * share, width), kind),
            pltpu.VMEM((NX, two, PAD, width), BF16),
            pltpu.VMEM((NX - 1, two, PAD, width), BF16),
            pltpu.VMEM((two, PAD, width), BF16),
            pltpu.VMEM((nz - 1, PAD, width), BF16),
            pltpu.VMEM((PAD, width), F32),
            pltpu.VMEM((NX, two, PAD, width), F32),
            dma((nh - 1, two)),
            dma((nh - 1, two)),
            dma((NX - 1,)),
            dma((NX - 1,)),
            dma((two,)),
            dma((nz - 1,)),
            dma((nh - 1,)),
            dma,
        ]

    def copies1(self):
        out = []
        for d in range(1, self.nh):
            peer = lax.rem(self.h + d, self.nh)
            for i in range(self.nz // self.nh):
                e = self.nh - d - 1
                out.append(
                    remote(
                        self.mine.at[peer + i * self.nh],
                        self.got1.at[e, i],
                        self.s1.at[d - 1, i],
                        self.r1.at[e, i],
                        (self.w, peer),
                    )
                )
        return out

    def copies2(self):
        out = []
        for d in range(1, NX):
            peer = lax.rem(self.x + d, NX)
            e = NX - d - 1
            out.append(
                remote(
                    self.mid.at[peer],
                    self.got2.at[e],
                    self.s2.at[d - 1],
                    self.r2.at[e],
                    (self.z * NX + peer, self.h),
                )
            )
        return out

    def each3(self, act):
        for i in range(self.nz // self.nh):
            there = self.h + i * self.nh
            off = lax.rem(self.z - there + self.nz, self.nz)

            @pl.when(off != 0)
            def _():
                act(
                    remote(
                        self.last.at[i],
                        self.got3.at[off - 1],
                        self.s3.at[i],
                        self.r3.at[off - 1],
                        (there * NX + self.x, self.h),
                    )
                )

    def copies4(self):
        return [
            remote(
                self.done, self.done, self.s4.at[d - 1], self.r4, (self.w, lax.rem(self.h + d, self.nh))
            )
            for d in range(1, self.nh)
        ]

    def stage1(self):
        for copy in self.copies1():
            copy.start()

    def stage2(self):
        self.wide[...] = jnp.zeros_like(self.wide)
        for copy in self.copies1():
            copy.wait_recv()
        for i in range(self.nz // self.nh):
            sums = self.mine[self.h + i * self.nh].astype(F32)
            for e in range(self.nh - 1):
                sums = sums + self.got1[e, i].astype(F32)
            for peer in range(NX):
                self.wide[peer, i, : self.share] = sums[peer * self.share : (peer + 1) * self.share]
        self.mid[...] = self.wide[...].astype(BF16)
        for copy in self.copies2():
            copy.start()

    def stage3(self):
        for copy in self.copies2():
            copy.wait_recv()
        sums = self.wide[self.x]
        for e in range(NX - 1):
            sums = sums + self.got2[e].astype(F32)
        self.wide[self.x] = sums
        self.last[...] = sums.astype(BF16)
        self.each3(lambda copy: copy.start())

    def stage4(self):
        @pl.when(lax.rem(self.z, self.nh) == self.h)
        def _():
            for o in range(self.nz - 1):
                remote(
                    self.last.at[0], self.got3.at[o], self.s3.at[0], self.r3.at[o], (self.w, self.h)
                ).wait_recv()
            sums = self.wide[self.x, self.z // self.nh]
            for o in range(self.nz - 1):
                sums = sums + self.got3[o].astype(F32)
            self.done[...] = sums
            for copy in self.copies4():
                copy.start()

    def finish(self, out):
        @pl.when(lax.rem(self.z, self.nh) != self.h)
        def _():
            self.copies4()[0].wait_recv()

        out[...] = self.done[: self.share]

    def drain(self):
        for copy in self.copies1() + self.copies2():
            copy.wait_send()
        self.each3(lambda copy: copy.wait_send())

        @pl.when(lax.rem(self.z, self.nh) == self.h)
        def _():
            for copy in self.copies4():
                copy.wait_send()


class AuthorSum:
    def __init__(self, where, nz, nh, refs):
        self.z, self.x, self.w, self.h = where
        self.nz, self.nh, self.np = nz, nh, nz // 2
        (self.mine, self.got1, self.mid, self.got2, self.cut, self.got3, self.sums4, self.rows5) = refs[:8]
        (self.s1, self.r1, self.s2, self.r2, self.s3, self.r3, self.s4, self.r4, self.s5, self.r5) = refs[8:18]

    @staticmethod
    def scratch(nz, nh, rows, width):
        dma = pltpu.SemaphoreType.DMA
        part = rows // NX
        pieces = nz // 2
        return [
            pltpu.VMEM((nh, rows, width), F32),
            pltpu.VMEM((nh - 1, rows, width), F32),
            pltpu.VMEM((NX, part, width), F32),
            pltpu.VMEM((NX - 1, part, width), F32),
            pltpu.VMEM((pieces, 8, width // 2), F32),
            pltpu.VMEM((nz - 1, 8, width // 2), F32),
            pltpu.VMEM((pieces, 8, width // 2), F32),
            pltpu.VMEM((NX, part, width), F32),
            dma((nh - 1,)),
            dma((nh - 1,)),
            dma((NX - 1,)),
            dma((NX - 1,)),
            dma((nz - 1,)),
            dma((nz - 1,)),
            dma((pieces - 1,)),
            dma((pieces - 1,)),
            dma((NX - 1,)),
            dma((NX - 1,)),
        ]

    def copies1(self):
        out = []
        for d in range(1, self.nh):
            peer = lax.rem(self.h + d, self.nh)
            e = self.nh - d - 1
            out.append(
                remote(self.mine.at[peer], self.got1.at[e], self.s1.at[d - 1], self.r1.at[e], (self.w, peer))
            )
        return out

    def copies2(self):
        out = []
        for d in range(1, NX):
            peer = lax.rem(self.x + d, NX)
            e = NX - d - 1
            to = (self.z * NX + peer, self.h)
            out.append(remote(self.mid.at[peer], self.got2.at[e], self.s2.at[d - 1], self.r2.at[e], to))
        return out

    def copies3(self):
        out = []
        for d in range(1, self.nz):
            peer = lax.rem(self.z + d, self.nz)
            e = self.nz - d - 1
            to = (peer * NX + self.x, self.h)
            out.append(
                remote(
                    self.cut.at[lax.rem(peer, self.np)], self.got3.at[e], self.s3.at[d - 1], self.r3.at[e], to
                )
            )
        return out

    def copies4(self, coming=False):
        out = []
        p = lax.rem(self.z, self.np)
        for d in range(1, self.np):
            other = lax.rem(p + d, self.np)
            to = ((self.z - p + other) * NX + self.x, self.h)
            e = d - 1 if coming else self.np - d - 1
            piece = self.sums4.at[other if coming else p]
            out.append(remote(piece, piece, self.s4.at[d - 1], self.r4.at[e], to))
        return out

    def copies5(self, coming=False):
        out = []
        for d in range(1, NX):
            peer = lax.rem(self.x + d, NX)
            e = d - 1 if coming else NX - d - 1
            rows = self.rows5.at[peer if coming else self.x]
            out.append(remote(rows, rows, self.s5.at[d - 1], self.r5.at[e], (self.z * NX + peer, self.h)))
        return out

    def stage1(self):
        for copy in self.copies1():
            copy.start()

    def stage2(self):
        for copy in self.copies1():
            copy.wait_recv()
        sums = self.mine[self.h]
        for e in range(self.nh - 1):
            sums = sums + self.got1[e]
        self.mid[...] = sums.reshape(self.mid.shape)
        for copy in self.copies2():
            copy.start()

    def stage3(self):
        for copy in self.copies2():
            copy.wait_recv()
        sums = self.mid[self.x]
        for e in range(NX - 1):
            sums = sums + self.got2[e]
        lanes = self.cut.shape[2]
        for p in range(self.np):
            g, c = p // 2, p % 2
            self.cut[p] = sums[g * 8 : (g + 1) * 8, c * lanes : (c + 1) * lanes]
        for copy in self.copies3():
            copy.start()

    def stage4(self):
        for copy in self.copies3():
            copy.wait_recv()
        p = lax.rem(self.z, self.np)
        sums = self.cut[p]
        for e in range(self.nz - 1):
            sums = sums + self.got3[e]
        self.sums4[p] = sums
        for copy in self.copies4():
            copy.start()

    def stage5(self):
        for copy in self.copies4(True):
            copy.wait_recv()
        lanes = self.cut.shape[2]
        for p in range(self.np):
            g, c = p // 2, p % 2
            self.rows5[self.x, g * 8 : (g + 1) * 8, c * lanes : (c + 1) * lanes] = self.sums4[p]
        for copy in self.copies5():
            copy.start()

    def finish(self, out):
        for copy in self.copies5(True):
            copy.wait_recv()
        out[...] = self.rows5[...].reshape(out.shape)

    def drain(self):
        for copy in self.copies1() + self.copies2() + self.copies3() + self.copies4() + self.copies5():
            copy.wait_send()


def layer_kernel(names, nz, nh, *refs):
    r = dict(zip(names, refs))
    half = nz // 2
    feat, w_cite, w_self, hot, ids, req, values, cotangent, used, target = refs[:10]
    hidden, self_out, cite_out, author_out = refs[10:14]
    own, packed, table, asks, asked, arrived = (
        r[n] for n in ("own", "packed", "table", "asks", "asked", "arrived")
    )
    spread, turned, counts, feat_t, base, total, grad, scaled = (
        r[n] for n in ("spread", "turned", "counts", "feat_t", "base", "total", "grad", "scaled")
    )
    where = place(nz)
    z, x, w, h = where
    selfs = WeightSum(where, nz, nh, [r["self%d" % i] for i in range(16)])
    cites = WeightSum(where, nz, nh, [r["cite%d" % i] for i in range(16)])
    authors = AuthorSum(where, nz, nh, [r["author%d" % i] for i in range(18)])
    blocks, size, width = own.shape
    hot_rows = hot.shape[0]
    hot_total = table.shape[0]
    per = blocks // SUBS
    to_right = (lax.rem(z + 1, nz) * NX + x, h)
    to_left = (lax.rem(z + nz - 1, nz) * NX + x, h)
    z_peers = [(lax.rem(z + d, nz) * NX + x, h) for d in range(1, nz)]
    x_peers = [(z * NX + lax.rem(x + d, NX), h) for d in range(1, NX)]
    h_peers = [(w, lax.rem(h + d, nh)) for d in range(1, nh)]
    wait_all = greet(z_peers + x_peers + h_peers)

    my_rows = pl.ds(pl.multiple_of(h * hot_rows, hot_rows), hot_rows)
    table[my_rows] = hot[...].astype(BF16)
    asks[0] = req[...]

    def spot(zoff):
        if zoff == 0:
            return 0
        return 2 * zoff if zoff < half else 2 * (nz - zoff) - 1

    def offsets(k):
        return [0] if k == 0 else [half] if k == half else [nz - k, k]

    f_right = [own] + [r["f_right%d" % k] for k in range(1, half + 1)]
    f_left = [own] + [r["f_left%d" % k] for k in range(1, half)] + [f_right[half]]
    rows_f32 = lax.broadcasted_iota(jnp.int32, (size, size), 0)

    def goes(side, k, s):
        if k > half:
            return False
        return k < half or (s < SUBS // 2) == (side == "r")

    def f_ring(side, k, s):
        part = pl.ds(s * per, per)
        bufs, to = (f_right, to_right) if side == "r" else (f_left, to_left)
        return remote(
            bufs[k - 1].at[part],
            bufs[k].at[part],
            r["fs_" + side].at[k - 1, s],
            r["fr_" + side].at[k - 1, s],
            to,
        )

    def project(j, carry):
        rows = pl.ds(pl.multiple_of(j * size, size), size)
        own[j] = jnp.dot(feat[rows], w_cite[...], preferred_element_type=F32).astype(BF16)
        return carry

    lax.fori_loop(0, blocks, project, 0)
    wait_all()
    for s in range(SUBS):
        for side in "rl":
            if goes(side, 1, s):
                f_ring(side, 1, s).start()

    def ask_copies(coming):
        return [
            remote(
                asks.at[0],
                asks.at[d if coming else NX - d],
                r["q_send"].at[d - 1],
                r["q_recv"].at[d - 1 if coming else NX - d - 1],
                x_peers[d - 1],
            )
            for d in range(1, NX)
        ]

    def hot_copies(coming):
        out = []
        for d in range(1, nh):
            peer = lax.rem(h + d, nh) if coming else h
            rows = table.at[pl.ds(pl.multiple_of(peer * hot_rows, hot_rows), hot_rows)]
            e = d - 1 if coming else nh - d - 1
            out.append(remote(rows, rows, r["h_send"].at[d - 1], r["h_recv"].at[e], h_peers[d - 1]))
        return out

    for copy in ask_copies(False) + hot_copies(False):
        copy.start()
    for copy in ask_copies(True):
        copy.wait_recv()
    local = pltpu.make_async_copy(asks, asked, r["q_local"])
    local.start()
    local.wait()

    def owner_at(zoff, d):
        return lax.rem(z + zoff, nz) * NX + lax.rem(x + d, NX)

    def f_copy(zoff, d, coming):
        return remote(
            packed.at[d - 1, zoff],
            arrived.at[spot(zoff), d if coming else NX - d],
            r["fx_send"].at[d - 1, zoff],
            r["fx_recv"].at[d - 1 if coming else NX - d - 1, zoff],
            x_peers[d - 1],
        )

    def f_exchange(zoff, source):
        owner = owner_at(zoff, 0)
        for d in range(1, NX):
            packed[d - 1, zoff] = source[jnp.maximum(asked[d, 0, owner], 0)]
            f_copy(zoff, d, False).start()
        arrived[spot(zoff), 0] = source[jnp.maximum(asked[0, 0, owner], 0)]

    def tile_of(zoff, d):
        t = asked[0, 1, owner_at(zoff, d)]
        number = jnp.maximum(t, 0)
        return values[number].astype(F32), jnp.where(t < 0, 0, used[number]), target[number]

    def lay_out(k, zoff, d):
        held = spread.at[k % 2]
        n = offsets(k).index(zoff) * NX + d
        m, live, block = tile_of(zoff, d)
        turned[spot(zoff), d] = jnp.where(rows_f32 < live, m, 0.0).T.astype(BF16)

        def lay(j, carry):
            there = jnp.where(block == j, live, 0)
            rows = pl.ds(pl.multiple_of(j * size, size), size)
            held[rows, n * size : (n + 1) * size] = jnp.where(rows_f32 < there, m, 0.0).astype(BF16)
            return carry

        lax.fori_loop(0, blocks, lay, 0)

    def degrees(k):
        span = len(offsets(k)) * NX * size
        ones = jnp.ones((span, size), BF16)

        def body(j, carry):
            rows = pl.ds(pl.multiple_of(j * size, size), size)
            more = jnp.dot(spread[k % 2, rows, :span], ones, preferred_element_type=F32)
            total[rows, width:] = more if k == 0 else total[rows, width:] + more
            return carry

        lax.fori_loop(0, blocks, body, 0)

    def prepare(k):
        parts = [functools.partial(lay_out, k, zoff, d) for zoff in offsets(k) for d in range(NX)]
        return parts + [functools.partial(degrees, k)]

    def share_out(work, s):
        for item in work[s * len(work) // SUBS : (s + 1) * len(work) // SUBS]:
            item()

    def messages(k):
        for zoff in offsets(k):
            for d in range(1, NX):
                f_copy(zoff, d, True).wait_recv()
        first = spot(offsets(k)[0])
        count = len(offsets(k))
        span = count * NX * size

        def gather(j, carry):
            rows = pl.ds(pl.multiple_of(j * size, size), size)
            more = jnp.dot(
                spread[k % 2, rows, :span],
                arrived[first : first + count].reshape(span, width),
                preferred_element_type=F32,
            )
            total[rows, :width] = more if k == 0 else total[rows, :width] + more
            return carry

        lax.fori_loop(0, blocks, gather, 0)

    def count(i):
        rows = pl.ds(i * size, size)

        def body(a, carry):
            there = pl.ds(pl.multiple_of(a * hot_rows, hot_rows), hot_rows)
            names = lax.broadcasted_iota(jnp.int32, (hot_rows, size), 0) + a * hot_rows
            many = jnp.zeros((hot_rows, size), F32)
            for k in range(HK):
                many = many + jnp.where(ids[k : k + 1, rows] == names, 1.0, 0.0)
            counts[there, rows] = many.astype(BF16)
            return carry

        lax.fori_loop(0, nh, body, 0)

    def start_rows(i):
        rows = pl.ds(i * size, size)
        mix = lax.dot_general(
            counts[:, rows], table[...], (((0,), (0,)), ((), ())), preferred_element_type=F32
        )
        base[rows] = jnp.dot(feat[rows], w_self[...], preferred_element_type=F32) + mix * (1.0 / HK)

    def turn(i):
        rows = pl.ds(i * size, size)
        feat_t[:, rows] = feat[rows].astype(F32).T.astype(BF16)

    def f_done(k):
        for s in range(SUBS):
            for side in "rl":
                if k >= 1 and goes(side, k, s):
                    f_ring(side, k, s).wait_send()
        for zoff in offsets(k):
            for d in range(1, NX):
                f_copy(zoff, d, False).wait_send()

    f_exchange(0, own)
    for item in prepare(0) + prepare(1):
        item()
    for k in range(1, half + 1):
        work = []
        for i in range(blocks):
            if i * (half - 1) // blocks == k - 1:
                work += [functools.partial(part, i) for part in (turn, count, start_rows)]
        work.append(functools.partial(messages, k - 1))
        if k < half:
            work += prepare(k + 1)
        if k >= 2:
            work.append(functools.partial(f_done, k - 2))
        if k == 1:
            for copy in hot_copies(True):
                copy.wait_recv()
        for s in range(SUBS):
            for side in "rl":
                if goes(side, k, s):
                    f_ring(side, k, s).wait_recv()
                if goes(side, k + 1, s):
                    f_ring(side, k + 1, s).start()
            if s == SUBS - 1:
                f_exchange(nz - k, f_right[k])
                if k < half:
                    f_exchange(k, f_left[k])
            share_out(work, s)
    messages(half)

    def finish(j, carry):
        rows = pl.ds(pl.multiple_of(j * size, size), size)
        inv = 1.0 / jnp.maximum(total[rows, width : width + 1], 1.0)
        pre = base[rows] + total[rows, :width] * inv
        s = jax.nn.sigmoid(pre)
        hidden[rows] = (pre * s).astype(BF16)
        g = (cotangent[rows].astype(F32) * s * (1.0 + pre * (1.0 - s))).astype(BF16)
        grad[rows] = g
        scaled[j] = (g.astype(F32) * inv).astype(BF16)
        return carry

    lax.fori_loop(0, blocks, finish, 0)

    back, came, mine, far, near = (r[n] for n in ("back", "came", "mine", "far", "near"))
    b_right = [r["b_right%d" % k] for k in range(half)]
    b_left = [r["b_left%d" % k] for k in range(half)]

    def b_copy(zoff, d, coming):
        return remote(
            back.at[d - 1, zoff],
            came.at[d - 1 if coming else NX - d - 1, zoff],
            r["bx_send"].at[d - 1, zoff],
            r["bx_recv"].at[d - 1 if coming else NX - d - 1, zoff],
            x_peers[d - 1],
        )

    def b_make(zoff, d):
        block = target[jnp.maximum(asked[0, 1, owner_at(zoff, d)], 0)]
        value = jnp.dot(turned[spot(zoff), d], scaled[block], preferred_element_type=F32).astype(BF16)
        if d == 0:
            mine[zoff] = value
        else:
            back[d - 1, zoff] = value
            b_copy(zoff, d, False).start()

    def b_exchange(k):
        return [functools.partial(b_make, zoff, d) for d in [*range(1, NX), 0] for zoff in offsets(k)]

    def b_done(k):
        for s in range(SUBS):
            for side in "rl":
                if k >= 1 and goes(side, k, s):
                    b_ring(side, k, s).wait_send()
        for zoff in offsets(k):
            for d in range(1, NX):
                b_copy(zoff, d, False).wait_send()

    def b_arrive(zoff):
        for d in range(1, NX):
            b_copy(zoff, d, True).wait_recv()

    step_rows = min(size, 32)

    def add_local(dst, sources, s, zoff):
        wanted = [asked[d, 0, owner_at(zoff, 0)] for d in range(NX)]

        def body(i, carry):
            rows = pl.ds(pl.multiple_of(i * step_rows, step_rows), step_rows)
            terms = [mine[zoff, rows].astype(F32)]
            for d in range(1, NX):
                terms.append(came[d - 1, zoff, rows].astype(F32))
            for j in range(s * per, (s + 1) * per):
                sums = None
                for d in range(NX):
                    term = jnp.where(wanted[d] == j, terms[d], 0.0)
                    sums = term if sums is None else sums + term
                for source in sources:
                    sums = sums + source[j, rows].astype(F32)
                dst[j, rows] = sums.astype(BF16)
            return carry

        lax.fori_loop(0, size // step_rows, body, 0)

    def b_ring(side, k, s):
        part = pl.ds(s * per, per)
        bufs, to = (b_right, to_right) if side == "r" else (b_left, to_left)
        src = far if k == half else bufs[k]
        return remote(
            src.at[part], bufs[k - 1].at[part], r["bs_" + side].at[k - 1, s], r["br_" + side].at[k - 1, s], to
        )

    group = selfs.mine.shape[1]

    def weight_product(rhs, dest):
        def body(i, carry):
            rows = pl.ds(pl.multiple_of(i * 4 * group, 4 * group), 4 * group)
            value = jnp.dot(feat_t[rows], rhs, preferred_element_type=F32)
            for q in range(4):
                dest.mine[i * 4 + q] = value[q * group : (q + 1) * group].astype(dest.mine.dtype)
            return carry

        lax.fori_loop(0, nz // 4, body, 0)

    def self_start():
        weight_product(grad[...], selfs)
        selfs.stage1()

    def author_start():
        def body(i, carry):
            rows = pl.ds(pl.multiple_of(i * hot_rows, hot_rows), hot_rows)
            authors.mine[i] = jnp.dot(counts[rows], grad[...], preferred_element_type=F32) * (1.0 / HK)
            return carry

        lax.fori_loop(0, nh, body, 0)
        authors.stage1()

    extras = [
        [self_start],
        [author_start],
        [selfs.stage2],
        [authors.stage2],
        [selfs.stage3, authors.stage3],
        [selfs.stage4],
        [authors.stage4],
        [authors.stage5],
    ]
    for item in b_exchange(half) + b_exchange(half - 1):
        item()
    for k in range(half, 0, -1):
        work = b_exchange(k - 2) if k >= 2 else []
        for group_of in extras[(half - k) * 8 // half : (half - k + 1) * 8 // half]:
            work += group_of
        if k == half:
            work += [functools.partial(f_done, half - 1), functools.partial(f_done, half)]
        if k + 2 <= half:
            work.append(functools.partial(b_done, k + 2))
        for zoff in offsets(k):
            b_arrive(zoff)
        for s in range(SUBS):
            for side in "rl":
                if not goes(side, k, s):
                    continue
                bufs = b_right if side == "r" else b_left
                sources = []
                if k < half and goes(side, k + 1, s):
                    b_ring(side, k + 1, s).wait_recv()
                    sources = [bufs[k]]
                add_local(far if k == half else bufs[k], sources, s, k if side == "r" else nz - k)
                b_ring(side, k, s).start()
            share_out(work, s)
    b_arrive(0)
    for s in range(SUBS):
        b_ring("r", 1, s).wait_recv()
        b_ring("l", 1, s).wait_recv()
        add_local(near, [b_right[0], b_left[0]], s, 0)
    weight_product(near[...].reshape(blocks * size, width), cites)
    cites.stage1()
    selfs.finish(self_out)
    authors.finish(author_out)
    for copy in ask_copies(False) + hot_copies(False):
        copy.wait_send()
    for k in (2, 1, 0):
        b_done(k)
    cites.stage2()
    selfs.drain()
    cites.stage3()
    authors.drain()
    cites.stage4()
    cites.finish(cite_out)
    cites.drain()


def layer(nz, nh, feat, w_cite, w_self, hot, ids, req, values, cotangent, used, target):
    half = nz // 2
    rows, din = feat.shape
    width = w_self.shape[1]
    size = values.shape[1]
    blocks = rows // size
    hot_total = hot.shape[0] * nh
    share = din // (nz * NX)
    vmem = pl.BlockSpec(memory_space=pltpu.VMEM)
    smem = pl.BlockSpec(memory_space=pltpu.SMEM)
    dma = pltpu.SemaphoreType.DMA
    chunk = pltpu.VMEM((blocks, size, width), BF16)
    column = pltpu.VMEM((NX - 1, nz, size, width), BF16)
    scratch = {
        "own": chunk,
        "packed": column,
        "table": pltpu.VMEM((hot_total, width), BF16),
        "asks": pltpu.VMEM((NX,) + req.shape, jnp.int32),
        "asked": pltpu.SMEM((NX,) + req.shape, jnp.int32),
        "arrived": pltpu.VMEM((nz, NX, size, width), BF16),
        "spread": pltpu.VMEM((2, rows, 2 * NX * size), BF16),
        "turned": pltpu.VMEM((nz, NX, size, size), BF16),
        "counts": pltpu.VMEM((hot_total, rows), BF16),
        "feat_t": pltpu.VMEM((din, rows), BF16),
        "base": pltpu.VMEM((rows, width), F32),
        "total": pltpu.VMEM((rows, width + size), F32),
        "grad": pltpu.VMEM((rows, width), BF16),
        "scaled": chunk,
        "back": column,
        "came": column,
        "mine": pltpu.VMEM((nz, size, width), BF16),
        "far": chunk,
        "near": chunk,
        "h_send": dma((nh - 1,)),
        "h_recv": dma((nh - 1,)),
        "q_send": dma((NX - 1,)),
        "q_recv": dma((NX - 1,)),
        "q_local": dma,
    }
    for k in range(1, half + 1):
        scratch["f_right%d" % k] = chunk
    for k in range(1, half):
        scratch["f_left%d" % k] = chunk
    for k in range(half):
        scratch["b_right%d" % k] = chunk
        scratch["b_left%d" % k] = chunk
    for name in ("fs_r", "fr_r", "fs_l", "fr_l", "bs_r", "br_r", "bs_l", "br_l"):
        scratch[name] = dma((half, SUBS))
    for name in ("fx_send", "fx_recv", "bx_send", "bx_recv"):
        scratch[name] = dma((NX - 1, nz))
    for name, parts in (
        ("self", WeightSum.scratch(nz, nh, share, width, F32)),
        ("cite", WeightSum.scratch(nz, nh, share, width, BF16)),
        ("author", AuthorSum.scratch(nz, nh, hot.shape[0], width)),
    ):
        for i, part in enumerate(parts):
            scratch[name + str(i)] = part
    names = ["in%d" % i for i in range(10)] + ["out%d" % i for i in range(4)] + list(scratch)
    return pl.pallas_call(
        functools.partial(layer_kernel, names, nz, nh),
        out_shape=(
            jax.ShapeDtypeStruct((rows, width), BF16),
            jax.ShapeDtypeStruct((share, width), F32),
            jax.ShapeDtypeStruct((share, width), F32),
            jax.ShapeDtypeStruct(hot.shape, F32),
        ),
        in_specs=[vmem] * 8 + [smem] * 2,
        out_specs=(vmem,) * 4,
        scratch_shapes=list(scratch.values()),
        compiler_params=pltpu.CompilerParams(
            collective_id=1, has_side_effects=True, vmem_limit_bytes=VMEM_LIMIT
        ),
    )(feat, w_cite, w_self, hot, ids, req, values, cotangent, used, target)


def hand_over_kernel(*refs):
    half = len(refs) // 2
    for src, dst in zip(refs[:half], refs[half:]):
        dst[...] = src[...]


def hand_over(arrays):
    vmem = pl.BlockSpec(memory_space=pltpu.VMEM)
    return pl.pallas_call(
        hand_over_kernel,
        out_shape=tuple(jax.ShapeDtypeStruct(a.shape, a.dtype) for a in arrays),
        in_specs=[vmem] * len(arrays),
        out_specs=(vmem,) * len(arrays),
    )(*arrays)


def on_device(
    paper_features,
    self_weight,
    cite_weight,
    hot_embed,
    hot_ids,
    tile_values,
    tile_rows,
    tile_target_block,
    tile_block,
    tile_owner,
    cotangent,
):
    wide = lax.axis_size("wide")
    nh = lax.axis_size("hot")
    nz = wide // NX
    tiles = tile_values.shape[0]
    shape = (8, tiles, max(128, wide))
    what = jnp.where(
        lax.broadcasted_iota(jnp.int32, shape, 0) == 0,
        tile_block[None, :, None],
        lax.broadcasted_iota(jnp.int32, shape, 1),
    )
    owned = tile_owner[None, :, None] == lax.broadcasted_iota(jnp.int32, shape, 2)
    req = jnp.max(jnp.where(owned, what, -1), axis=1)
    return hand_over(
        layer(
            nz,
            nh,
            paper_features,
            cite_weight,
            self_weight,
            hot_embed,
            hot_ids.T,
            req,
            tile_values,
            cotangent,
            tile_rows,
            tile_target_block,
        )
    )


def solution(mesh):
    return jax.shard_map(
        on_device,
        mesh=mesh,
        in_specs=(
            P(("wide", "hot"), None),
            P(),
            P(),
            P("hot", None),
            P(("wide", "hot"), None),
            P(("wide", "hot"), None, None),
            P(("wide", "hot")),
            P(("wide", "hot")),
            P(("wide", "hot")),
            P(("wide", "hot")),
            P(("wide", "hot"), None),
        ),
        out_specs=(P(("wide", "hot"), None), P("wide", None), P("wide", None), P("hot", None)),
        check_vma=False,
    )
```

```python
import functools

import jax
import jax.numpy as jnp
from jax import lax
from jax.experimental import pallas as pl
from jax.experimental.pallas import tpu as pltpu
from jax.sharding import PartitionSpec as P

HK = 8
NX = 4
SUBS = 4
PAD = 16
MESH = pl.DeviceIdType.MESH
F32 = jnp.float32
BF16 = jnp.bfloat16
VMEM_LIMIT = 58 * 1024 * 1024


def place(nz):
    w = lax.axis_index("wide")
    h = lax.axis_index("hot")
    return w // NX, w % NX, w, h


def greet(partners):
    barrier = pltpu.get_barrier_semaphore()
    for partner in partners:
        pl.semaphore_signal(barrier, inc=1, device_id=partner, device_id_type=MESH)
    return lambda: pl.semaphore_wait(barrier, len(partners))


def remote(src, dst, send, recv, target):
    return pltpu.make_async_remote_copy(
        src_ref=src, dst_ref=dst, send_sem=send, recv_sem=recv, device_id=target, device_id_type=MESH
    )


class WeightSum:
    def __init__(self, where, nz, nh, refs):
        self.z, self.x, self.w, self.h = where
        self.nz, self.nh = nz, nh
        (self.mine, self.got1, self.mid, self.got2, self.last, self.got3, self.done) = refs[:7]
        (self.wide, self.s1, self.r1, self.s2, self.r2, self.s3, self.r3, self.s4, self.r4) = refs[7:16]
        self.share = self.mine.shape[1] // NX

    @staticmethod
    def scratch(nz, nh, share, width, kind):
        dma = pltpu.SemaphoreType.DMA
        two = nz // nh
        return [
            pltpu.VMEM((nz, NX * share, width), kind),
            pltpu.VMEM((nh - 1, two, NX * share, width), kind),
            pltpu.VMEM((NX, two, PAD, width), BF16),
            pltpu.VMEM((NX - 1, two, PAD, width), BF16),
            pltpu.VMEM((two, PAD, width), BF16),
            pltpu.VMEM((nz - 1, PAD, width), BF16),
            pltpu.VMEM((PAD, width), F32),
            pltpu.VMEM((NX, two, PAD, width), F32),
            dma((nh - 1, two)),
            dma((nh - 1, two)),
            dma((NX - 1,)),
            dma((NX - 1,)),
            dma((two,)),
            dma((nz - 1,)),
            dma((nh - 1,)),
            dma,
        ]

    def copies1(self):
        out = []
        for d in range(1, self.nh):
            peer = lax.rem(self.h + d, self.nh)
            for i in range(self.nz // self.nh):
                e = self.nh - d - 1
                out.append(
                    remote(
                        self.mine.at[peer + i * self.nh],
                        self.got1.at[e, i],
                        self.s1.at[d - 1, i],
                        self.r1.at[e, i],
                        (self.w, peer),
                    )
                )
        return out

    def copies2(self):
        out = []
        for d in range(1, NX):
            peer = lax.rem(self.x + d, NX)
            e = NX - d - 1
            out.append(
                remote(
                    self.mid.at[peer],
                    self.got2.at[e],
                    self.s2.at[d - 1],
                    self.r2.at[e],
                    (self.z * NX + peer, self.h),
                )
            )
        return out

    def each3(self, act):
        for i in range(self.nz // self.nh):
            there = self.h + i * self.nh
            off = lax.rem(self.z - there + self.nz, self.nz)

            @pl.when(off != 0)
            def _():
                act(
                    remote(
                        self.last.at[i],
                        self.got3.at[off - 1],
                        self.s3.at[i],
                        self.r3.at[off - 1],
                        (there * NX + self.x, self.h),
                    )
                )

    def copies4(self):
        return [
            remote(
                self.done, self.done, self.s4.at[d - 1], self.r4, (self.w, lax.rem(self.h + d, self.nh))
            )
            for d in range(1, self.nh)
        ]

    def stage1(self):
        for copy in self.copies1():
            copy.start()

    def stage2(self):
        self.wide[...] = jnp.zeros_like(self.wide)
        for copy in self.copies1():
            copy.wait_recv()
        for i in range(self.nz // self.nh):
            sums = self.mine[self.h + i * self.nh].astype(F32)
            for e in range(self.nh - 1):
                sums = sums + self.got1[e, i].astype(F32)
            for peer in range(NX):
                self.wide[peer, i, : self.share] = sums[peer * self.share : (peer + 1) * self.share]
        self.mid[...] = self.wide[...].astype(BF16)
        for copy in self.copies2():
            copy.start()

    def stage3(self):
        for copy in self.copies2():
            copy.wait_recv()
        sums = self.wide[self.x]
        for e in range(NX - 1):
            sums = sums + self.got2[e].astype(F32)
        self.wide[self.x] = sums
        self.last[...] = sums.astype(BF16)
        self.each3(lambda copy: copy.start())

    def stage4(self):
        @pl.when(lax.rem(self.z, self.nh) == self.h)
        def _():
            for o in range(self.nz - 1):
                remote(
                    self.last.at[0], self.got3.at[o], self.s3.at[0], self.r3.at[o], (self.w, self.h)
                ).wait_recv()
            sums = self.wide[self.x, self.z // self.nh]
            for o in range(self.nz - 1):
                sums = sums + self.got3[o].astype(F32)
            self.done[...] = sums
            for copy in self.copies4():
                copy.start()

    def finish(self, out):
        @pl.when(lax.rem(self.z, self.nh) != self.h)
        def _():
            self.copies4()[0].wait_recv()

        out[...] = self.done[: self.share]

    def drain(self):
        for copy in self.copies1() + self.copies2():
            copy.wait_send()
        self.each3(lambda copy: copy.wait_send())

        @pl.when(lax.rem(self.z, self.nh) == self.h)
        def _():
            for copy in self.copies4():
                copy.wait_send()


class AuthorSum:
    def __init__(self, where, nz, nh, refs):
        self.z, self.x, self.w, self.h = where
        self.nz, self.nh, self.np = nz, nh, nz // 2
        (self.mine, self.got1, self.mid, self.got2, self.cut, self.got3, self.sums4, self.rows5) = refs[:8]
        (self.s1, self.r1, self.s2, self.r2, self.s3, self.r3, self.s4, self.r4, self.s5, self.r5) = refs[8:18]

    @staticmethod
    def scratch(nz, nh, rows, width):
        dma = pltpu.SemaphoreType.DMA
        part = rows // NX
        pieces = nz // 2
        return [
            pltpu.VMEM((nh, rows, width), F32),
            pltpu.VMEM((nh - 1, rows, width), F32),
            pltpu.VMEM((NX, part, width), F32),
            pltpu.VMEM((NX - 1, part, width), F32),
            pltpu.VMEM((pieces, 8, width // 2), F32),
            pltpu.VMEM((nz - 1, 8, width // 2), F32),
            pltpu.VMEM((pieces, 8, width // 2), F32),
            pltpu.VMEM((NX, part, width), F32),
            dma((nh - 1,)),
            dma((nh - 1,)),
            dma((NX - 1,)),
            dma((NX - 1,)),
            dma((nz - 1,)),
            dma((nz - 1,)),
            dma((pieces - 1,)),
            dma((pieces - 1,)),
            dma((NX - 1,)),
            dma((NX - 1,)),
        ]

    def copies1(self):
        out = []
        for d in range(1, self.nh):
            peer = lax.rem(self.h + d, self.nh)
            e = self.nh - d - 1
            out.append(
                remote(self.mine.at[peer], self.got1.at[e], self.s1.at[d - 1], self.r1.at[e], (self.w, peer))
            )
        return out

    def copies2(self):
        out = []
        for d in range(1, NX):
            peer = lax.rem(self.x + d, NX)
            e = NX - d - 1
            to = (self.z * NX + peer, self.h)
            out.append(remote(self.mid.at[peer], self.got2.at[e], self.s2.at[d - 1], self.r2.at[e], to))
        return out

    def copies3(self):
        out = []
        for d in range(1, self.nz):
            peer = lax.rem(self.z + d, self.nz)
            e = self.nz - d - 1
            to = (peer * NX + self.x, self.h)
            out.append(
                remote(
                    self.cut.at[lax.rem(peer, self.np)], self.got3.at[e], self.s3.at[d - 1], self.r3.at[e], to
                )
            )
        return out

    def copies4(self, coming=False):
        out = []
        p = lax.rem(self.z, self.np)
        for d in range(1, self.np):
            other = lax.rem(p + d, self.np)
            to = ((self.z - p + other) * NX + self.x, self.h)
            e = d - 1 if coming else self.np - d - 1
            piece = self.sums4.at[other if coming else p]
            out.append(remote(piece, piece, self.s4.at[d - 1], self.r4.at[e], to))
        return out

    def copies5(self, coming=False):
        out = []
        for d in range(1, NX):
            peer = lax.rem(self.x + d, NX)
            e = d - 1 if coming else NX - d - 1
            rows = self.rows5.at[peer if coming else self.x]
            out.append(remote(rows, rows, self.s5.at[d - 1], self.r5.at[e], (self.z * NX + peer, self.h)))
        return out

    def stage1(self):
        for copy in self.copies1():
            copy.start()

    def stage2(self):
        for copy in self.copies1():
            copy.wait_recv()
        sums = self.mine[self.h]
        for e in range(self.nh - 1):
            sums = sums + self.got1[e]
        self.mid[...] = sums.reshape(self.mid.shape)
        for copy in self.copies2():
            copy.start()

    def stage3(self):
        for copy in self.copies2():
            copy.wait_recv()
        sums = self.mid[self.x]
        for e in range(NX - 1):
            sums = sums + self.got2[e]
        lanes = self.cut.shape[2]
        for p in range(self.np):
            g, c = p // 2, p % 2
            self.cut[p] = sums[g * 8 : (g + 1) * 8, c * lanes : (c + 1) * lanes]
        for copy in self.copies3():
            copy.start()

    def stage4(self):
        for copy in self.copies3():
            copy.wait_recv()
        p = lax.rem(self.z, self.np)
        sums = self.cut[p]
        for e in range(self.nz - 1):
            sums = sums + self.got3[e]
        self.sums4[p] = sums
        for copy in self.copies4():
            copy.start()

    def stage5(self):
        for copy in self.copies4(True):
            copy.wait_recv()
        lanes = self.cut.shape[2]
        for p in range(self.np):
            g, c = p // 2, p % 2
            self.rows5[self.x, g * 8 : (g + 1) * 8, c * lanes : (c + 1) * lanes] = self.sums4[p]
        for copy in self.copies5():
            copy.start()

    def finish(self, out):
        for copy in self.copies5(True):
            copy.wait_recv()
        out[...] = self.rows5[...].reshape(out.shape)

    def drain(self):
        for copy in self.copies1() + self.copies2() + self.copies3() + self.copies4() + self.copies5():
            copy.wait_send()


def layer_kernel(names, nz, nh, *refs):
    r = dict(zip(names, refs))
    half = nz // 2
    feat, w_cite, w_self, hot, ids, req, values, cotangent, used, target = refs[:10]
    hidden, self_out, cite_out, author_out = refs[10:14]
    own, packed, table, asks, asked, arrived = (
        r[n] for n in ("own", "packed", "table", "asks", "asked", "arrived")
    )
    spread, turned, counts, feat_t, base, total, grad, scaled = (
        r[n] for n in ("spread", "turned", "counts", "feat_t", "base", "total", "grad", "scaled")
    )
    degree, inverse = r["degree"], r["inverse"]
    where = place(nz)
    z, x, w, h = where
    selfs = WeightSum(where, nz, nh, [r["self%d" % i] for i in range(16)])
    cites = WeightSum(where, nz, nh, [r["cite%d" % i] for i in range(16)])
    authors = AuthorSum(where, nz, nh, [r["author%d" % i] for i in range(18)])
    blocks, size, width = own.shape
    hot_rows = hot.shape[0]
    hot_total = table.shape[0]
    per = blocks // SUBS
    to_right = (lax.rem(z + 1, nz) * NX + x, h)
    to_left = (lax.rem(z + nz - 1, nz) * NX + x, h)
    z_peers = [(lax.rem(z + d, nz) * NX + x, h) for d in range(1, nz)]
    x_peers = [(z * NX + lax.rem(x + d, NX), h) for d in range(1, NX)]
    h_peers = [(w, lax.rem(h + d, nh)) for d in range(1, nh)]
    wait_all = greet(z_peers + x_peers + h_peers)

    my_rows = pl.ds(pl.multiple_of(h * hot_rows, hot_rows), hot_rows)
    table[my_rows] = hot[...].astype(BF16)
    asks[0] = req[...]

    def spot(zoff):
        if zoff == 0:
            return 0
        return 2 * zoff if zoff < half else 2 * (nz - zoff) - 1

    def offsets(k):
        return [0] if k == 0 else [half] if k == half else [nz - k, k]

    f_right = [own] + [r["f_right%d" % k] for k in range(1, half + 1)]
    f_left = [own] + [r["f_left%d" % k] for k in range(1, half)] + [f_right[half]]
    rows_f32 = lax.broadcasted_iota(jnp.int32, (size, size), 0)

    def goes(side, k, s):
        if k > half:
            return False
        return k < half or (s < SUBS // 2) == (side == "r")

    def f_ring(side, k, s):
        part = pl.ds(s * per, per)
        bufs, to = (f_right, to_right) if side == "r" else (f_left, to_left)
        return remote(
            bufs[k - 1].at[part],
            bufs[k].at[part],
            r["fs_" + side].at[k - 1, s],
            r["fr_" + side].at[k - 1, s],
            to,
        )

    def project(j, carry):
        rows = pl.ds(pl.multiple_of(j * size, size), size)
        own[j] = jnp.dot(feat[rows], w_cite[...], preferred_element_type=F32).astype(BF16)
        return carry

    lax.fori_loop(0, blocks, project, 0)
    wait_all()
    for s in range(SUBS):
        for side in "rl":
            if goes(side, 1, s):
                f_ring(side, 1, s).start()

    def ask_copies(coming):
        return [
            remote(
                asks.at[0],
                asks.at[d if coming else NX - d],
                r["q_send"].at[d - 1],
                r["q_recv"].at[d - 1 if coming else NX - d - 1],
                x_peers[d - 1],
            )
            for d in range(1, NX)
        ]

    def hot_copies(coming):
        out = []
        for d in range(1, nh):
            peer = lax.rem(h + d, nh) if coming else h
            rows = table.at[pl.ds(pl.multiple_of(peer * hot_rows, hot_rows), hot_rows)]
            e = d - 1 if coming else nh - d - 1
            out.append(remote(rows, rows, r["h_send"].at[d - 1], r["h_recv"].at[e], h_peers[d - 1]))
        return out

    for copy in ask_copies(False) + hot_copies(False):
        copy.start()
    for copy in ask_copies(True):
        copy.wait_recv()
    local = pltpu.make_async_copy(asks, asked, r["q_local"])
    local.start()
    local.wait()

    def owner_at(zoff, d):
        return lax.rem(z + zoff, nz) * NX + lax.rem(x + d, NX)

    def f_copy(zoff, d, coming):
        return remote(
            packed.at[d - 1, zoff],
            arrived.at[spot(zoff), d if coming else NX - d],
            r["fx_send"].at[d - 1, zoff],
            r["fx_recv"].at[d - 1 if coming else NX - d - 1, zoff],
            x_peers[d - 1],
        )

    def f_exchange(zoff, source):
        owner = owner_at(zoff, 0)
        for d in range(1, NX):
            packed[d - 1, zoff] = source[jnp.maximum(asked[d, 0, owner], 0)]
        for d in range(1, NX):
            f_copy(zoff, d, False).start()
        arrived[spot(zoff), 0] = source[jnp.maximum(asked[0, 0, owner], 0)]

    def tile_of(zoff, d):
        t = asked[0, 1, owner_at(zoff, d)]
        number = jnp.maximum(t, 0)
        return values[number].astype(F32), jnp.where(t < 0, 0, used[number]), target[number]

    def lay_out(k, zoff, d):
        held = spread.at[k % 2]
        n = offsets(k).index(zoff) * NX + d
        m, live, block = tile_of(zoff, d)
        turned[spot(zoff), d] = jnp.where(rows_f32 < live, m, 0.0).T.astype(BF16)

        def lay(j, carry):
            there = jnp.where(block == j, live, 0)
            rows = pl.ds(pl.multiple_of(j * size, size), size)
            laid = jnp.where(rows_f32 < there, m, 0.0)
            held[rows, n * size : (n + 1) * size] = laid.astype(BF16)
            degree[rows] = laid if k == 0 and n == 0 else degree[rows] + laid
            return carry

        lax.fori_loop(0, blocks, lay, 0)

    def invert():
        def body(j, carry):
            rows = pl.ds(pl.multiple_of(j * size, size), size)
            sums = jnp.sum(degree[rows], axis=1, keepdims=True)
            inverse[rows] = jnp.broadcast_to(1.0 / jnp.maximum(sums, 1.0), (size, width))
            return carry

        lax.fori_loop(0, blocks, body, 0)

    def prepare(k):
        return [functools.partial(lay_out, k, zoff, d) for zoff in offsets(k) for d in range(NX)]

    def share_out(work, s):
        for item in work[s * len(work) // SUBS : (s + 1) * len(work) // SUBS]:
            item()

    def messages(k):
        for zoff in offsets(k):
            for d in range(1, NX):
                f_copy(zoff, d, True).wait_recv()
        first = spot(offsets(k)[0])
        count = len(offsets(k))
        span = count * NX * size

        step = blocks * size // 2

        def gather(j, carry):
            rows = pl.ds(pl.multiple_of(j * step, step), step)
            more = jnp.dot(
                spread[k % 2, rows, :span],
                arrived[first : first + count].reshape(span, width),
                preferred_element_type=F32,
            )
            total[rows] = more if k == 0 else total[rows] + more
            return carry

        lax.fori_loop(0, 2, gather, 0)

    def count(i):
        rows = pl.ds(i * size, size)

        def body(a, carry):
            there = pl.ds(pl.multiple_of(a * hot_rows, hot_rows), hot_rows)
            names = lax.broadcasted_iota(jnp.int32, (hot_rows, size), 0) + a * hot_rows
            many = jnp.zeros((hot_rows, size), F32)
            for k in range(HK):
                many = many + jnp.where(ids[k : k + 1, rows] == names, 1.0, 0.0)
            counts[there, rows] = many.astype(BF16)
            return carry

        lax.fori_loop(0, nh, body, 0)

    def start_rows(i):
        rows = pl.ds(i * size, size)
        mix = lax.dot_general(
            counts[:, rows], table[...], (((0,), (0,)), ((), ())), preferred_element_type=F32
        )
        base[rows] = jnp.dot(feat[rows], w_self[...], preferred_element_type=F32) + mix * (1.0 / HK)

    def turn(i):
        rows = pl.ds(i * size, size)
        feat_t[:, rows] = feat[rows].astype(F32).T.astype(BF16)

    def f_done(k):
        for s in range(SUBS):
            for side in "rl":
                if k >= 1 and goes(side, k, s):
                    f_ring(side, k, s).wait_send()
        for zoff in offsets(k):
            for d in range(1, NX):
                f_copy(zoff, d, False).wait_send()

    f_exchange(0, own)
    for item in prepare(0) + prepare(1):
        item()
    for k in range(1, half + 1):
        work = []
        for i in range(blocks):
            if i * (half - 1) // blocks == k - 1:
                work += [functools.partial(part, i) for part in (turn, count, start_rows)]
        work.append(functools.partial(messages, k - 1))
        if k < half:
            work += prepare(k + 1)
        else:
            work.append(invert)
        if k >= 2:
            work.append(functools.partial(f_done, k - 2))
        if k == 1:
            for copy in hot_copies(True):
                copy.wait_recv()
        for s in range(SUBS):
            for side in "rl":
                if goes(side, k, s):
                    f_ring(side, k, s).wait_recv()
                if goes(side, k + 1, s):
                    f_ring(side, k + 1, s).start()
            if s == SUBS - 1:
                f_exchange(nz - k, f_right[k])
                if k < half:
                    f_exchange(k, f_left[k])
            share_out(work, s)
    messages(half)

    def finish(j, carry):
        rows = pl.ds(pl.multiple_of(j * size, size), size)
        inv = inverse[rows]
        pre = base[rows] + total[rows] * inv
        s = jax.nn.sigmoid(pre)
        hidden[rows] = (pre * s).astype(BF16)
        g = (cotangent[rows].astype(F32) * s * (1.0 + pre * (1.0 - s))).astype(BF16)
        grad[rows] = g
        scaled[j] = (g.astype(F32) * inv).astype(BF16)
        return carry

    lax.fori_loop(0, blocks, finish, 0)

    back, came, mine, far, near = (r[n] for n in ("back", "came", "mine", "far", "near"))
    b_right = [r["b_right%d" % k] for k in range(half)]
    b_left = [r["b_left%d" % k] for k in range(half)]

    def b_copy(zoff, d, coming):
        return remote(
            back.at[d - 1, zoff],
            came.at[d - 1 if coming else NX - d - 1, zoff],
            r["bx_send"].at[d - 1, zoff],
            r["bx_recv"].at[d - 1 if coming else NX - d - 1, zoff],
            x_peers[d - 1],
        )

    def b_make(zoff):
        made = []
        for d in range(NX):
            block = target[jnp.maximum(asked[0, 1, owner_at(zoff, d)], 0)]
            made.append(jnp.dot(turned[spot(zoff), d], scaled[block], preferred_element_type=F32).astype(BF16))
        for d in range(1, NX):
            back[d - 1, zoff] = made[d]
        mine[zoff] = made[0]
        for d in range(1, NX):
            b_copy(zoff, d, False).start()

    def b_exchange(k):
        return [functools.partial(b_make, zoff) for zoff in offsets(k)]

    def b_done(k):
        for s in range(SUBS):
            for side in "rl":
                if k >= 1 and goes(side, k, s):
                    b_ring(side, k, s).wait_send()
        for zoff in offsets(k):
            for d in range(1, NX):
                b_copy(zoff, d, False).wait_send()

    def b_arrive(zoff):
        for d in range(1, NX):
            b_copy(zoff, d, True).wait_recv()

    step_rows = min(size, 64)

    def add_local(dst, sources, s, zoff):
        wanted = [asked[d, 0, owner_at(zoff, 0)] for d in range(NX)]

        def body(i, carry):
            rows = pl.ds(pl.multiple_of(i * step_rows, step_rows), step_rows)
            terms = [mine[zoff, rows]] + [came[d - 1, zoff, rows] for d in range(1, NX)]
            for j in range(s * per, (s + 1) * per):
                sums = None
                for d in range(NX):
                    term = jnp.where(wanted[d] == j, terms[d], jnp.zeros_like(terms[d]))
                    sums = term if sums is None else sums + term
                for source in sources:
                    sums = sums + source[j, rows]
                dst[j, rows] = sums
            return carry

        lax.fori_loop(0, size // step_rows, body, 0)

    def b_ring(side, k, s):
        part = pl.ds(s * per, per)
        bufs, to = (b_right, to_right) if side == "r" else (b_left, to_left)
        src = far if k == half else bufs[k]
        return remote(
            src.at[part], bufs[k - 1].at[part], r["bs_" + side].at[k - 1, s], r["br_" + side].at[k - 1, s], to
        )

    group = selfs.mine.shape[1]

    def weight_product(rhs, dest):
        many = nz // 2

        def body(i, carry):
            rows = pl.ds(pl.multiple_of(i * many * group, many * group), many * group)
            value = jnp.dot(feat_t[rows], rhs, preferred_element_type=F32)
            for q in range(many):
                dest.mine[i * many + q] = value[q * group : (q + 1) * group].astype(dest.mine.dtype)
            return carry

        lax.fori_loop(0, 2, body, 0)

    def self_start():
        weight_product(grad[...], selfs)
        selfs.stage1()

    def author_start():
        def body(i, carry):
            rows = pl.ds(pl.multiple_of(i * hot_total // 2, hot_total // 2), hot_total // 2)
            value = jnp.dot(counts[rows], grad[...], preferred_element_type=F32) * (1.0 / HK)
            for q in range(nh // 2):
                authors.mine[i * (nh // 2) + q] = value[q * hot_rows : (q + 1) * hot_rows]
            return carry

        lax.fori_loop(0, 2, body, 0)
        authors.stage1()

    extras = [
        [self_start],
        [author_start],
        [selfs.stage2],
        [authors.stage2],
        [selfs.stage3, authors.stage3],
        [selfs.stage4],
        [authors.stage4],
        [authors.stage5],
    ]
    for item in b_exchange(half) + b_exchange(half - 1):
        item()
    for k in range(half, 0, -1):
        work = b_exchange(k - 2) if k >= 2 else []
        for group_of in extras[(half - k) * 8 // half : (half - k + 1) * 8 // half]:
            work += group_of
        if k == half:
            work += [functools.partial(f_done, half - 1), functools.partial(f_done, half)]
        if k + 2 <= half:
            work.append(functools.partial(b_done, k + 2))
        for zoff in offsets(k):
            b_arrive(zoff)
        for s in range(SUBS):
            for side in "rl":
                if not goes(side, k, s):
                    continue
                bufs = b_right if side == "r" else b_left
                sources = []
                if k < half and goes(side, k + 1, s):
                    b_ring(side, k + 1, s).wait_recv()
                    sources = [bufs[k]]
                add_local(far if k == half else bufs[k], sources, s, k if side == "r" else nz - k)
                b_ring(side, k, s).start()
            share_out(work, s)
    b_arrive(0)
    for s in range(SUBS):
        b_ring("r", 1, s).wait_recv()
        b_ring("l", 1, s).wait_recv()
        add_local(near, [b_right[0], b_left[0]], s, 0)
    weight_product(near[...].reshape(blocks * size, width), cites)
    cites.stage1()
    selfs.finish(self_out)
    authors.finish(author_out)
    for copy in ask_copies(False) + hot_copies(False):
        copy.wait_send()
    for k in (2, 1, 0):
        b_done(k)
    cites.stage2()
    selfs.drain()
    cites.stage3()
    authors.drain()
    cites.stage4()
    cites.finish(cite_out)
    cites.drain()


def layer(nz, nh, feat, w_cite, w_self, hot, ids, req, values, cotangent, used, target):
    half = nz // 2
    rows, din = feat.shape
    width = w_self.shape[1]
    size = values.shape[1]
    blocks = rows // size
    hot_total = hot.shape[0] * nh
    share = din // (nz * NX)
    vmem = pl.BlockSpec(memory_space=pltpu.VMEM)
    smem = pl.BlockSpec(memory_space=pltpu.SMEM)
    dma = pltpu.SemaphoreType.DMA
    chunk = pltpu.VMEM((blocks, size, width), BF16)
    column = pltpu.VMEM((NX - 1, nz, size, width), BF16)
    scratch = {
        "own": chunk,
        "packed": column,
        "table": pltpu.VMEM((hot_total, width), BF16),
        "asks": pltpu.VMEM((NX,) + req.shape, jnp.int32),
        "asked": pltpu.SMEM((NX,) + req.shape, jnp.int32),
        "arrived": pltpu.VMEM((nz, NX, size, width), BF16),
        "spread": pltpu.VMEM((2, rows, 2 * NX * size), BF16),
        "turned": pltpu.VMEM((nz, NX, size, size), BF16),
        "counts": pltpu.VMEM((hot_total, rows), BF16),
        "feat_t": pltpu.VMEM((din, rows), BF16),
        "base": pltpu.VMEM((rows, width), F32),
        "total": pltpu.VMEM((rows, width), F32),
        "degree": pltpu.VMEM((rows, size), F32),
        "inverse": pltpu.VMEM((rows, width), F32),
        "grad": pltpu.VMEM((rows, width), BF16),
        "scaled": chunk,
        "back": column,
        "came": column,
        "mine": pltpu.VMEM((nz, size, width), BF16),
        "far": chunk,
        "near": chunk,
        "h_send": dma((nh - 1,)),
        "h_recv": dma((nh - 1,)),
        "q_send": dma((NX - 1,)),
        "q_recv": dma((NX - 1,)),
        "q_local": dma,
    }
    for k in range(1, half + 1):
        scratch["f_right%d" % k] = chunk
    for k in range(1, half):
        scratch["f_left%d" % k] = chunk
    for k in range(half):
        scratch["b_right%d" % k] = chunk
        scratch["b_left%d" % k] = chunk
    for name in ("fs_r", "fr_r", "fs_l", "fr_l", "bs_r", "br_r", "bs_l", "br_l"):
        scratch[name] = dma((half, SUBS))
    for name in ("fx_send", "fx_recv", "bx_send", "bx_recv"):
        scratch[name] = dma((NX - 1, nz))
    for name, parts in (
        ("self", WeightSum.scratch(nz, nh, share, width, F32)),
        ("cite", WeightSum.scratch(nz, nh, share, width, BF16)),
        ("author", AuthorSum.scratch(nz, nh, hot.shape[0], width)),
    ):
        for i, part in enumerate(parts):
            scratch[name + str(i)] = part
    names = ["in%d" % i for i in range(10)] + ["out%d" % i for i in range(4)] + list(scratch)
    return pl.pallas_call(
        functools.partial(layer_kernel, names, nz, nh),
        out_shape=(
            jax.ShapeDtypeStruct((rows, width), BF16),
            jax.ShapeDtypeStruct((share, width), F32),
            jax.ShapeDtypeStruct((share, width), F32),
            jax.ShapeDtypeStruct(hot.shape, F32),
        ),
        in_specs=[vmem] * 8 + [smem] * 2,
        out_specs=(vmem,) * 4,
        scratch_shapes=list(scratch.values()),
        compiler_params=pltpu.CompilerParams(
            collective_id=1, has_side_effects=True, vmem_limit_bytes=VMEM_LIMIT
        ),
    )(feat, w_cite, w_self, hot, ids, req, values, cotangent, used, target)


def hand_over_kernel(*refs):
    half = len(refs) // 2
    for src, dst in zip(refs[:half], refs[half:]):
        dst[...] = src[...]


def hand_over(arrays):
    vmem = pl.BlockSpec(memory_space=pltpu.VMEM)
    return pl.pallas_call(
        hand_over_kernel,
        out_shape=tuple(jax.ShapeDtypeStruct(a.shape, a.dtype) for a in arrays),
        in_specs=[vmem] * len(arrays),
        out_specs=(vmem,) * len(arrays),
    )(*arrays)


def on_device(
    paper_features,
    self_weight,
    cite_weight,
    hot_embed,
    hot_ids,
    tile_values,
    tile_rows,
    tile_target_block,
    tile_block,
    tile_owner,
    cotangent,
):
    wide = lax.axis_size("wide")
    nh = lax.axis_size("hot")
    nz = wide // NX
    tiles = tile_values.shape[0]
    shape = (8, tiles, max(128, wide))
    what = jnp.where(
        lax.broadcasted_iota(jnp.int32, shape, 0) == 0,
        tile_block[None, :, None],
        lax.broadcasted_iota(jnp.int32, shape, 1),
    )
    owned = tile_owner[None, :, None] == lax.broadcasted_iota(jnp.int32, shape, 2)
    req = jnp.max(jnp.where(owned, what, -1), axis=1)
    return hand_over(
        layer(
            nz,
            nh,
            paper_features,
            cite_weight,
            self_weight,
            hot_embed,
            hot_ids.T,
            req,
            tile_values,
            cotangent,
            tile_rows,
            tile_target_block,
        )
    )


def solution(mesh):
    return jax.shard_map(
        on_device,
        mesh=mesh,
        in_specs=(
            P(("wide", "hot"), None),
            P(),
            P(),
            P("hot", None),
            P(("wide", "hot"), None),
            P(("wide", "hot"), None, None),
            P(("wide", "hot")),
            P(("wide", "hot")),
            P(("wide", "hot")),
            P(("wide", "hot")),
            P(("wide", "hot"), None),
        ),
        out_specs=(P(("wide", "hot"), None), P("wide", None), P("wide", None), P("hot", None)),
        check_vma=False,
    )
```

```python
import functools

import jax
import jax.numpy as jnp
from jax import lax
from jax.experimental import pallas as pl
from jax.experimental.pallas import tpu as pltpu
from jax.sharding import PartitionSpec as P

HK = 8
NX = 4
SUBS = 4
PAD = 16
MESH = pl.DeviceIdType.MESH
F32 = jnp.float32
BF16 = jnp.bfloat16
VMEM_LIMIT = 58 * 1024 * 1024


def place(nz):
    w = lax.axis_index("wide")
    h = lax.axis_index("hot")
    return w // NX, w % NX, w, h


def greet(partners):
    barrier = pltpu.get_barrier_semaphore()
    for partner in partners:
        pl.semaphore_signal(barrier, inc=1, device_id=partner, device_id_type=MESH)
    return lambda: pl.semaphore_wait(barrier, len(partners))


def remote(src, dst, send, recv, target):
    return pltpu.make_async_remote_copy(
        src_ref=src, dst_ref=dst, send_sem=send, recv_sem=recv, device_id=target, device_id_type=MESH
    )


class WeightSum:
    def __init__(self, where, nz, nh, refs):
        self.z, self.x, self.w, self.h = where
        self.nz, self.nh = nz, nh
        (self.mine, self.got1, self.mid, self.got2, self.last, self.got3, self.done) = refs[:7]
        (self.wide, self.s1, self.r1, self.s2, self.r2, self.s3, self.r3, self.s4, self.r4) = refs[7:16]
        self.share = self.mine.shape[1] // NX

    @staticmethod
    def scratch(nz, nh, share, width, kind):
        dma = pltpu.SemaphoreType.DMA
        two = nz // nh
        return [
            pltpu.VMEM((nz, NX * share, width), kind),
            pltpu.VMEM((nh - 1, two, NX * share, width), kind),
            pltpu.VMEM((NX, two, PAD, width), BF16),
            pltpu.VMEM((NX - 1, two, PAD, width), BF16),
            pltpu.VMEM((two, PAD, width), BF16),
            pltpu.VMEM((nz - 1, PAD, width), BF16),
            pltpu.VMEM((PAD, width), F32),
            pltpu.VMEM((NX, two, PAD, width), F32),
            dma((nh - 1, two)),
            dma((nh - 1, two)),
            dma((NX - 1,)),
            dma((NX - 1,)),
            dma((two,)),
            dma((nz - 1,)),
            dma((nh - 1,)),
            dma,
        ]

    def copies1(self):
        out = []
        for d in range(1, self.nh):
            peer = lax.rem(self.h + d, self.nh)
            for i in range(self.nz // self.nh):
                e = self.nh - d - 1
                out.append(
                    remote(
                        self.mine.at[peer + i * self.nh],
                        self.got1.at[e, i],
                        self.s1.at[d - 1, i],
                        self.r1.at[e, i],
                        (self.w, peer),
                    )
                )
        return out

    def copies2(self):
        out = []
        for d in range(1, NX):
            peer = lax.rem(self.x + d, NX)
            e = NX - d - 1
            out.append(
                remote(
                    self.mid.at[peer],
                    self.got2.at[e],
                    self.s2.at[d - 1],
                    self.r2.at[e],
                    (self.z * NX + peer, self.h),
                )
            )
        return out

    def each3(self, act):
        for i in range(self.nz // self.nh):
            there = self.h + i * self.nh
            off = lax.rem(self.z - there + self.nz, self.nz)

            @pl.when(off != 0)
            def _():
                act(
                    remote(
                        self.last.at[i],
                        self.got3.at[off - 1],
                        self.s3.at[i],
                        self.r3.at[off - 1],
                        (there * NX + self.x, self.h),
                    )
                )

    def copies4(self):
        return [
            remote(
                self.done, self.done, self.s4.at[d - 1], self.r4, (self.w, lax.rem(self.h + d, self.nh))
            )
            for d in range(1, self.nh)
        ]

    def stage1(self):
        for copy in self.copies1():
            copy.start()

    def stage2(self):
        self.wide[...] = jnp.zeros_like(self.wide)
        for copy in self.copies1():
            copy.wait_recv()
        for i in range(self.nz // self.nh):
            sums = self.mine[self.h + i * self.nh].astype(F32)
            for e in range(self.nh - 1):
                sums = sums + self.got1[e, i].astype(F32)
            for peer in range(NX):
                self.wide[peer, i, : self.share] = sums[peer * self.share : (peer + 1) * self.share]
        self.mid[...] = self.wide[...].astype(BF16)
        for copy in self.copies2():
            copy.start()

    def stage3(self):
        for copy in self.copies2():
            copy.wait_recv()
        sums = self.wide[self.x]
        for e in range(NX - 1):
            sums = sums + self.got2[e].astype(F32)
        self.wide[self.x] = sums
        self.last[...] = sums.astype(BF16)
        self.each3(lambda copy: copy.start())

    def stage4(self):
        @pl.when(lax.rem(self.z, self.nh) == self.h)
        def _():
            for o in range(self.nz - 1):
                remote(
                    self.last.at[0], self.got3.at[o], self.s3.at[0], self.r3.at[o], (self.w, self.h)
                ).wait_recv()
            sums = self.wide[self.x, self.z // self.nh]
            for o in range(self.nz - 1):
                sums = sums + self.got3[o].astype(F32)
            self.done[...] = sums
            for copy in self.copies4():
                copy.start()

    def finish(self, out):
        @pl.when(lax.rem(self.z, self.nh) != self.h)
        def _():
            self.copies4()[0].wait_recv()

        out[...] = self.done[: self.share]

    def drain(self):
        for copy in self.copies1() + self.copies2():
            copy.wait_send()
        self.each3(lambda copy: copy.wait_send())

        @pl.when(lax.rem(self.z, self.nh) == self.h)
        def _():
            for copy in self.copies4():
                copy.wait_send()


class AuthorSum:
    def __init__(self, where, nz, nh, refs):
        self.z, self.x, self.w, self.h = where
        self.nz, self.nh, self.np = nz, nh, nz // 2
        (self.mine, self.got1, self.mid, self.got2, self.cut, self.got3, self.sums4, self.rows5) = refs[:8]
        (self.s1, self.r1, self.s2, self.r2, self.s3, self.r3, self.s4, self.r4, self.s5, self.r5) = refs[8:18]

    @staticmethod
    def scratch(nz, nh, rows, width):
        dma = pltpu.SemaphoreType.DMA
        part = rows // NX
        pieces = nz // 2
        return [
            pltpu.VMEM((nh, rows, width), F32),
            pltpu.VMEM((nh - 1, rows, width), F32),
            pltpu.VMEM((NX, part, width), F32),
            pltpu.VMEM((NX - 1, part, width), F32),
            pltpu.VMEM((pieces, 8, width // 2), F32),
            pltpu.VMEM((nz - 1, 8, width // 2), F32),
            pltpu.VMEM((pieces, 8, width // 2), F32),
            pltpu.VMEM((NX, part, width), F32),
            dma((nh - 1,)),
            dma((nh - 1,)),
            dma((NX - 1,)),
            dma((NX - 1,)),
            dma((nz - 1,)),
            dma((nz - 1,)),
            dma((pieces - 1,)),
            dma((pieces - 1,)),
            dma((NX - 1,)),
            dma((NX - 1,)),
        ]

    def copies1(self):
        out = []
        for d in range(1, self.nh):
            peer = lax.rem(self.h + d, self.nh)
            e = self.nh - d - 1
            out.append(
                remote(self.mine.at[peer], self.got1.at[e], self.s1.at[d - 1], self.r1.at[e], (self.w, peer))
            )
        return out

    def copies2(self):
        out = []
        for d in range(1, NX):
            peer = lax.rem(self.x + d, NX)
            e = NX - d - 1
            to = (self.z * NX + peer, self.h)
            out.append(remote(self.mid.at[peer], self.got2.at[e], self.s2.at[d - 1], self.r2.at[e], to))
        return out

    def copies3(self):
        out = []
        for d in range(1, self.nz):
            peer = lax.rem(self.z + d, self.nz)
            e = self.nz - d - 1
            to = (peer * NX + self.x, self.h)
            out.append(
                remote(
                    self.cut.at[lax.rem(peer, self.np)], self.got3.at[e], self.s3.at[d - 1], self.r3.at[e], to
                )
            )
        return out

    def copies4(self, coming=False):
        out = []
        p = lax.rem(self.z, self.np)
        for d in range(1, self.np):
            other = lax.rem(p + d, self.np)
            to = ((self.z - p + other) * NX + self.x, self.h)
            e = d - 1 if coming else self.np - d - 1
            piece = self.sums4.at[other if coming else p]
            out.append(remote(piece, piece, self.s4.at[d - 1], self.r4.at[e], to))
        return out

    def copies5(self, coming=False):
        out = []
        for d in range(1, NX):
            peer = lax.rem(self.x + d, NX)
            e = d - 1 if coming else NX - d - 1
            rows = self.rows5.at[peer if coming else self.x]
            out.append(remote(rows, rows, self.s5.at[d - 1], self.r5.at[e], (self.z * NX + peer, self.h)))
        return out

    def stage1(self):
        for copy in self.copies1():
            copy.start()

    def stage2(self):
        for copy in self.copies1():
            copy.wait_recv()
        sums = self.mine[self.h]
        for e in range(self.nh - 1):
            sums = sums + self.got1[e]
        self.mid[...] = sums.reshape(self.mid.shape)
        for copy in self.copies2():
            copy.start()

    def stage3(self):
        for copy in self.copies2():
            copy.wait_recv()
        sums = self.mid[self.x]
        for e in range(NX - 1):
            sums = sums + self.got2[e]
        lanes = self.cut.shape[2]
        for p in range(self.np):
            g, c = p // 2, p % 2
            self.cut[p] = sums[g * 8 : (g + 1) * 8, c * lanes : (c + 1) * lanes]
        for copy in self.copies3():
            copy.start()

    def stage4(self):
        for copy in self.copies3():
            copy.wait_recv()
        p = lax.rem(self.z, self.np)
        sums = self.cut[p]
        for e in range(self.nz - 1):
            sums = sums + self.got3[e]
        self.sums4[p] = sums
        for copy in self.copies4():
            copy.start()

    def stage5(self):
        for copy in self.copies4(True):
            copy.wait_recv()
        lanes = self.cut.shape[2]
        for p in range(self.np):
            g, c = p // 2, p % 2
            self.rows5[self.x, g * 8 : (g + 1) * 8, c * lanes : (c + 1) * lanes] = self.sums4[p]
        for copy in self.copies5():
            copy.start()

    def finish(self, out):
        for copy in self.copies5(True):
            copy.wait_recv()
        out[...] = self.rows5[...].reshape(out.shape)

    def drain(self):
        for copy in self.copies1() + self.copies2() + self.copies3() + self.copies4() + self.copies5():
            copy.wait_send()


def layer_kernel(names, nz, nh, *refs):
    r = dict(zip(names, refs))
    half = nz // 2
    feat, w_cite, w_self, hot, ids, req, values, cotangent, used, target = refs[:10]
    hidden, self_out, cite_out, author_out = refs[10:14]
    own, packed, table, asks, asked, arrived = (
        r[n] for n in ("own", "packed", "table", "asks", "asked", "arrived")
    )
    spread, turned, counts, feat_t, base, total, grad, scaled = (
        r[n] for n in ("spread", "turned", "counts", "feat_t", "base", "total", "grad", "scaled")
    )
    degree, inverse = r["degree"], r["inverse"]
    where = place(nz)
    z, x, w, h = where
    selfs = WeightSum(where, nz, nh, [r["self%d" % i] for i in range(16)])
    cites = WeightSum(where, nz, nh, [r["cite%d" % i] for i in range(16)])
    authors = AuthorSum(where, nz, nh, [r["author%d" % i] for i in range(18)])
    blocks, size, width = own.shape
    hot_rows = hot.shape[0]
    hot_total = table.shape[0]
    per = blocks // SUBS
    to_right = (lax.rem(z + 1, nz) * NX + x, h)
    to_left = (lax.rem(z + nz - 1, nz) * NX + x, h)
    z_peers = [(lax.rem(z + d, nz) * NX + x, h) for d in range(1, nz)]
    x_peers = [(z * NX + lax.rem(x + d, NX), h) for d in range(1, NX)]
    h_peers = [(w, lax.rem(h + d, nh)) for d in range(1, nh)]
    wait_all = greet(z_peers + x_peers + h_peers)

    my_rows = pl.ds(pl.multiple_of(h * hot_rows, hot_rows), hot_rows)
    table[my_rows] = hot[...].astype(BF16)
    asks[0] = req[...]

    def spot(zoff):
        if zoff == 0:
            return 0
        return 2 * zoff if zoff < half else 2 * (nz - zoff) - 1

    def offsets(k):
        return [0] if k == 0 else [half] if k == half else [nz - k, k]

    last, few = half - 2, NX // 2
    f_right = [own] + [r["f_right%d" % k] for k in range(1, last + 1)]
    f_left = [own] + [r["f_left%d" % k] for k in range(1, last + 1)]
    rows_f32 = lax.broadcasted_iota(jnp.int32, (size, size), 0)
    far_devices = {"r": list(range(few)), "l": list(range(few, NX))}
    ahead = {"r": (0, 2), "l": (1, 3)}
    behind = {"r": (1, 3), "l": (0, 2)}
    side_to = {"r": to_right, "l": to_left}

    def goes(side, k, s):
        return k <= last

    def f_ring(side, k, s):
        part = pl.ds(s * per, per)
        bufs, to = (f_right if side == "r" else f_left), side_to[side]
        return remote(
            bufs[k - 1].at[part],
            bufs[k].at[part],
            r["fs_" + side].at[k - 1, s],
            r["fr_" + side].at[k - 1, s],
            to,
        )

    def project(j, carry):
        rows = pl.ds(pl.multiple_of(j * size, size), size)
        own[j] = jnp.dot(feat[rows], w_cite[...], preferred_element_type=F32).astype(BF16)
        return carry

    lax.fori_loop(0, blocks, project, 0)
    wait_all()
    for s in range(SUBS):
        for side in "rl":
            if goes(side, 1, s):
                f_ring(side, 1, s).start()

    def ask_copies(coming):
        return [
            remote(
                asks.at[0],
                asks.at[d if coming else NX - d],
                r["q_send"].at[d - 1],
                r["q_recv"].at[d - 1 if coming else NX - d - 1],
                x_peers[d - 1],
            )
            for d in range(1, NX)
        ]

    def hot_copies(coming):
        out = []
        for d in range(1, nh):
            peer = lax.rem(h + d, nh) if coming else h
            rows = table.at[pl.ds(pl.multiple_of(peer * hot_rows, hot_rows), hot_rows)]
            e = d - 1 if coming else nh - d - 1
            out.append(remote(rows, rows, r["h_send"].at[d - 1], r["h_recv"].at[e], h_peers[d - 1]))
        return out

    for copy in ask_copies(False) + hot_copies(False):
        copy.start()
    for copy in ask_copies(True):
        copy.wait_recv()
    local = pltpu.make_async_copy(asks, asked, r["q_local"])
    local.start()
    local.wait()

    def near_copies(coming):
        out = []
        for m, off in enumerate((1, -1, 2, -2)):
            to = (lax.rem(z - off + nz, nz) * NX + x, h)
            out.append(remote(asks, r["nears"].at[m], r["n_send"].at[m], r["n_recv"].at[m], to))
        return out

    for copy in near_copies(False):
        copy.start()
    nearby = r["nearby"]

    def near_arrive():
        for copy in near_copies(True):
            copy.wait_recv()
        copy = pltpu.make_async_copy(r["nears"], nearby, r["n_local"])
        copy.start()
        copy.wait()

    def f_hand(side, g):
        part = pl.ds(g * few, few)
        return remote(
            r["f_pack_" + side].at[part],
            r["f_next_" + side].at[part],
            r["fhs_" + side].at[g],
            r["fhr_" + side].at[g],
            side_to[side],
        )

    def f_pass(side):
        return remote(
            r["f_next_" + side].at[pl.ds(0, few)],
            r["f_far_" + side],
            r["fps_" + side],
            r["fpr_" + side],
            side_to[side],
        )

    def f_pick(side, source):
        owner = lax.rem(z + nz + (-last if side == "r" else last), nz) * NX + x
        first, second = ahead[side]
        pack = r["f_pack_" + side]
        for i, d in enumerate(far_devices[side]):
            pack[i] = source[jnp.maximum(nearby[second, d, 0, owner], 0)]
        for d in range(NX):
            pack[few + d] = source[jnp.maximum(nearby[first, d, 0, owner], 0)]

    def f_source(zoff, d):
        if zoff == half:
            side = "r" if d < few else "l"
            return r["f_far_" + side].at[d - (0 if d < few else few)]
        if zoff in (half - 1, half + 1):
            return r["f_next_" + ("r" if zoff == half + 1 else "l")].at[few + d]
        return packed.at[d - 1, zoff]

    def f_spread(zoff):
        for d in range(1, NX):
            f_copy(zoff, d, False).start()
        arrived[spot(zoff), 0] = f_source(zoff, 0)[...]

    def owner_at(zoff, d):
        return lax.rem(z + zoff, nz) * NX + lax.rem(x + d, NX)

    def f_copy(zoff, d, coming):
        return remote(
            f_source(zoff, d),
            arrived.at[spot(zoff), d if coming else NX - d],
            r["fx_send"].at[d - 1, zoff],
            r["fx_recv"].at[d - 1 if coming else NX - d - 1, zoff],
            x_peers[d - 1],
        )

    def f_exchange(zoff, source):
        owner = owner_at(zoff, 0)
        for d in range(1, NX):
            packed[d - 1, zoff] = source[jnp.maximum(asked[d, 0, owner], 0)]
        for d in range(1, NX):
            f_copy(zoff, d, False).start()
        arrived[spot(zoff), 0] = source[jnp.maximum(asked[0, 0, owner], 0)]

    def tile_of(zoff, d):
        t = asked[0, 1, owner_at(zoff, d)]
        number = jnp.maximum(t, 0)
        return values[number].astype(F32), jnp.where(t < 0, 0, used[number]), target[number]

    def lay_out(k, zoff, d):
        held = spread.at[k % 2]
        n = offsets(k).index(zoff) * NX + d
        m, live, block = tile_of(zoff, d)
        turned[spot(zoff), d] = jnp.where(rows_f32 < live, m, 0.0).T.astype(BF16)

        def lay(j, carry):
            there = jnp.where(block == j, live, 0)
            rows = pl.ds(pl.multiple_of(j * size, size), size)
            laid = jnp.where(rows_f32 < there, m, 0.0)
            held[rows, n * size : (n + 1) * size] = laid.astype(BF16)
            degree[rows] = laid if k == 0 and n == 0 else degree[rows] + laid
            return carry

        lax.fori_loop(0, blocks, lay, 0)

    def invert():
        def body(j, carry):
            rows = pl.ds(pl.multiple_of(j * size, size), size)
            sums = jnp.sum(degree[rows], axis=1, keepdims=True)
            inverse[rows] = jnp.broadcast_to(1.0 / jnp.maximum(sums, 1.0), (size, width))
            return carry

        lax.fori_loop(0, blocks, body, 0)

    def prepare(k):
        return [functools.partial(lay_out, k, zoff, d) for zoff in offsets(k) for d in range(NX)]

    def share_out(work, s):
        for item in work[s * len(work) // SUBS : (s + 1) * len(work) // SUBS]:
            item()

    def messages(k):
        for zoff in offsets(k):
            for d in range(1, NX):
                f_copy(zoff, d, True).wait_recv()
        first = spot(offsets(k)[0])
        count = len(offsets(k))
        span = count * NX * size

        step = blocks * size // 2

        def gather(j, carry):
            rows = pl.ds(pl.multiple_of(j * step, step), step)
            more = jnp.dot(
                spread[k % 2, rows, :span],
                arrived[first : first + count].reshape(span, width),
                preferred_element_type=F32,
            )
            total[rows] = more if k == 0 else total[rows] + more
            return carry

        lax.fori_loop(0, 2, gather, 0)

    def count(i):
        rows = pl.ds(i * size, size)

        def body(a, carry):
            there = pl.ds(pl.multiple_of(a * hot_rows, hot_rows), hot_rows)
            names = lax.broadcasted_iota(jnp.int32, (hot_rows, size), 0) + a * hot_rows
            many = jnp.zeros((hot_rows, size), F32)
            for k in range(HK):
                many = many + jnp.where(ids[k : k + 1, rows] == names, 1.0, 0.0)
            counts[there, rows] = many.astype(BF16)
            return carry

        lax.fori_loop(0, nh, body, 0)

    def start_rows(i):
        rows = pl.ds(i * size, size)
        mix = lax.dot_general(
            counts[:, rows], table[...], (((0,), (0,)), ((), ())), preferred_element_type=F32
        )
        base[rows] = jnp.dot(feat[rows], w_self[...], preferred_element_type=F32) + mix * (1.0 / HK)

    def turn(i):
        rows = pl.ds(i * size, size)
        feat_t[:, rows] = feat[rows].astype(F32).T.astype(BF16)

    def f_done(k):
        for side in "rl":
            if 1 <= k <= last:
                for s in range(SUBS):
                    f_ring(side, k, s).wait_send()
            elif k == last + 1:
                for g in range(3):
                    f_hand(side, g).wait_send()
            elif k == half:
                f_pass(side).wait_send()
        for zoff in offsets(k):
            for d in range(1, NX):
                f_copy(zoff, d, False).wait_send()

    f_exchange(0, own)
    for item in prepare(0) + prepare(1):
        item()
    for k in range(1, half + 1):
        work = []
        for i in range(blocks):
            if i * (half - 1) // blocks == k - 1:
                work += [functools.partial(part, i) for part in (turn, count, start_rows)]
        work.append(functools.partial(messages, k - 1))
        if k < half:
            work += prepare(k + 1)
        else:
            work.append(invert)
        if k >= 2:
            work.append(functools.partial(f_done, k - 2))
        if k == 1:
            for copy in hot_copies(True):
                copy.wait_recv()
        if k == last:
            work = [near_arrive] + work
        if k <= last:
            for s in range(SUBS):
                for side in "rl":
                    f_ring(side, k, s).wait_recv()
                    if goes(side, k + 1, s):
                        f_ring(side, k + 1, s).start()
                if s < SUBS - 1:
                    share_out(work, s)
            if k == last:
                for side, bufs in (("r", f_right), ("l", f_left)):
                    f_pick(side, bufs[last])
                    for g in range(3):
                        f_hand(side, g).start()
            f_exchange(nz - k, f_right[k])
            f_exchange(k, f_left[k])
            share_out(work, SUBS - 1)
        elif k == last + 1:
            for side in "rl":
                f_hand(side, 0).wait_recv()
                f_pass(side).start()
            for g in (1, 2):
                for side in "rl":
                    f_hand(side, g).wait_recv()
            f_spread(half + 1)
            f_spread(half - 1)
            for item in work:
                item()
        else:
            for side in "rl":
                f_pass(side).wait_recv()
            f_spread(half)
            for item in work:
                item()
    messages(half)

    def finish(j, carry):
        rows = pl.ds(pl.multiple_of(j * size, size), size)
        inv = inverse[rows]
        pre = base[rows] + total[rows] * inv
        s = jax.nn.sigmoid(pre)
        hidden[rows] = (pre * s).astype(BF16)
        g = (cotangent[rows].astype(F32) * s * (1.0 + pre * (1.0 - s))).astype(BF16)
        grad[rows] = g
        scaled[j] = (g.astype(F32) * inv).astype(BF16)
        return carry

    lax.fori_loop(0, blocks, finish, 0)

    back, came, mine, near = (r[n] for n in ("back", "came", "mine", "near"))
    b_right = [r["b_right%d" % k] for k in range(last + 1)]
    b_left = [r["b_left%d" % k] for k in range(last + 1)]

    def b_copy(zoff, d, coming):
        return remote(
            back.at[d - 1, zoff],
            came.at[d - 1 if coming else NX - d - 1, zoff],
            r["bx_send"].at[d - 1, zoff],
            r["bx_recv"].at[d - 1 if coming else NX - d - 1, zoff],
            x_peers[d - 1],
        )

    def b_make(zoff):
        made = []
        for d in range(NX):
            block = target[jnp.maximum(asked[0, 1, owner_at(zoff, d)], 0)]
            made.append(jnp.dot(turned[spot(zoff), d], scaled[block], preferred_element_type=F32).astype(BF16))
        for d in range(1, NX):
            back[d - 1, zoff] = made[d]
        mine[zoff] = made[0]
        for d in range(1, NX):
            b_copy(zoff, d, False).start()

    def b_exchange(k):
        return [functools.partial(b_make, zoff) for zoff in offsets(k)]

    def b_done(k):
        for side in "rl":
            if 1 <= k <= last:
                for s in range(SUBS):
                    b_ring(side, k, s).wait_send()
            elif k == last + 1:
                b_onward(side).wait_send()
                for d in range(NX):
                    b_hand(side, d).wait_send()
            elif k == half:
                for i in range(few):
                    b_pass(side, i).wait_send()
        for zoff in offsets(k):
            for d in range(1, NX):
                b_copy(zoff, d, False).wait_send()

    def b_arrive(zoff):
        for d in range(1, NX):
            b_copy(zoff, d, True).wait_recv()

    step_rows = min(size, 64)

    def b_source(zoff, d):
        return mine.at[zoff] if d == 0 else came.at[d - 1, zoff]

    def b_pass(side, i):
        return remote(
            b_source(half, far_devices[side][i]),
            r["b_far_" + side].at[i],
            r["bps_" + side].at[i],
            r["bpr_" + side].at[i],
            side_to[side],
        )

    def b_onward(side):
        return remote(
            r["b_far_" + side],
            r["b_next_" + side].at[pl.ds(0, few)],
            r["bos_" + side],
            r["bor_" + side],
            side_to[side],
        )

    def b_hand(side, d):
        return remote(
            b_source(half - 1 if side == "r" else half + 1, d),
            r["b_next_" + side].at[few + d],
            r["bhs_" + side].at[d],
            r["bhr_" + side].at[d],
            side_to[side],
        )

    def loose(side):
        owner = owner_at(last if side == "r" else nz - last, 0)
        first, second = behind[side]
        held = r["b_next_" + side]
        out = [(nearby[second, d, 0, owner], held.at[i]) for i, d in enumerate(far_devices[side])]
        return out + [(nearby[first, d, 0, owner], held.at[few + d]) for d in range(NX)]

    def add_local(dst, sources, s, zoff, others=()):
        wanted = [asked[d, 0, owner_at(zoff, 0)] for d in range(NX)] + [place for place, _ in others]

        def body(i, carry):
            rows = pl.ds(pl.multiple_of(i * step_rows, step_rows), step_rows)
            terms = [mine[zoff, rows]] + [came[d - 1, zoff, rows] for d in range(1, NX)]
            terms += [block[rows] for _, block in others]
            for j in range(s * per, (s + 1) * per):
                sums = None
                for d in range(len(terms)):
                    term = jnp.where(wanted[d] == j, terms[d], jnp.zeros_like(terms[d]))
                    sums = term if sums is None else sums + term
                for source in sources:
                    sums = sums + source[j, rows]
                dst[j, rows] = sums
            return carry

        lax.fori_loop(0, size // step_rows, body, 0)

    def b_ring(side, k, s):
        part = pl.ds(s * per, per)
        bufs, to = (b_right if side == "r" else b_left), side_to[side]
        return remote(
            bufs[k].at[part], bufs[k - 1].at[part], r["bs_" + side].at[k - 1, s], r["br_" + side].at[k - 1, s], to
        )

    group = selfs.mine.shape[1]

    def weight_product(rhs, dest):
        many = nz // 2

        def body(i, carry):
            rows = pl.ds(pl.multiple_of(i * many * group, many * group), many * group)
            value = jnp.dot(feat_t[rows], rhs, preferred_element_type=F32)
            for q in range(many):
                dest.mine[i * many + q] = value[q * group : (q + 1) * group].astype(dest.mine.dtype)
            return carry

        lax.fori_loop(0, 2, body, 0)

    def self_start():
        weight_product(grad[...], selfs)
        selfs.stage1()

    def author_start():
        def body(i, carry):
            rows = pl.ds(pl.multiple_of(i * hot_total // 2, hot_total // 2), hot_total // 2)
            value = jnp.dot(counts[rows], grad[...], preferred_element_type=F32) * (1.0 / HK)
            for q in range(nh // 2):
                authors.mine[i * (nh // 2) + q] = value[q * hot_rows : (q + 1) * hot_rows]
            return carry

        lax.fori_loop(0, 2, body, 0)
        authors.stage1()

    extras = [
        [self_start],
        [author_start],
        [selfs.stage2],
        [authors.stage2],
        [selfs.stage3, authors.stage3],
        [selfs.stage4],
        [authors.stage4],
        [authors.stage5],
    ]
    for item in b_exchange(half) + b_exchange(half - 1):
        item()
    for k in range(half, 0, -1):
        work = b_exchange(k - 2) if k >= 2 else []
        for group_of in extras[(half - k) * 8 // half : (half - k + 1) * 8 // half]:
            work += group_of
        if k == half:
            work += [functools.partial(f_done, half - 1), functools.partial(f_done, half)]
        if k + 2 <= half:
            work.append(functools.partial(b_done, k + 2))
        for zoff in offsets(k):
            b_arrive(zoff)
        if k == half:
            for i in range(few):
                for side in "rl":
                    b_pass(side, i).start()
            for item in work:
                item()
        elif k == last + 1:
            for d in range(NX):
                for side in "rl":
                    b_hand(side, d).start()
            for side in "rl":
                for i in range(few):
                    b_pass(side, i).wait_recv()
                b_onward(side).start()
            for item in work:
                item()
        else:
            if k == last:
                for side in "rl":
                    for d in range(NX):
                        b_hand(side, d).wait_recv()
                    b_onward(side).wait_recv()
            for s in range(SUBS):
                for side in "rl":
                    bufs = b_right if side == "r" else b_left
                    sources, others = [], ()
                    if k < last:
                        b_ring(side, k + 1, s).wait_recv()
                        sources = [bufs[k]]
                    else:
                        others = loose(side)
                    add_local(bufs[k], sources, s, k if side == "r" else nz - k, others)
                    b_ring(side, k, s).start()
                share_out(work, s)
    b_arrive(0)
    for s in range(SUBS):
        b_ring("r", 1, s).wait_recv()
        b_ring("l", 1, s).wait_recv()
        add_local(near, [b_right[0], b_left[0]], s, 0)
    weight_product(near[...].reshape(blocks * size, width), cites)
    cites.stage1()
    selfs.finish(self_out)
    authors.finish(author_out)
    for copy in ask_copies(False) + hot_copies(False) + near_copies(False):
        copy.wait_send()
    for k in (2, 1, 0):
        b_done(k)
    cites.stage2()
    selfs.drain()
    cites.stage3()
    authors.drain()
    cites.stage4()
    cites.finish(cite_out)
    cites.drain()


def layer(nz, nh, feat, w_cite, w_self, hot, ids, req, values, cotangent, used, target):
    half = nz // 2
    rows, din = feat.shape
    width = w_self.shape[1]
    size = values.shape[1]
    blocks = rows // size
    hot_total = hot.shape[0] * nh
    share = din // (nz * NX)
    vmem = pl.BlockSpec(memory_space=pltpu.VMEM)
    smem = pl.BlockSpec(memory_space=pltpu.SMEM)
    dma = pltpu.SemaphoreType.DMA
    chunk = pltpu.VMEM((blocks, size, width), BF16)
    column = pltpu.VMEM((NX - 1, nz, size, width), BF16)
    scratch = {
        "own": chunk,
        "packed": column,
        "table": pltpu.VMEM((hot_total, width), BF16),
        "asks": pltpu.VMEM((NX,) + req.shape, jnp.int32),
        "asked": pltpu.SMEM((NX,) + req.shape, jnp.int32),
        "arrived": pltpu.VMEM((nz, NX, size, width), BF16),
        "spread": pltpu.VMEM((2, rows, 2 * NX * size), BF16),
        "turned": pltpu.VMEM((nz, NX, size, size), BF16),
        "counts": pltpu.VMEM((hot_total, rows), BF16),
        "feat_t": pltpu.VMEM((din, rows), BF16),
        "base": pltpu.VMEM((rows, width), F32),
        "total": pltpu.VMEM((rows, width), F32),
        "degree": pltpu.VMEM((rows, size), F32),
        "inverse": pltpu.VMEM((rows, width), F32),
        "grad": pltpu.VMEM((rows, width), BF16),
        "scaled": chunk,
        "back": column,
        "came": column,
        "mine": pltpu.VMEM((nz, size, width), BF16),
        "near": chunk,
        "h_send": dma((nh - 1,)),
        "h_recv": dma((nh - 1,)),
        "q_send": dma((NX - 1,)),
        "q_recv": dma((NX - 1,)),
        "q_local": dma,
    }
    few = NX // 2
    several = pltpu.VMEM((NX + few, size, width), BF16)
    scratch["nears"] = pltpu.VMEM((4, NX) + req.shape, jnp.int32)
    scratch["nearby"] = pltpu.SMEM((4, NX) + req.shape, jnp.int32)
    scratch["n_send"] = dma((4,))
    scratch["n_recv"] = dma((4,))
    scratch["n_local"] = dma
    for side, word in (("r", "right"), ("l", "left")):
        for k in range(1, half - 1):
            scratch["f_%s%d" % (word, k)] = chunk
        for k in range(half - 1):
            scratch["b_%s%d" % (word, k)] = chunk
        for name in ("f_pack_", "f_next_", "b_next_"):
            scratch[name + side] = several
        for name in ("f_far_", "b_far_"):
            scratch[name + side] = pltpu.VMEM((few, size, width), BF16)
        for name, count in (("fh", 3), ("bp", few), ("bh", NX)):
            scratch[name + "s_" + side] = dma((count,))
            scratch[name + "r_" + side] = dma((count,))
        for name in ("fp", "bo"):
            scratch[name + "s_" + side] = dma
            scratch[name + "r_" + side] = dma
    for name in ("fs_r", "fr_r", "fs_l", "fr_l", "bs_r", "br_r", "bs_l", "br_l"):
        scratch[name] = dma((half - 2, SUBS))
    for name in ("fx_send", "fx_recv", "bx_send", "bx_recv"):
        scratch[name] = dma((NX - 1, nz))
    for name, parts in (
        ("self", WeightSum.scratch(nz, nh, share, width, F32)),
        ("cite", WeightSum.scratch(nz, nh, share, width, BF16)),
        ("author", AuthorSum.scratch(nz, nh, hot.shape[0], width)),
    ):
        for i, part in enumerate(parts):
            scratch[name + str(i)] = part
    names = ["in%d" % i for i in range(10)] + ["out%d" % i for i in range(4)] + list(scratch)
    return pl.pallas_call(
        functools.partial(layer_kernel, names, nz, nh),
        out_shape=(
            jax.ShapeDtypeStruct((rows, width), BF16),
            jax.ShapeDtypeStruct((share, width), F32),
            jax.ShapeDtypeStruct((share, width), F32),
            jax.ShapeDtypeStruct(hot.shape, F32),
        ),
        in_specs=[vmem] * 8 + [smem] * 2,
        out_specs=(vmem,) * 4,
        scratch_shapes=list(scratch.values()),
        compiler_params=pltpu.CompilerParams(
            collective_id=1, has_side_effects=True, vmem_limit_bytes=VMEM_LIMIT
        ),
    )(feat, w_cite, w_self, hot, ids, req, values, cotangent, used, target)


def hand_over_kernel(*refs):
    half = len(refs) // 2
    for src, dst in zip(refs[:half], refs[half:]):
        dst[...] = src[...]


def hand_over(arrays):
    vmem = pl.BlockSpec(memory_space=pltpu.VMEM)
    return pl.pallas_call(
        hand_over_kernel,
        out_shape=tuple(jax.ShapeDtypeStruct(a.shape, a.dtype) for a in arrays),
        in_specs=[vmem] * len(arrays),
        out_specs=(vmem,) * len(arrays),
    )(*arrays)


def on_device(
    paper_features,
    self_weight,
    cite_weight,
    hot_embed,
    hot_ids,
    tile_values,
    tile_rows,
    tile_target_block,
    tile_block,
    tile_owner,
    cotangent,
):
    wide = lax.axis_size("wide")
    nh = lax.axis_size("hot")
    nz = wide // NX
    tiles = tile_values.shape[0]
    shape = (8, tiles, max(128, wide))
    what = jnp.where(
        lax.broadcasted_iota(jnp.int32, shape, 0) == 0,
        tile_block[None, :, None],
        lax.broadcasted_iota(jnp.int32, shape, 1),
    )
    owned = tile_owner[None, :, None] == lax.broadcasted_iota(jnp.int32, shape, 2)
    req = jnp.max(jnp.where(owned, what, -1), axis=1)
    return hand_over(
        layer(
            nz,
            nh,
            paper_features,
            cite_weight,
            self_weight,
            hot_embed,
            hot_ids.T,
            req,
            tile_values,
            cotangent,
            tile_rows,
            tile_target_block,
        )
    )


def solution(mesh):
    return jax.shard_map(
        on_device,
        mesh=mesh,
        in_specs=(
            P(("wide", "hot"), None),
            P(),
            P(),
            P("hot", None),
            P(("wide", "hot"), None),
            P(("wide", "hot"), None, None),
            P(("wide", "hot")),
            P(("wide", "hot")),
            P(("wide", "hot")),
            P(("wide", "hot")),
            P(("wide", "hot"), None),
        ),
        out_specs=(P(("wide", "hot"), None), P("wide", None), P("wide", None), P("hot", None)),
        check_vma=False,
    )
```

```python
import functools

import jax
import jax.numpy as jnp
from jax import lax
from jax.experimental import pallas as pl
from jax.experimental.pallas import tpu as pltpu
from jax.sharding import PartitionSpec as P

HK = 8
NX = 4
SUBS = 4
PAD = 16
MESH = pl.DeviceIdType.MESH
F32 = jnp.float32
BF16 = jnp.bfloat16
VMEM_LIMIT = 58 * 1024 * 1024


def place(nz):
    w = lax.axis_index("wide")
    h = lax.axis_index("hot")
    return w // NX, w % NX, w, h


def greet(partners):
    barrier = pltpu.get_barrier_semaphore()
    for partner in partners:
        pl.semaphore_signal(barrier, inc=1, device_id=partner, device_id_type=MESH)
    return lambda: pl.semaphore_wait(barrier, len(partners))


def remote(src, dst, send, recv, target):
    return pltpu.make_async_remote_copy(
        src_ref=src, dst_ref=dst, send_sem=send, recv_sem=recv, device_id=target, device_id_type=MESH
    )


class WeightSum:
    def __init__(self, where, nz, nh, refs):
        self.z, self.x, self.w, self.h = where
        self.nz, self.nh = nz, nh
        (self.mine, self.got1, self.mid, self.got2, self.last, self.got3, self.done) = refs[:7]
        (self.wide, self.s1, self.r1, self.s2, self.r2, self.s3, self.r3, self.s4, self.r4) = refs[7:16]
        self.share = self.mine.shape[1] // NX

    @staticmethod
    def scratch(nz, nh, share, width, kind):
        dma = pltpu.SemaphoreType.DMA
        two = nz // nh
        return [
            pltpu.VMEM((nz, NX * share, width), kind),
            pltpu.VMEM((nh - 1, two, NX * share, width), kind),
            pltpu.VMEM((NX, two, PAD, width), BF16),
            pltpu.VMEM((NX - 1, two, PAD, width), BF16),
            pltpu.VMEM((two, PAD, width), BF16),
            pltpu.VMEM((nz - 1, PAD, width), BF16),
            pltpu.VMEM((PAD, width), F32),
            pltpu.VMEM((NX, two, PAD, width), F32),
            dma((nh - 1, two)),
            dma((nh - 1, two)),
            dma((NX - 1,)),
            dma((NX - 1,)),
            dma((two,)),
            dma((nz - 1,)),
            dma((nh - 1,)),
            dma,
        ]

    def copies1(self):
        out = []
        for d in range(1, self.nh):
            peer = lax.rem(self.h + d, self.nh)
            for i in range(self.nz // self.nh):
                e = self.nh - d - 1
                out.append(
                    remote(
                        self.mine.at[peer + i * self.nh],
                        self.got1.at[e, i],
                        self.s1.at[d - 1, i],
                        self.r1.at[e, i],
                        (self.w, peer),
                    )
                )
        return out

    def copies2(self):
        out = []
        for d in range(1, NX):
            peer = lax.rem(self.x + d, NX)
            e = NX - d - 1
            out.append(
                remote(
                    self.mid.at[peer],
                    self.got2.at[e],
                    self.s2.at[d - 1],
                    self.r2.at[e],
                    (self.z * NX + peer, self.h),
                )
            )
        return out

    def each3(self, act):
        for i in range(self.nz // self.nh):
            there = self.h + i * self.nh
            off = lax.rem(self.z - there + self.nz, self.nz)

            @pl.when(off != 0)
            def _():
                act(
                    remote(
                        self.last.at[i],
                        self.got3.at[off - 1],
                        self.s3.at[i],
                        self.r3.at[off - 1],
                        (there * NX + self.x, self.h),
                    )
                )

    def copies4(self):
        return [
            remote(
                self.done, self.done, self.s4.at[d - 1], self.r4, (self.w, lax.rem(self.h + d, self.nh))
            )
            for d in range(1, self.nh)
        ]

    def stage1(self):
        for copy in self.copies1():
            copy.start()

    def stage2(self):
        self.wide[...] = jnp.zeros_like(self.wide)
        for copy in self.copies1():
            copy.wait_recv()
        for i in range(self.nz // self.nh):
            sums = self.mine[self.h + i * self.nh].astype(F32)
            for e in range(self.nh - 1):
                sums = sums + self.got1[e, i].astype(F32)
            for peer in range(NX):
                self.wide[peer, i, : self.share] = sums[peer * self.share : (peer + 1) * self.share]
        self.mid[...] = self.wide[...].astype(BF16)
        for copy in self.copies2():
            copy.start()

    def stage3(self):
        for copy in self.copies2():
            copy.wait_recv()
        sums = self.wide[self.x]
        for e in range(NX - 1):
            sums = sums + self.got2[e].astype(F32)
        self.wide[self.x] = sums
        self.last[...] = sums.astype(BF16)
        self.each3(lambda copy: copy.start())

    def stage4(self):
        @pl.when(lax.rem(self.z, self.nh) == self.h)
        def _():
            for o in range(self.nz - 1):
                remote(
                    self.last.at[0], self.got3.at[o], self.s3.at[0], self.r3.at[o], (self.w, self.h)
                ).wait_recv()
            sums = self.wide[self.x, self.z // self.nh]
            for o in range(self.nz - 1):
                sums = sums + self.got3[o].astype(F32)
            self.done[...] = sums
            for copy in self.copies4():
                copy.start()

    def finish(self, out):
        @pl.when(lax.rem(self.z, self.nh) != self.h)
        def _():
            self.copies4()[0].wait_recv()

        out[...] = self.done[: self.share]

    def drain(self):
        for copy in self.copies1() + self.copies2():
            copy.wait_send()
        self.each3(lambda copy: copy.wait_send())

        @pl.when(lax.rem(self.z, self.nh) == self.h)
        def _():
            for copy in self.copies4():
                copy.wait_send()


class AuthorSum:
    def __init__(self, where, nz, nh, refs):
        self.z, self.x, self.w, self.h = where
        self.nz, self.nh, self.np = nz, nh, nz // 2
        (self.mine, self.got1, self.mid, self.got2, self.cut, self.got3, self.sums4, self.rows5) = refs[:8]
        (self.s1, self.r1, self.s2, self.r2, self.s3, self.r3, self.s4, self.r4, self.s5, self.r5) = refs[8:18]

    @staticmethod
    def scratch(nz, nh, rows, width):
        dma = pltpu.SemaphoreType.DMA
        part = rows // NX
        pieces = nz // 2
        return [
            pltpu.VMEM((nh, rows, width), F32),
            pltpu.VMEM((nh - 1, rows, width), F32),
            pltpu.VMEM((NX, part, width), F32),
            pltpu.VMEM((NX - 1, part, width), F32),
            pltpu.VMEM((pieces, 8, width // 2), F32),
            pltpu.VMEM((nz - 1, 8, width // 2), F32),
            pltpu.VMEM((pieces, 8, width // 2), F32),
            pltpu.VMEM((NX, part, width), F32),
            dma((nh - 1,)),
            dma((nh - 1,)),
            dma((NX - 1,)),
            dma((NX - 1,)),
            dma((nz - 1,)),
            dma((nz - 1,)),
            dma((pieces - 1,)),
            dma((pieces - 1,)),
            dma((NX - 1,)),
            dma((NX - 1,)),
        ]

    def copies1(self):
        out = []
        for d in range(1, self.nh):
            peer = lax.rem(self.h + d, self.nh)
            e = self.nh - d - 1
            out.append(
                remote(self.mine.at[peer], self.got1.at[e], self.s1.at[d - 1], self.r1.at[e], (self.w, peer))
            )
        return out

    def copies2(self):
        out = []
        for d in range(1, NX):
            peer = lax.rem(self.x + d, NX)
            e = NX - d - 1
            to = (self.z * NX + peer, self.h)
            out.append(remote(self.mid.at[peer], self.got2.at[e], self.s2.at[d - 1], self.r2.at[e], to))
        return out

    def copies3(self):
        out = []
        for d in range(1, self.nz):
            peer = lax.rem(self.z + d, self.nz)
            e = self.nz - d - 1
            to = (peer * NX + self.x, self.h)
            out.append(
                remote(
                    self.cut.at[lax.rem(peer, self.np)], self.got3.at[e], self.s3.at[d - 1], self.r3.at[e], to
                )
            )
        return out

    def copies4(self, coming=False):
        out = []
        p = lax.rem(self.z, self.np)
        for d in range(1, self.np):
            other = lax.rem(p + d, self.np)
            to = ((self.z - p + other) * NX + self.x, self.h)
            e = d - 1 if coming else self.np - d - 1
            piece = self.sums4.at[other if coming else p]
            out.append(remote(piece, piece, self.s4.at[d - 1], self.r4.at[e], to))
        return out

    def copies5(self, coming=False):
        out = []
        for d in range(1, NX):
            peer = lax.rem(self.x + d, NX)
            e = d - 1 if coming else NX - d - 1
            rows = self.rows5.at[peer if coming else self.x]
            out.append(remote(rows, rows, self.s5.at[d - 1], self.r5.at[e], (self.z * NX + peer, self.h)))
        return out

    def stage1(self):
        for copy in self.copies1():
            copy.start()

    def stage2(self):
        for copy in self.copies1():
            copy.wait_recv()
        sums = self.mine[self.h]
        for e in range(self.nh - 1):
            sums = sums + self.got1[e]
        self.mid[...] = sums.reshape(self.mid.shape)
        for copy in self.copies2():
            copy.start()

    def stage3(self):
        for copy in self.copies2():
            copy.wait_recv()
        sums = self.mid[self.x]
        for e in range(NX - 1):
            sums = sums + self.got2[e]
        lanes = self.cut.shape[2]
        for p in range(self.np):
            g, c = p // 2, p % 2
            self.cut[p] = sums[g * 8 : (g + 1) * 8, c * lanes : (c + 1) * lanes]
        for copy in self.copies3():
            copy.start()

    def stage4(self):
        for copy in self.copies3():
            copy.wait_recv()
        p = lax.rem(self.z, self.np)
        sums = self.cut[p]
        for e in range(self.nz - 1):
            sums = sums + self.got3[e]
        self.sums4[p] = sums
        for copy in self.copies4():
            copy.start()

    def stage5(self):
        for copy in self.copies4(True):
            copy.wait_recv()
        lanes = self.cut.shape[2]
        for p in range(self.np):
            g, c = p // 2, p % 2
            self.rows5[self.x, g * 8 : (g + 1) * 8, c * lanes : (c + 1) * lanes] = self.sums4[p]
        for copy in self.copies5():
            copy.start()

    def finish(self, out):
        for copy in self.copies5(True):
            copy.wait_recv()
        out[...] = self.rows5[...].reshape(out.shape)

    def drain(self):
        for copy in self.copies1() + self.copies2() + self.copies3() + self.copies4() + self.copies5():
            copy.wait_send()


def layer_kernel(names, nz, nh, *refs):
    r = dict(zip(names, refs))
    half = nz // 2
    feat, w_cite, w_self, hot, ids, req, values, cotangent, used, target = refs[:10]
    hidden, self_out, cite_out, author_out = refs[10:14]
    own, packed, table, asks, asked, arrived = (
        r[n] for n in ("own", "packed", "table", "asks", "asked", "arrived")
    )
    spread, turned, counts, feat_t, base, total, grad, scaled = (
        r[n] for n in ("spread", "turned", "counts", "feat_t", "base", "total", "grad", "scaled")
    )
    degree, inverse = r["degree"], r["inverse"]
    where = place(nz)
    z, x, w, h = where
    selfs = WeightSum(where, nz, nh, [r["self%d" % i] for i in range(16)])
    cites = WeightSum(where, nz, nh, [r["cite%d" % i] for i in range(16)])
    authors = AuthorSum(where, nz, nh, [r["author%d" % i] for i in range(18)])
    blocks, size, width = own.shape
    hot_rows = hot.shape[0]
    hot_total = table.shape[0]
    per = blocks // SUBS
    to_right = (lax.rem(z + 1, nz) * NX + x, h)
    to_left = (lax.rem(z + nz - 1, nz) * NX + x, h)
    z_peers = [(lax.rem(z + d, nz) * NX + x, h) for d in range(1, nz)]
    x_peers = [(z * NX + lax.rem(x + d, NX), h) for d in range(1, NX)]
    h_peers = [(w, lax.rem(h + d, nh)) for d in range(1, nh)]
    wait_all = greet(z_peers + x_peers + h_peers)

    my_rows = pl.ds(pl.multiple_of(h * hot_rows, hot_rows), hot_rows)
    table[my_rows] = hot[...].astype(BF16)
    asks[0] = req[...]

    def spot(zoff):
        if zoff == 0:
            return 0
        return 2 * zoff if zoff < half else 2 * (nz - zoff) - 1

    def offsets(k):
        return [0] if k == 0 else [half] if k == half else [nz - k, k]

    last, few = half - 2, NX // 2
    f_right = [own] + [r["f_right%d" % k] for k in range(1, last + 1)]
    f_left = [own] + [r["f_left%d" % k] for k in range(1, last + 1)]
    rows_f32 = lax.broadcasted_iota(jnp.int32, (size, size), 0)
    far_devices = {"r": list(range(few)), "l": list(range(few, NX))}
    ahead = {"r": (0, 2), "l": (1, 3)}
    behind = {"r": (1, 3), "l": (0, 2)}
    side_to = {"r": to_right, "l": to_left}
    side_two = {
        "r": (lax.rem(z + 2, nz) * NX + x, h),
        "l": (lax.rem(z + nz - 2, nz) * NX + x, h),
    }

    def goes(side, k, s):
        return k <= last

    def f_ring(side, k, s):
        part = pl.ds(s * per, per)
        bufs, to = (f_right if side == "r" else f_left), side_to[side]
        return remote(
            bufs[k - 1].at[part],
            bufs[k].at[part],
            r["fs_" + side].at[k - 1, s],
            r["fr_" + side].at[k - 1, s],
            to,
        )

    def project(j, carry):
        many = blocks // 2
        rows = pl.ds(pl.multiple_of(j * many * size, many * size), many * size)
        value = jnp.dot(feat[rows], w_cite[...], preferred_element_type=F32).astype(BF16)
        for i in range(many):
            own[j * many + i] = value[i * size : (i + 1) * size]
        return carry

    lax.fori_loop(0, 2, project, 0)
    wait_all()
    for s in range(SUBS):
        for side in "rl":
            if goes(side, 1, s):
                f_ring(side, 1, s).start()

    def ask_copies(coming):
        return [
            remote(
                asks.at[0],
                asks.at[d if coming else NX - d],
                r["q_send"].at[d - 1],
                r["q_recv"].at[d - 1 if coming else NX - d - 1],
                x_peers[d - 1],
            )
            for d in range(1, NX)
        ]

    def hot_copies(coming):
        out = []
        for d in range(1, nh):
            peer = lax.rem(h + d, nh) if coming else h
            rows = table.at[pl.ds(pl.multiple_of(peer * hot_rows, hot_rows), hot_rows)]
            e = d - 1 if coming else nh - d - 1
            out.append(remote(rows, rows, r["h_send"].at[d - 1], r["h_recv"].at[e], h_peers[d - 1]))
        return out

    for copy in ask_copies(False) + hot_copies(False):
        copy.start()
    for copy in ask_copies(True):
        copy.wait_recv()
    local = pltpu.make_async_copy(asks, asked, r["q_local"])
    local.start()
    local.wait()

    def near_copies(coming):
        out = []
        for m, off in enumerate((1, -1, 2, -2)):
            to = (lax.rem(z - off + nz, nz) * NX + x, h)
            out.append(remote(asks, r["nears"].at[m], r["n_send"].at[m], r["n_recv"].at[m], to))
        return out

    for copy in near_copies(False):
        copy.start()
    nearby = r["nearby"]

    def near_arrive():
        for copy in near_copies(True):
            copy.wait_recv()
        copy = pltpu.make_async_copy(r["nears"], nearby, r["n_local"])
        copy.start()
        copy.wait()

    def f_hand(side, g):
        part = pl.ds(g * few, few)
        if g == 0:
            return remote(
                r["f_pack_" + side].at[part],
                r["f_far_" + side],
                r["fps_" + side],
                r["fpr_" + side],
                side_two[side],
            )
        return remote(
            r["f_pack_" + side].at[part],
            r["f_next_" + side].at[part],
            r["fhs_" + side].at[g],
            r["fhr_" + side].at[g],
            side_to[side],
        )

    def f_pick(side, source):
        owner = lax.rem(z + nz + (-last if side == "r" else last), nz) * NX + x
        first, second = ahead[side]
        pack = r["f_pack_" + side]
        for i, d in enumerate(far_devices[side]):
            pack[i] = source[jnp.maximum(nearby[second, d, 0, owner], 0)]
        for d in range(NX):
            pack[few + d] = source[jnp.maximum(nearby[first, d, 0, owner], 0)]

    def f_source(zoff, d):
        if zoff == half:
            side = "r" if d < few else "l"
            return r["f_far_" + side].at[d - (0 if d < few else few)]
        if zoff in (half - 1, half + 1):
            return r["f_next_" + ("r" if zoff == half + 1 else "l")].at[few + d]
        return packed.at[d - 1, zoff]

    def f_spread(zoff):
        for d in range(1, NX):
            f_copy(zoff, d, False).start()
        arrived[spot(zoff), 0] = f_source(zoff, 0)[...]

    def owner_at(zoff, d):
        return lax.rem(z + zoff, nz) * NX + lax.rem(x + d, NX)

    def f_copy(zoff, d, coming):
        return remote(
            f_source(zoff, d),
            arrived.at[spot(zoff), d if coming else NX - d],
            r["fx_send"].at[d - 1, zoff],
            r["fx_recv"].at[d - 1 if coming else NX - d - 1, zoff],
            x_peers[d - 1],
        )

    def f_exchange(zoff, source):
        owner = owner_at(zoff, 0)
        for d in range(1, NX):
            packed[d - 1, zoff] = source[jnp.maximum(asked[d, 0, owner], 0)]
        for d in range(1, NX):
            f_copy(zoff, d, False).start()
        arrived[spot(zoff), 0] = source[jnp.maximum(asked[0, 0, owner], 0)]

    def tile_of(zoff, d):
        t = asked[0, 1, owner_at(zoff, d)]
        number = jnp.maximum(t, 0)
        return values[number].astype(F32), jnp.where(t < 0, 0, used[number]), target[number]

    def lay_out(k, zoff, d):
        held = spread.at[k % 2]
        n = offsets(k).index(zoff) * NX + d
        m, live, block = tile_of(zoff, d)
        turned[spot(zoff), d] = jnp.where(rows_f32 < live, m, 0.0).T.astype(BF16)

        def lay(j, carry):
            there = jnp.where(block == j, live, 0)
            rows = pl.ds(pl.multiple_of(j * size, size), size)
            laid = jnp.where(rows_f32 < there, m, 0.0)
            held[rows, n * size : (n + 1) * size] = laid.astype(BF16)
            degree[rows] = laid if k == 0 and n == 0 else degree[rows] + laid
            return carry

        lax.fori_loop(0, blocks, lay, 0)

    def invert():
        def body(j, carry):
            rows = pl.ds(pl.multiple_of(j * size, size), size)
            sums = jnp.sum(degree[rows], axis=1, keepdims=True)
            inverse[rows] = jnp.broadcast_to(1.0 / jnp.maximum(sums, 1.0), (size, width))
            return carry

        lax.fori_loop(0, blocks, body, 0)

    def prepare(k):
        return [functools.partial(lay_out, k, zoff, d) for zoff in offsets(k) for d in range(NX)]

    def share_out(work, s):
        for item in work[s * len(work) // SUBS : (s + 1) * len(work) // SUBS]:
            item()

    def messages(k):
        for zoff in offsets(k):
            for d in range(1, NX):
                f_copy(zoff, d, True).wait_recv()
        first = spot(offsets(k)[0])
        count = len(offsets(k))
        span = count * NX * size

        step = blocks * size // 2

        def gather(j, carry):
            rows = pl.ds(pl.multiple_of(j * step, step), step)
            more = jnp.dot(
                spread[k % 2, rows, :span],
                arrived[first : first + count].reshape(span, width),
                preferred_element_type=F32,
            )
            total[rows] = more if k == 0 else total[rows] + more
            return carry

        lax.fori_loop(0, 2, gather, 0)

    def count(i):
        rows = pl.ds(i * size, size)

        def body(a, carry):
            there = pl.ds(pl.multiple_of(a * hot_rows, hot_rows), hot_rows)
            names = lax.broadcasted_iota(jnp.int32, (hot_rows, size), 0) + a * hot_rows
            many = jnp.zeros((hot_rows, size), F32)
            for k in range(HK):
                many = many + jnp.where(ids[k : k + 1, rows] == names, 1.0, 0.0)
            counts[there, rows] = many.astype(BF16)
            return carry

        lax.fori_loop(0, nh, body, 0)

    def start_rows(i):
        rows = pl.ds(i * size, size)
        mix = lax.dot_general(
            counts[:, rows], table[...], (((0,), (0,)), ((), ())), preferred_element_type=F32
        )
        base[rows] = jnp.dot(feat[rows], w_self[...], preferred_element_type=F32) + mix * (1.0 / HK)

    def turn(i):
        rows = pl.ds(i * size, size)
        feat_t[:, rows] = feat[rows].astype(F32).T.astype(BF16)

    def f_done(k):
        for side in "rl":
            if 1 <= k <= last:
                for s in range(SUBS):
                    f_ring(side, k, s).wait_send()
            elif k == last + 1:
                for g in range(3):
                    f_hand(side, g).wait_send()
        for zoff in offsets(k):
            for d in range(1, NX):
                f_copy(zoff, d, False).wait_send()

    f_exchange(0, own)
    for item in prepare(0) + prepare(1):
        item()
    for k in range(1, half + 1):
        work = []
        for i in range(blocks):
            if i * (half - 1) // blocks == k - 1:
                work += [functools.partial(part, i) for part in (turn, count, start_rows)]
        work.append(functools.partial(messages, k - 1))
        if k < half:
            work += prepare(k + 1)
        else:
            work.append(invert)
        if k >= 2:
            work.append(functools.partial(f_done, k - 2))
        if k == 1:
            for copy in hot_copies(True):
                copy.wait_recv()
        if k == last:
            work = [near_arrive] + work
        if k <= last:
            for s in range(SUBS):
                for side in "rl":
                    f_ring(side, k, s).wait_recv()
                    if goes(side, k + 1, s):
                        f_ring(side, k + 1, s).start()
                if s < SUBS - 1:
                    share_out(work, s)
            if k == last:
                for side, bufs in (("r", f_right), ("l", f_left)):
                    f_pick(side, bufs[last])
                    for g in range(3):
                        f_hand(side, g).start()
            f_exchange(nz - k, f_right[k])
            f_exchange(k, f_left[k])
            share_out(work, SUBS - 1)
        elif k == last + 1:
            for g in (1, 2):
                for side in "rl":
                    f_hand(side, g).wait_recv()
            f_spread(half + 1)
            f_spread(half - 1)
            for item in work:
                item()
        else:
            for side in "rl":
                f_hand(side, 0).wait_recv()
            f_spread(half)
            for item in work:
                item()
    messages(half)

    def finish(j, carry):
        rows = pl.ds(pl.multiple_of(j * size, size), size)
        inv = inverse[rows]
        pre = base[rows] + total[rows] * inv
        s = jax.nn.sigmoid(pre)
        hidden[rows] = (pre * s).astype(BF16)
        g = (cotangent[rows].astype(F32) * s * (1.0 + pre * (1.0 - s))).astype(BF16)
        grad[rows] = g
        scaled[j] = (g.astype(F32) * inv).astype(BF16)
        return carry

    lax.fori_loop(0, blocks, finish, 0)

    back, came, mine, near = (r[n] for n in ("back", "came", "mine", "near"))
    b_right = [r["b_right%d" % k] for k in range(last + 1)]
    b_left = [r["b_left%d" % k] for k in range(last + 1)]

    def b_copy(zoff, d, coming):
        return remote(
            back.at[d - 1, zoff],
            came.at[d - 1 if coming else NX - d - 1, zoff],
            r["bx_send"].at[d - 1, zoff],
            r["bx_recv"].at[d - 1 if coming else NX - d - 1, zoff],
            x_peers[d - 1],
        )

    def b_make(zoff):
        made = []
        for d in range(NX):
            block = target[jnp.maximum(asked[0, 1, owner_at(zoff, d)], 0)]
            made.append(jnp.dot(turned[spot(zoff), d], scaled[block], preferred_element_type=F32).astype(BF16))
        for d in range(1, NX):
            back[d - 1, zoff] = made[d]
        mine[zoff] = made[0]
        for d in range(1, NX):
            b_copy(zoff, d, False).start()

    def b_exchange(k):
        return [functools.partial(b_make, zoff) for zoff in offsets(k)]

    def b_done(k):
        for side in "rl":
            if 1 <= k <= last:
                for s in range(SUBS):
                    b_ring(side, k, s).wait_send()
            elif k == last + 1:
                for d in range(NX):
                    b_hand(side, d).wait_send()
            elif k == half:
                for i in range(few):
                    b_pass(side, i).wait_send()
        for zoff in offsets(k):
            for d in range(1, NX):
                b_copy(zoff, d, False).wait_send()

    def b_arrive(zoff):
        for d in range(1, NX):
            b_copy(zoff, d, True).wait_recv()

    step_rows = min(size, 64)

    def b_source(zoff, d):
        return mine.at[zoff] if d == 0 else came.at[d - 1, zoff]

    def b_pass(side, i):
        return remote(
            b_source(half, far_devices[side][i]),
            r["b_next_" + side].at[i],
            r["bps_" + side].at[i],
            r["bpr_" + side].at[i],
            side_two[side],
        )

    def b_hand(side, d):
        return remote(
            b_source(half - 1 if side == "r" else half + 1, d),
            r["b_next_" + side].at[few + d],
            r["bhs_" + side].at[d],
            r["bhr_" + side].at[d],
            side_to[side],
        )

    def loose(side):
        owner = owner_at(last if side == "r" else nz - last, 0)
        first, second = behind[side]
        held = r["b_next_" + side]
        out = [(nearby[second, d, 0, owner], held.at[i]) for i, d in enumerate(far_devices[side])]
        return out + [(nearby[first, d, 0, owner], held.at[few + d]) for d in range(NX)]

    def add_local(dst, sources, s, zoff, others=()):
        wanted = [asked[d, 0, owner_at(zoff, 0)] for d in range(NX)] + [place for place, _ in others]

        def body(i, carry):
            rows = pl.ds(pl.multiple_of(i * step_rows, step_rows), step_rows)
            terms = [mine[zoff, rows]] + [came[d - 1, zoff, rows] for d in range(1, NX)]
            terms += [block[rows] for _, block in others]
            for j in range(s * per, (s + 1) * per):
                sums = None
                for d in range(len(terms)):
                    term = jnp.where(wanted[d] == j, terms[d], jnp.zeros_like(terms[d]))
                    sums = term if sums is None else sums + term
                for source in sources:
                    sums = sums + source[j, rows]
                dst[j, rows] = sums
            return carry

        lax.fori_loop(0, size // step_rows, body, 0)

    def b_ring(side, k, s):
        part = pl.ds(s * per, per)
        bufs, to = (b_right if side == "r" else b_left), side_to[side]
        return remote(
            bufs[k].at[part], bufs[k - 1].at[part], r["bs_" + side].at[k - 1, s], r["br_" + side].at[k - 1, s], to
        )

    group = selfs.mine.shape[1]

    def weight_product(rhs, dest):
        many = nz // 2

        def body(i, carry):
            rows = pl.ds(pl.multiple_of(i * many * group, many * group), many * group)
            value = jnp.dot(feat_t[rows], rhs, preferred_element_type=F32)
            for q in range(many):
                dest.mine[i * many + q] = value[q * group : (q + 1) * group].astype(dest.mine.dtype)
            return carry

        lax.fori_loop(0, 2, body, 0)

    def self_start():
        weight_product(grad[...], selfs)
        selfs.stage1()

    def author_start():
        def body(i, carry):
            rows = pl.ds(pl.multiple_of(i * hot_total // 2, hot_total // 2), hot_total // 2)
            value = jnp.dot(counts[rows], grad[...], preferred_element_type=F32) * (1.0 / HK)
            for q in range(nh // 2):
                authors.mine[i * (nh // 2) + q] = value[q * hot_rows : (q + 1) * hot_rows]
            return carry

        lax.fori_loop(0, 2, body, 0)
        authors.stage1()

    extras = [
        [self_start],
        [author_start],
        [selfs.stage2],
        [authors.stage2],
        [selfs.stage3, authors.stage3],
        [selfs.stage4],
        [authors.stage4],
        [authors.stage5],
    ]
    for item in b_exchange(half) + b_exchange(half - 1):
        item()
    for k in range(half, 0, -1):
        work = b_exchange(k - 2) if k >= 2 else []
        for group_of in extras[(half - k) * 8 // half : (half - k + 1) * 8 // half]:
            work += group_of
        if k == half:
            work += [functools.partial(f_done, half - 1), functools.partial(f_done, half)]
        if k + 2 <= half:
            work.append(functools.partial(b_done, k + 2))
        for zoff in offsets(k):
            b_arrive(zoff)
        if k == half:
            for i in range(few):
                for side in "rl":
                    b_pass(side, i).start()
            for item in work:
                item()
        elif k == last + 1:
            for d in range(NX):
                for side in "rl":
                    b_hand(side, d).start()
            for item in work:
                item()
        else:
            if k == last:
                for side in "rl":
                    for d in range(NX):
                        b_hand(side, d).wait_recv()
                    for i in range(few):
                        b_pass(side, i).wait_recv()
            for s in range(SUBS):
                for side in "rl":
                    bufs = b_right if side == "r" else b_left
                    sources, others = [], ()
                    if k < last:
                        b_ring(side, k + 1, s).wait_recv()
                        sources = [bufs[k]]
                    else:
                        others = loose(side)
                    add_local(bufs[k], sources, s, k if side == "r" else nz - k, others)
                    b_ring(side, k, s).start()
                share_out(work, s)
    b_arrive(0)
    for s in range(SUBS):
        b_ring("r", 1, s).wait_recv()
        b_ring("l", 1, s).wait_recv()
        add_local(near, [b_right[0], b_left[0]], s, 0)
    weight_product(near[...].reshape(blocks * size, width), cites)
    cites.stage1()
    selfs.finish(self_out)
    authors.finish(author_out)
    for copy in ask_copies(False) + hot_copies(False) + near_copies(False):
        copy.wait_send()
    for k in (2, 1, 0):
        b_done(k)
    cites.stage2()
    selfs.drain()
    cites.stage3()
    authors.drain()
    cites.stage4()
    cites.finish(cite_out)
    cites.drain()


def layer(nz, nh, feat, w_cite, w_self, hot, ids, req, values, cotangent, used, target):
    half = nz // 2
    rows, din = feat.shape
    width = w_self.shape[1]
    size = values.shape[1]
    blocks = rows // size
    hot_total = hot.shape[0] * nh
    share = din // (nz * NX)
    vmem = pl.BlockSpec(memory_space=pltpu.VMEM)
    smem = pl.BlockSpec(memory_space=pltpu.SMEM)
    dma = pltpu.SemaphoreType.DMA
    chunk = pltpu.VMEM((blocks, size, width), BF16)
    column = pltpu.VMEM((NX - 1, nz, size, width), BF16)
    scratch = {
        "own": chunk,
        "packed": column,
        "table": pltpu.VMEM((hot_total, width), BF16),
        "asks": pltpu.VMEM((NX,) + req.shape, jnp.int32),
        "asked": pltpu.SMEM((NX,) + req.shape, jnp.int32),
        "arrived": pltpu.VMEM((nz, NX, size, width), BF16),
        "spread": pltpu.VMEM((2, rows, 2 * NX * size), BF16),
        "turned": pltpu.VMEM((nz, NX, size, size), BF16),
        "counts": pltpu.VMEM((hot_total, rows), BF16),
        "feat_t": pltpu.VMEM((din, rows), BF16),
        "base": pltpu.VMEM((rows, width), F32),
        "total": pltpu.VMEM((rows, width), F32),
        "degree": pltpu.VMEM((rows, size), F32),
        "inverse": pltpu.VMEM((rows, width), F32),
        "grad": pltpu.VMEM((rows, width), BF16),
        "scaled": chunk,
        "back": column,
        "came": column,
        "mine": pltpu.VMEM((nz, size, width), BF16),
        "near": chunk,
        "h_send": dma((nh - 1,)),
        "h_recv": dma((nh - 1,)),
        "q_send": dma((NX - 1,)),
        "q_recv": dma((NX - 1,)),
        "q_local": dma,
    }
    few = NX // 2
    several = pltpu.VMEM((NX + few, size, width), BF16)
    scratch["nears"] = pltpu.VMEM((4, NX) + req.shape, jnp.int32)
    scratch["nearby"] = pltpu.SMEM((4, NX) + req.shape, jnp.int32)
    scratch["n_send"] = dma((4,))
    scratch["n_recv"] = dma((4,))
    scratch["n_local"] = dma
    for side, word in (("r", "right"), ("l", "left")):
        for k in range(1, half - 1):
            scratch["f_%s%d" % (word, k)] = chunk
        for k in range(half - 1):
            scratch["b_%s%d" % (word, k)] = chunk
        for name in ("f_pack_", "f_next_", "b_next_"):
            scratch[name + side] = several
        scratch["f_far_" + side] = pltpu.VMEM((few, size, width), BF16)
        for name, count in (("fh", 3), ("bp", few), ("bh", NX)):
            scratch[name + "s_" + side] = dma((count,))
            scratch[name + "r_" + side] = dma((count,))
        scratch["fps_" + side] = dma
        scratch["fpr_" + side] = dma
    for name in ("fs_r", "fr_r", "fs_l", "fr_l", "bs_r", "br_r", "bs_l", "br_l"):
        scratch[name] = dma((half - 2, SUBS))
    for name in ("fx_send", "fx_recv", "bx_send", "bx_recv"):
        scratch[name] = dma((NX - 1, nz))
    for name, parts in (
        ("self", WeightSum.scratch(nz, nh, share, width, F32)),
        ("cite", WeightSum.scratch(nz, nh, share, width, BF16)),
        ("author", AuthorSum.scratch(nz, nh, hot.shape[0], width)),
    ):
        for i, part in enumerate(parts):
            scratch[name + str(i)] = part
    names = ["in%d" % i for i in range(10)] + ["out%d" % i for i in range(4)] + list(scratch)
    return pl.pallas_call(
        functools.partial(layer_kernel, names, nz, nh),
        out_shape=(
            jax.ShapeDtypeStruct((rows, width), BF16),
            jax.ShapeDtypeStruct((share, width), F32),
            jax.ShapeDtypeStruct((share, width), F32),
            jax.ShapeDtypeStruct(hot.shape, F32),
        ),
        in_specs=[vmem] * 8 + [smem] * 2,
        out_specs=(vmem,) * 4,
        scratch_shapes=list(scratch.values()),
        compiler_params=pltpu.CompilerParams(
            collective_id=1, has_side_effects=True, vmem_limit_bytes=VMEM_LIMIT
        ),
    )(feat, w_cite, w_self, hot, ids, req, values, cotangent, used, target)


def hand_over_kernel(*refs):
    half = len(refs) // 2
    for src, dst in zip(refs[:half], refs[half:]):
        dst[...] = src[...]


def hand_over(arrays):
    vmem = pl.BlockSpec(memory_space=pltpu.VMEM)
    return pl.pallas_call(
        hand_over_kernel,
        out_shape=tuple(jax.ShapeDtypeStruct(a.shape, a.dtype) for a in arrays),
        in_specs=[vmem] * len(arrays),
        out_specs=(vmem,) * len(arrays),
    )(*arrays)


def on_device(
    paper_features,
    self_weight,
    cite_weight,
    hot_embed,
    hot_ids,
    tile_values,
    tile_rows,
    tile_target_block,
    tile_block,
    tile_owner,
    cotangent,
):
    wide = lax.axis_size("wide")
    nh = lax.axis_size("hot")
    nz = wide // NX
    tiles = tile_values.shape[0]
    shape = (8, tiles, max(128, wide))
    what = jnp.where(
        lax.broadcasted_iota(jnp.int32, shape, 0) == 0,
        tile_block[None, :, None],
        lax.broadcasted_iota(jnp.int32, shape, 1),
    )
    owned = tile_owner[None, :, None] == lax.broadcasted_iota(jnp.int32, shape, 2)
    req = jnp.max(jnp.where(owned, what, -1), axis=1)
    return hand_over(
        layer(
            nz,
            nh,
            paper_features,
            cite_weight,
            self_weight,
            hot_embed,
            hot_ids.T,
            req,
            tile_values,
            cotangent,
            tile_rows,
            tile_target_block,
        )
    )


def solution(mesh):
    return jax.shard_map(
        on_device,
        mesh=mesh,
        in_specs=(
            P(("wide", "hot"), None),
            P(),
            P(),
            P("hot", None),
            P(("wide", "hot"), None),
            P(("wide", "hot"), None, None),
            P(("wide", "hot")),
            P(("wide", "hot")),
            P(("wide", "hot")),
            P(("wide", "hot")),
            P(("wide", "hot"), None),
        ),
        out_specs=(P(("wide", "hot"), None), P("wide", None), P("wide", None), P("hot", None)),
        check_vma=False,
    )
```

```python
import functools

import jax
import jax.numpy as jnp
from jax import lax
from jax.experimental import pallas as pl
from jax.experimental.pallas import tpu as pltpu
from jax.sharding import PartitionSpec as P

HK = 8
NX = 4
SUBS = 4
PAD = 16
MESH = pl.DeviceIdType.MESH
F32 = jnp.float32
BF16 = jnp.bfloat16
VMEM_LIMIT = 58 * 1024 * 1024


def place(nz):
    w = lax.axis_index("wide")
    h = lax.axis_index("hot")
    return w // NX, w % NX, w, h


def greet(partners):
    barrier = pltpu.get_barrier_semaphore()
    for partner in partners:
        pl.semaphore_signal(barrier, inc=1, device_id=partner, device_id_type=MESH)
    return lambda: pl.semaphore_wait(barrier, len(partners))


def remote(src, dst, send, recv, target):
    return pltpu.make_async_remote_copy(
        src_ref=src, dst_ref=dst, send_sem=send, recv_sem=recv, device_id=target, device_id_type=MESH
    )


class WeightSum:
    def __init__(self, where, nz, nh, refs):
        self.z, self.x, self.w, self.h = where
        self.nz, self.nh = nz, nh
        (self.mine, self.got1, self.mid, self.got2, self.last, self.got3, self.done) = refs[:7]
        (self.wide, self.s1, self.r1, self.s2, self.r2, self.s3, self.r3, self.s4, self.r4) = refs[7:16]
        self.share = self.mine.shape[1] // NX

    @staticmethod
    def scratch(nz, nh, share, width, kind):
        dma = pltpu.SemaphoreType.DMA
        two = nz // nh
        return [
            pltpu.VMEM((nz, NX * share, width), kind),
            pltpu.VMEM((nh - 1, two, NX * share, width), kind),
            pltpu.VMEM((NX, two, PAD, width), BF16),
            pltpu.VMEM((NX - 1, two, PAD, width), BF16),
            pltpu.VMEM((two, PAD, width), BF16),
            pltpu.VMEM((nz - 1, PAD, width), BF16),
            pltpu.VMEM((PAD, width), F32),
            pltpu.VMEM((NX, two, PAD, width), F32),
            dma((nh - 1, two)),
            dma((nh - 1, two)),
            dma((NX - 1,)),
            dma((NX - 1,)),
            dma((two,)),
            dma((nz - 1,)),
            dma((nh - 1,)),
            dma,
        ]

    def copies1(self):
        out = []
        for d in range(1, self.nh):
            peer = lax.rem(self.h + d, self.nh)
            for i in range(self.nz // self.nh):
                e = self.nh - d - 1
                out.append(
                    remote(
                        self.mine.at[peer + i * self.nh],
                        self.got1.at[e, i],
                        self.s1.at[d - 1, i],
                        self.r1.at[e, i],
                        (self.w, peer),
                    )
                )
        return out

    def copies2(self):
        out = []
        for d in range(1, NX):
            peer = lax.rem(self.x + d, NX)
            e = NX - d - 1
            out.append(
                remote(
                    self.mid.at[peer],
                    self.got2.at[e],
                    self.s2.at[d - 1],
                    self.r2.at[e],
                    (self.z * NX + peer, self.h),
                )
            )
        return out

    def each3(self, act):
        for i in range(self.nz // self.nh):
            there = self.h + i * self.nh
            off = lax.rem(self.z - there + self.nz, self.nz)

            @pl.when(off != 0)
            def _():
                act(
                    remote(
                        self.last.at[i],
                        self.got3.at[off - 1],
                        self.s3.at[i],
                        self.r3.at[off - 1],
                        (there * NX + self.x, self.h),
                    )
                )

    def copies4(self):
        return [
            remote(
                self.done, self.done, self.s4.at[d - 1], self.r4, (self.w, lax.rem(self.h + d, self.nh))
            )
            for d in range(1, self.nh)
        ]

    def stage1(self):
        for copy in self.copies1():
            copy.start()

    def stage2(self):
        self.wide[...] = jnp.zeros_like(self.wide)
        for copy in self.copies1():
            copy.wait_recv()
        for i in range(self.nz // self.nh):
            sums = self.mine[self.h + i * self.nh].astype(F32)
            for e in range(self.nh - 1):
                sums = sums + self.got1[e, i].astype(F32)
            for peer in range(NX):
                self.wide[peer, i, : self.share] = sums[peer * self.share : (peer + 1) * self.share]
        self.mid[...] = self.wide[...].astype(BF16)
        for copy in self.copies2():
            copy.start()

    def stage3(self):
        for copy in self.copies2():
            copy.wait_recv()
        sums = self.wide[self.x]
        for e in range(NX - 1):
            sums = sums + self.got2[e].astype(F32)
        self.wide[self.x] = sums
        self.last[...] = sums.astype(BF16)
        self.each3(lambda copy: copy.start())

    def stage4(self):
        @pl.when(lax.rem(self.z, self.nh) == self.h)
        def _():
            for o in range(self.nz - 1):
                remote(
                    self.last.at[0], self.got3.at[o], self.s3.at[0], self.r3.at[o], (self.w, self.h)
                ).wait_recv()
            sums = self.wide[self.x, self.z // self.nh]
            for o in range(self.nz - 1):
                sums = sums + self.got3[o].astype(F32)
            self.done[...] = sums
            for copy in self.copies4():
                copy.start()

    def finish(self, out):
        @pl.when(lax.rem(self.z, self.nh) != self.h)
        def _():
            self.copies4()[0].wait_recv()

        out[...] = self.done[: self.share]

    def drain(self):
        for copy in self.copies1() + self.copies2():
            copy.wait_send()
        self.each3(lambda copy: copy.wait_send())

        @pl.when(lax.rem(self.z, self.nh) == self.h)
        def _():
            for copy in self.copies4():
                copy.wait_send()


class AuthorSum:
    def __init__(self, where, nz, nh, refs):
        self.z, self.x, self.w, self.h = where
        self.nz, self.nh, self.np = nz, nh, nz // 2
        (self.mine, self.got1, self.mid, self.got2, self.cut, self.got3, self.sums4, self.rows5) = refs[:8]
        (self.s1, self.r1, self.s2, self.r2, self.s3, self.r3, self.s4, self.r4, self.s5, self.r5) = refs[8:18]

    @staticmethod
    def scratch(nz, nh, rows, width):
        dma = pltpu.SemaphoreType.DMA
        part = rows // NX
        pieces = nz // 2
        return [
            pltpu.VMEM((nh, rows, width), F32),
            pltpu.VMEM((nh - 1, rows, width), F32),
            pltpu.VMEM((NX, part, width), F32),
            pltpu.VMEM((NX - 1, part, width), F32),
            pltpu.VMEM((pieces, 8, width // 2), F32),
            pltpu.VMEM((nz - 1, 8, width // 2), F32),
            pltpu.VMEM((pieces, 8, width // 2), F32),
            pltpu.VMEM((NX, part, width), F32),
            dma((nh - 1,)),
            dma((nh - 1,)),
            dma((NX - 1,)),
            dma((NX - 1,)),
            dma((nz - 1,)),
            dma((nz - 1,)),
            dma((pieces - 1,)),
            dma((pieces - 1,)),
            dma((NX - 1,)),
            dma((NX - 1,)),
        ]

    def copies1(self):
        out = []
        for d in range(1, self.nh):
            peer = lax.rem(self.h + d, self.nh)
            e = self.nh - d - 1
            out.append(
                remote(self.mine.at[peer], self.got1.at[e], self.s1.at[d - 1], self.r1.at[e], (self.w, peer))
            )
        return out

    def copies2(self):
        out = []
        for d in range(1, NX):
            peer = lax.rem(self.x + d, NX)
            e = NX - d - 1
            to = (self.z * NX + peer, self.h)
            out.append(remote(self.mid.at[peer], self.got2.at[e], self.s2.at[d - 1], self.r2.at[e], to))
        return out

    def copies3(self):
        out = []
        for d in range(1, self.nz):
            peer = lax.rem(self.z + d, self.nz)
            e = self.nz - d - 1
            to = (peer * NX + self.x, self.h)
            out.append(
                remote(
                    self.cut.at[lax.rem(peer, self.np)], self.got3.at[e], self.s3.at[d - 1], self.r3.at[e], to
                )
            )
        return out

    def copies4(self, coming=False):
        out = []
        p = lax.rem(self.z, self.np)
        for d in range(1, self.np):
            other = lax.rem(p + d, self.np)
            to = ((self.z - p + other) * NX + self.x, self.h)
            e = d - 1 if coming else self.np - d - 1
            piece = self.sums4.at[other if coming else p]
            out.append(remote(piece, piece, self.s4.at[d - 1], self.r4.at[e], to))
        return out

    def copies5(self, coming=False):
        out = []
        for d in range(1, NX):
            peer = lax.rem(self.x + d, NX)
            e = d - 1 if coming else NX - d - 1
            rows = self.rows5.at[peer if coming else self.x]
            out.append(remote(rows, rows, self.s5.at[d - 1], self.r5.at[e], (self.z * NX + peer, self.h)))
        return out

    def stage1(self):
        for copy in self.copies1():
            copy.start()

    def stage2(self):
        for copy in self.copies1():
            copy.wait_recv()
        sums = self.mine[self.h]
        for e in range(self.nh - 1):
            sums = sums + self.got1[e]
        self.mid[...] = sums.reshape(self.mid.shape)
        for copy in self.copies2():
            copy.start()

    def stage3(self):
        for copy in self.copies2():
            copy.wait_recv()
        sums = self.mid[self.x]
        for e in range(NX - 1):
            sums = sums + self.got2[e]
        lanes = self.cut.shape[2]
        for p in range(self.np):
            g, c = p // 2, p % 2
            self.cut[p] = sums[g * 8 : (g + 1) * 8, c * lanes : (c + 1) * lanes]
        for copy in self.copies3():
            copy.start()

    def stage4(self):
        for copy in self.copies3():
            copy.wait_recv()
        p = lax.rem(self.z, self.np)
        sums = self.cut[p]
        for e in range(self.nz - 1):
            sums = sums + self.got3[e]
        self.sums4[p] = sums
        for copy in self.copies4():
            copy.start()

    def stage5(self):
        for copy in self.copies4(True):
            copy.wait_recv()
        lanes = self.cut.shape[2]
        for p in range(self.np):
            g, c = p // 2, p % 2
            self.rows5[self.x, g * 8 : (g + 1) * 8, c * lanes : (c + 1) * lanes] = self.sums4[p]
        for copy in self.copies5():
            copy.start()

    def finish(self, out):
        for copy in self.copies5(True):
            copy.wait_recv()
        out[...] = self.rows5[...].reshape(out.shape)

    def drain(self):
        for copy in self.copies1() + self.copies2() + self.copies3() + self.copies4() + self.copies5():
            copy.wait_send()


def layer_kernel(names, nz, nh, *refs):
    r = dict(zip(names, refs))
    half = nz // 2
    feat, w_cite, w_self, hot, ids, req, values, cotangent, used, target = refs[:10]
    hidden, self_out, cite_out, author_out = refs[10:14]
    own, packed, table, asks, asked, arrived = (
        r[n] for n in ("own", "packed", "table", "asks", "asked", "arrived")
    )
    spread, turned, counts, feat_t, base, total, grad, scaled = (
        r[n] for n in ("spread", "turned", "counts", "feat_t", "base", "total", "grad", "scaled")
    )
    degree, inverse = r["degree"], r["inverse"]
    where = place(nz)
    z, x, w, h = where
    selfs = WeightSum(where, nz, nh, [r["self%d" % i] for i in range(16)])
    cites = WeightSum(where, nz, nh, [r["cite%d" % i] for i in range(16)])
    authors = AuthorSum(where, nz, nh, [r["author%d" % i] for i in range(18)])
    blocks, size, width = own.shape
    hot_rows = hot.shape[0]
    hot_total = table.shape[0]
    per = blocks // SUBS
    to_right = (lax.rem(z + 1, nz) * NX + x, h)
    to_left = (lax.rem(z + nz - 1, nz) * NX + x, h)
    z_peers = [(lax.rem(z + d, nz) * NX + x, h) for d in range(1, nz)]
    x_peers = [(z * NX + lax.rem(x + d, NX), h) for d in range(1, NX)]
    h_peers = [(w, lax.rem(h + d, nh)) for d in range(1, nh)]
    wait_all = greet(z_peers + x_peers + h_peers)

    my_rows = pl.ds(pl.multiple_of(h * hot_rows, hot_rows), hot_rows)
    table[my_rows] = hot[...].astype(BF16)
    asks[0] = req[...]

    def spot(zoff):
        if zoff == 0:
            return 0
        return 2 * zoff if zoff < half else 2 * (nz - zoff) - 1

    def offsets(k):
        return [0] if k == 0 else [half] if k == half else [nz - k, k]

    last, few = half - 2, NX // 2
    f_right = [own] + [r["f_right%d" % k] for k in range(1, last + 1)]
    f_left = [own] + [r["f_left%d" % k] for k in range(1, last + 1)]
    rows_f32 = lax.broadcasted_iota(jnp.int32, (size, size), 0)
    far_devices = {"r": list(range(few)), "l": list(range(few, NX))}
    ahead = {"r": (0, 2), "l": (1, 3)}
    behind = {"r": (1, 3), "l": (0, 2)}
    side_to = {"r": to_right, "l": to_left}

    def goes(side, k, s):
        return k <= last

    def f_ring(side, k, s):
        part = pl.ds(s * per, per)
        bufs, to = (f_right if side == "r" else f_left), side_to[side]
        return remote(
            bufs[k - 1].at[part],
            bufs[k].at[part],
            r["fs_" + side].at[k - 1, s],
            r["fr_" + side].at[k - 1, s],
            to,
        )

    def project(j, carry):
        many = blocks // 2
        rows = pl.ds(pl.multiple_of(j * many * size, many * size), many * size)
        value = jnp.dot(feat[rows], w_cite[...], preferred_element_type=F32).astype(BF16)
        for i in range(many):
            own[j * many + i] = value[i * size : (i + 1) * size]
        return carry

    lax.fori_loop(0, 2, project, 0)
    wait_all()
    for s in range(SUBS):
        for side in "rl":
            if goes(side, 1, s):
                f_ring(side, 1, s).start()

    def ask_copies(coming):
        return [
            remote(
                asks.at[0],
                asks.at[d if coming else NX - d],
                r["q_send"].at[d - 1],
                r["q_recv"].at[d - 1 if coming else NX - d - 1],
                x_peers[d - 1],
            )
            for d in range(1, NX)
        ]

    def hot_copies(coming):
        out = []
        for d in range(1, nh):
            peer = lax.rem(h + d, nh) if coming else h
            rows = table.at[pl.ds(pl.multiple_of(peer * hot_rows, hot_rows), hot_rows)]
            e = d - 1 if coming else nh - d - 1
            out.append(remote(rows, rows, r["h_send"].at[d - 1], r["h_recv"].at[e], h_peers[d - 1]))
        return out

    for copy in ask_copies(False) + hot_copies(False):
        copy.start()
    for copy in ask_copies(True):
        copy.wait_recv()
    local = pltpu.make_async_copy(asks, asked, r["q_local"])
    local.start()
    local.wait()

    def near_copies(coming):
        out = []
        for m, off in enumerate((1, -1, 2, -2)):
            to = (lax.rem(z - off + nz, nz) * NX + x, h)
            out.append(remote(asks, r["nears"].at[m], r["n_send"].at[m], r["n_recv"].at[m], to))
        return out

    for copy in near_copies(False):
        copy.start()
    nearby = r["nearby"]

    def near_arrive():
        for copy in near_copies(True):
            copy.wait_recv()
        copy = pltpu.make_async_copy(r["nears"], nearby, r["n_local"])
        copy.start()
        copy.wait()

    def f_hand(side, g):
        part = pl.ds(g * few, few)
        return remote(
            r["f_pack_" + side].at[part],
            r["f_next_" + side].at[part],
            r["fhs_" + side].at[g],
            r["fhr_" + side].at[g],
            side_to[side],
        )

    def f_pass(side):
        return remote(
            r["f_next_" + side].at[pl.ds(0, few)],
            r["f_far_" + side],
            r["fps_" + side],
            r["fpr_" + side],
            side_to[side],
        )

    def f_pick(side, source):
        owner = lax.rem(z + nz + (-last if side == "r" else last), nz) * NX + x
        first, second = ahead[side]
        pack = r["f_pack_" + side]
        for i, d in enumerate(far_devices[side]):
            pack[i] = source[jnp.maximum(nearby[second, d, 0, owner], 0)]
        for d in range(NX):
            pack[few + d] = source[jnp.maximum(nearby[first, d, 0, owner], 0)]

    def f_source(zoff, d):
        if zoff == half:
            side = "r" if d < few else "l"
            return r["f_far_" + side].at[d - (0 if d < few else few)]
        if zoff in (half - 1, half + 1):
            return r["f_next_" + ("r" if zoff == half + 1 else "l")].at[few + d]
        return packed.at[d - 1, zoff]

    def f_spread(zoff):
        for d in range(1, NX):
            f_copy(zoff, d, False).start()
        arrived[spot(zoff), 0] = f_source(zoff, 0)[...]

    def owner_at(zoff, d):
        return lax.rem(z + zoff, nz) * NX + lax.rem(x + d, NX)

    def f_copy(zoff, d, coming):
        return remote(
            f_source(zoff, d),
            arrived.at[spot(zoff), d if coming else NX - d],
            r["fx_send"].at[d - 1, zoff],
            r["fx_recv"].at[d - 1 if coming else NX - d - 1, zoff],
            x_peers[d - 1],
        )

    def f_exchange(zoff, source):
        owner = owner_at(zoff, 0)
        for d in range(1, NX):
            packed[d - 1, zoff] = source[jnp.maximum(asked[d, 0, owner], 0)]
        for d in range(1, NX):
            f_copy(zoff, d, False).start()
        arrived[spot(zoff), 0] = source[jnp.maximum(asked[0, 0, owner], 0)]

    def tile_of(zoff, d):
        t = asked[0, 1, owner_at(zoff, d)]
        number = jnp.maximum(t, 0)
        return values[number].astype(F32), jnp.where(t < 0, 0, used[number]), target[number]

    def lay_out(k, zoff, d):
        held = spread.at[k % 2]
        n = offsets(k).index(zoff) * NX + d
        m, live, block = tile_of(zoff, d)
        turned[spot(zoff), d] = jnp.where(rows_f32 < live, m, 0.0).T.astype(BF16)

        def lay(j, carry):
            there = jnp.where(block == j, live, 0)
            rows = pl.ds(pl.multiple_of(j * size, size), size)
            laid = jnp.where(rows_f32 < there, m, 0.0)
            held[rows, n * size : (n + 1) * size] = laid.astype(BF16)
            degree[rows] = laid if k == 0 and n == 0 else degree[rows] + laid
            return carry

        lax.fori_loop(0, blocks, lay, 0)

    def invert():
        def body(j, carry):
            rows = pl.ds(pl.multiple_of(j * size, size), size)
            sums = jnp.sum(degree[rows], axis=1, keepdims=True)
            inverse[rows] = jnp.broadcast_to(1.0 / jnp.maximum(sums, 1.0), (size, width))
            return carry

        lax.fori_loop(0, blocks, body, 0)

    def prepare(k):
        return [functools.partial(lay_out, k, zoff, d) for zoff in offsets(k) for d in range(NX)]

    def share_out(work, s):
        for item in work[s * len(work) // SUBS : (s + 1) * len(work) // SUBS]:
            item()

    def messages(k):
        for zoff in offsets(k):
            for d in range(1, NX):
                f_copy(zoff, d, True).wait_recv()
        first = spot(offsets(k)[0])
        count = len(offsets(k))
        span = count * NX * size

        step = blocks * size // 2

        def gather(j, carry):
            rows = pl.ds(pl.multiple_of(j * step, step), step)
            more = jnp.dot(
                spread[k % 2, rows, :span],
                arrived[first : first + count].reshape(span, width),
                preferred_element_type=F32,
            )
            total[rows] = more if k == 0 else total[rows] + more
            return carry

        lax.fori_loop(0, 2, gather, 0)

    def count(i):
        rows = pl.ds(i * size, size)

        def body(a, carry):
            there = pl.ds(pl.multiple_of(a * hot_rows, hot_rows), hot_rows)
            names = lax.broadcasted_iota(jnp.int32, (hot_rows, size), 0) + a * hot_rows
            many = jnp.zeros((hot_rows, size), F32)
            for k in range(HK):
                many = many + jnp.where(ids[k : k + 1, rows] == names, 1.0, 0.0)
            counts[there, rows] = many.astype(BF16)
            return carry

        lax.fori_loop(0, nh, body, 0)

    def start_rows(i):
        rows = pl.ds(i * size, size)
        mix = lax.dot_general(
            counts[:, rows], table[...], (((0,), (0,)), ((), ())), preferred_element_type=F32
        )
        base[rows] = jnp.dot(feat[rows], w_self[...], preferred_element_type=F32) + mix * (1.0 / HK)

    def turn(i):
        rows = pl.ds(i * size, size)
        feat_t[:, rows] = feat[rows].astype(F32).T.astype(BF16)

    def f_done(k):
        for side in "rl":
            if 1 <= k <= last:
                for s in range(SUBS):
                    f_ring(side, k, s).wait_send()
            elif k == last + 1:
                for g in range(3):
                    f_hand(side, g).wait_send()
            elif k == half:
                f_pass(side).wait_send()
        for zoff in offsets(k):
            for d in range(1, NX):
                f_copy(zoff, d, False).wait_send()

    f_exchange(0, own)
    for item in prepare(0) + prepare(1):
        item()
    for k in range(1, half + 1):
        work = []
        for i in range(blocks):
            if i * (half - 1) // blocks == k - 1:
                work += [functools.partial(part, i) for part in (turn, count, start_rows)]
        work.append(functools.partial(messages, k - 1))
        if k < half:
            work += prepare(k + 1)
        else:
            work.append(invert)
        if k >= 2:
            work.append(functools.partial(f_done, k - 2))
        if k == 1:
            for copy in hot_copies(True):
                copy.wait_recv()
        if k == last:
            work = [near_arrive] + work
        if k <= last:
            for s in range(SUBS):
                for side in "rl":
                    f_ring(side, k, s).wait_recv()
                    if goes(side, k + 1, s):
                        f_ring(side, k + 1, s).start()
                if s < SUBS - 1:
                    share_out(work, s)
            if k == last:
                for side, bufs in (("r", f_right), ("l", f_left)):
                    f_pick(side, bufs[last])
                    for g in range(3):
                        f_hand(side, g).start()
            f_exchange(nz - k, f_right[k])
            f_exchange(k, f_left[k])
            share_out(work, SUBS - 1)
        elif k == last + 1:
            for side in "rl":
                f_hand(side, 0).wait_recv()
                f_pass(side).start()
            for g in (1, 2):
                for side in "rl":
                    f_hand(side, g).wait_recv()
            f_spread(half + 1)
            f_spread(half - 1)
            for item in work:
                item()
        else:
            for side in "rl":
                f_pass(side).wait_recv()
            f_spread(half)
            for item in work:
                item()
    messages(half)

    def finish(j, carry):
        rows = pl.ds(pl.multiple_of(j * size, size), size)
        inv = inverse[rows]
        pre = base[rows] + total[rows] * inv
        s = jax.nn.sigmoid(pre)
        hidden[rows] = (pre * s).astype(BF16)
        g = (cotangent[rows].astype(F32) * s * (1.0 + pre * (1.0 - s))).astype(BF16)
        grad[rows] = g
        scaled[j] = (g.astype(F32) * inv).astype(BF16)
        return carry

    lax.fori_loop(0, blocks, finish, 0)

    back, came, mine, near = (r[n] for n in ("back", "came", "mine", "near"))
    b_right = [r["b_right%d" % k] for k in range(last + 1)]
    b_left = [r["b_left%d" % k] for k in range(last + 1)]

    def b_copy(zoff, d, coming):
        return remote(
            back.at[d - 1, zoff],
            came.at[d - 1 if coming else NX - d - 1, zoff],
            r["bx_send"].at[d - 1, zoff],
            r["bx_recv"].at[d - 1 if coming else NX - d - 1, zoff],
            x_peers[d - 1],
        )

    def b_make(zoff):
        made = []
        for d in range(NX):
            block = target[jnp.maximum(asked[0, 1, owner_at(zoff, d)], 0)]
            made.append(jnp.dot(turned[spot(zoff), d], scaled[block], preferred_element_type=F32).astype(BF16))
        for d in range(1, NX):
            back[d - 1, zoff] = made[d]
        mine[zoff] = made[0]
        for d in range(1, NX):
            b_copy(zoff, d, False).start()

    def b_exchange(k):
        return [functools.partial(b_make, zoff) for zoff in offsets(k)]

    def b_done(k):
        for side in "rl":
            if 1 <= k <= last:
                for s in range(SUBS):
                    b_ring(side, k, s).wait_send()
            elif k == last + 1:
                b_onward(side).wait_send()
                for d in range(NX):
                    b_hand(side, d).wait_send()
            elif k == half:
                for i in range(few):
                    b_pass(side, i).wait_send()
        for zoff in offsets(k):
            for d in range(1, NX):
                b_copy(zoff, d, False).wait_send()

    def b_arrive(zoff):
        for d in range(1, NX):
            b_copy(zoff, d, True).wait_recv()

    step_rows = min(size, 64)

    def b_source(zoff, d):
        return mine.at[zoff] if d == 0 else came.at[d - 1, zoff]

    def b_pass(side, i):
        return remote(
            b_source(half, far_devices[side][i]),
            r["b_far_" + side].at[i],
            r["bps_" + side].at[i],
            r["bpr_" + side].at[i],
            side_to[side],
        )

    def b_onward(side):
        return remote(
            r["b_far_" + side],
            r["b_next_" + side].at[pl.ds(0, few)],
            r["bos_" + side],
            r["bor_" + side],
            side_to[side],
        )

    def b_hand(side, d):
        return remote(
            b_source(half - 1 if side == "r" else half + 1, d),
            r["b_next_" + side].at[few + d],
            r["bhs_" + side].at[d],
            r["bhr_" + side].at[d],
            side_to[side],
        )

    def loose(side):
        owner = owner_at(last if side == "r" else nz - last, 0)
        first, second = behind[side]
        held = r["b_next_" + side]
        out = [(nearby[second, d, 0, owner], held.at[i]) for i, d in enumerate(far_devices[side])]
        return out + [(nearby[first, d, 0, owner], held.at[few + d]) for d in range(NX)]

    def add_local(dst, sources, s, zoff, others=()):
        wanted = [asked[d, 0, owner_at(zoff, 0)] for d in range(NX)] + [place for place, _ in others]

        def body(i, carry):
            rows = pl.ds(pl.multiple_of(i * step_rows, step_rows), step_rows)
            terms = [mine[zoff, rows]] + [came[d - 1, zoff, rows] for d in range(1, NX)]
            terms += [block[rows] for _, block in others]
            for j in range(s * per, (s + 1) * per):
                sums = None
                for d in range(len(terms)):
                    term = jnp.where(wanted[d] == j, terms[d], jnp.zeros_like(terms[d]))
                    sums = term if sums is None else sums + term
                for source in sources:
                    sums = sums + source[j, rows]
                dst[j, rows] = sums
            return carry

        lax.fori_loop(0, size // step_rows, body, 0)

    def b_ring(side, k, s):
        part = pl.ds(s * per, per)
        bufs, to = (b_right if side == "r" else b_left), side_to[side]
        return remote(
            bufs[k].at[part], bufs[k - 1].at[part], r["bs_" + side].at[k - 1, s], r["br_" + side].at[k - 1, s], to
        )

    group = selfs.mine.shape[1]

    def weight_product(rhs, dest):
        many = nz // 2

        def body(i, carry):
            rows = pl.ds(pl.multiple_of(i * many * group, many * group), many * group)
            value = jnp.dot(feat_t[rows], rhs, preferred_element_type=F32)
            for q in range(many):
                dest.mine[i * many + q] = value[q * group : (q + 1) * group].astype(dest.mine.dtype)
            return carry

        lax.fori_loop(0, 2, body, 0)

    def self_start():
        weight_product(grad[...], selfs)
        selfs.stage1()

    def author_start():
        def body(i, carry):
            rows = pl.ds(pl.multiple_of(i * hot_total // 2, hot_total // 2), hot_total // 2)
            value = jnp.dot(counts[rows], grad[...], preferred_element_type=F32) * (1.0 / HK)
            for q in range(nh // 2):
                authors.mine[i * (nh // 2) + q] = value[q * hot_rows : (q + 1) * hot_rows]
            return carry

        lax.fori_loop(0, 2, body, 0)
        authors.stage1()

    extras = [
        [self_start],
        [author_start],
        [selfs.stage2],
        [authors.stage2],
        [selfs.stage3, authors.stage3],
        [selfs.stage4],
        [authors.stage4],
        [authors.stage5],
    ]
    for item in b_exchange(half) + b_exchange(half - 1):
        item()
    for k in range(half, 0, -1):
        work = b_exchange(k - 2) if k >= 2 else []
        for group_of in extras[(half - k) * 8 // half : (half - k + 1) * 8 // half]:
            work += group_of
        if k == half:
            work += [functools.partial(f_done, half - 1), functools.partial(f_done, half)]
        if k + 2 <= half:
            work.append(functools.partial(b_done, k + 2))
        for zoff in offsets(k):
            b_arrive(zoff)
        if k == half:
            for i in range(few):
                for side in "rl":
                    b_pass(side, i).start()
            for item in work:
                item()
        elif k == last + 1:
            for d in range(NX):
                for side in "rl":
                    b_hand(side, d).start()
            for side in "rl":
                for i in range(few):
                    b_pass(side, i).wait_recv()
                b_onward(side).start()
            for item in work:
                item()
        else:
            if k == last:
                for side in "rl":
                    for d in range(NX):
                        b_hand(side, d).wait_recv()
                    b_onward(side).wait_recv()
            for s in range(SUBS):
                for side in "rl":
                    bufs = b_right if side == "r" else b_left
                    sources, others = [], ()
                    if k < last:
                        b_ring(side, k + 1, s).wait_recv()
                        sources = [bufs[k]]
                    else:
                        others = loose(side)
                    add_local(bufs[k], sources, s, k if side == "r" else nz - k, others)
                    b_ring(side, k, s).start()
                share_out(work, s)
    b_arrive(0)
    for s in range(SUBS):
        b_ring("r", 1, s).wait_recv()
        b_ring("l", 1, s).wait_recv()
        add_local(near, [b_right[0], b_left[0]], s, 0)
    weight_product(near[...].reshape(blocks * size, width), cites)
    cites.stage1()
    selfs.finish(self_out)
    authors.finish(author_out)
    for copy in ask_copies(False) + hot_copies(False) + near_copies(False):
        copy.wait_send()
    for k in (2, 1, 0):
        b_done(k)
    cites.stage2()
    selfs.drain()
    cites.stage3()
    authors.drain()
    cites.stage4()
    cites.finish(cite_out)
    cites.drain()


def layer(nz, nh, feat, w_cite, w_self, hot, ids, req, values, cotangent, used, target):
    half = nz // 2
    rows, din = feat.shape
    width = w_self.shape[1]
    size = values.shape[1]
    blocks = rows // size
    hot_total = hot.shape[0] * nh
    share = din // (nz * NX)
    vmem = pl.BlockSpec(memory_space=pltpu.VMEM)
    smem = pl.BlockSpec(memory_space=pltpu.SMEM)
    dma = pltpu.SemaphoreType.DMA
    chunk = pltpu.VMEM((blocks, size, width), BF16)
    column = pltpu.VMEM((NX - 1, nz, size, width), BF16)
    scratch = {
        "own": chunk,
        "packed": column,
        "table": pltpu.VMEM((hot_total, width), BF16),
        "asks": pltpu.VMEM((NX,) + req.shape, jnp.int32),
        "asked": pltpu.SMEM((NX,) + req.shape, jnp.int32),
        "arrived": pltpu.VMEM((nz, NX, size, width), BF16),
        "spread": pltpu.VMEM((2, rows, 2 * NX * size), BF16),
        "turned": pltpu.VMEM((nz, NX, size, size), BF16),
        "counts": pltpu.VMEM((hot_total, rows), BF16),
        "feat_t": pltpu.VMEM((din, rows), BF16),
        "base": pltpu.VMEM((rows, width), F32),
        "total": pltpu.VMEM((rows, width), F32),
        "degree": pltpu.VMEM((rows, size), F32),
        "inverse": pltpu.VMEM((rows, width), F32),
        "grad": pltpu.VMEM((rows, width), BF16),
        "scaled": chunk,
        "back": column,
        "came": column,
        "mine": pltpu.VMEM((nz, size, width), BF16),
        "near": chunk,
        "h_send": dma((nh - 1,)),
        "h_recv": dma((nh - 1,)),
        "q_send": dma((NX - 1,)),
        "q_recv": dma((NX - 1,)),
        "q_local": dma,
    }
    few = NX // 2
    several = pltpu.VMEM((NX + few, size, width), BF16)
    scratch["nears"] = pltpu.VMEM((4, NX) + req.shape, jnp.int32)
    scratch["nearby"] = pltpu.SMEM((4, NX) + req.shape, jnp.int32)
    scratch["n_send"] = dma((4,))
    scratch["n_recv"] = dma((4,))
    scratch["n_local"] = dma
    for side, word in (("r", "right"), ("l", "left")):
        for k in range(1, half - 1):
            scratch["f_%s%d" % (word, k)] = chunk
        for k in range(half - 1):
            scratch["b_%s%d" % (word, k)] = chunk
        for name in ("f_pack_", "f_next_", "b_next_"):
            scratch[name + side] = several
        for name in ("f_far_", "b_far_"):
            scratch[name + side] = pltpu.VMEM((few, size, width), BF16)
        for name, count in (("fh", 3), ("bp", few), ("bh", NX)):
            scratch[name + "s_" + side] = dma((count,))
            scratch[name + "r_" + side] = dma((count,))
        for name in ("fp", "bo"):
            scratch[name + "s_" + side] = dma
            scratch[name + "r_" + side] = dma
    for name in ("fs_r", "fr_r", "fs_l", "fr_l", "bs_r", "br_r", "bs_l", "br_l"):
        scratch[name] = dma((half - 2, SUBS))
    for name in ("fx_send", "fx_recv", "bx_send", "bx_recv"):
        scratch[name] = dma((NX - 1, nz))
    for name, parts in (
        ("self", WeightSum.scratch(nz, nh, share, width, F32)),
        ("cite", WeightSum.scratch(nz, nh, share, width, BF16)),
        ("author", AuthorSum.scratch(nz, nh, hot.shape[0], width)),
    ):
        for i, part in enumerate(parts):
            scratch[name + str(i)] = part
    names = ["in%d" % i for i in range(10)] + ["out%d" % i for i in range(4)] + list(scratch)
    return pl.pallas_call(
        functools.partial(layer_kernel, names, nz, nh),
        out_shape=(
            jax.ShapeDtypeStruct((rows, width), BF16),
            jax.ShapeDtypeStruct((share, width), F32),
            jax.ShapeDtypeStruct((share, width), F32),
            jax.ShapeDtypeStruct(hot.shape, F32),
        ),
        in_specs=[vmem] * 8 + [smem] * 2,
        out_specs=(vmem,) * 4,
        scratch_shapes=list(scratch.values()),
        compiler_params=pltpu.CompilerParams(
            collective_id=1, has_side_effects=True, vmem_limit_bytes=VMEM_LIMIT
        ),
    )(feat, w_cite, w_self, hot, ids, req, values, cotangent, used, target)


def hand_over_kernel(*refs):
    half = len(refs) // 2
    for src, dst in zip(refs[:half], refs[half:]):
        dst[...] = src[...]


def hand_over(arrays):
    vmem = pl.BlockSpec(memory_space=pltpu.VMEM)
    return pl.pallas_call(
        hand_over_kernel,
        out_shape=tuple(jax.ShapeDtypeStruct(a.shape, a.dtype) for a in arrays),
        in_specs=[vmem] * len(arrays),
        out_specs=(vmem,) * len(arrays),
    )(*arrays)


def on_device(
    paper_features,
    self_weight,
    cite_weight,
    hot_embed,
    hot_ids,
    tile_values,
    tile_rows,
    tile_target_block,
    tile_block,
    tile_owner,
    cotangent,
):
    wide = lax.axis_size("wide")
    nh = lax.axis_size("hot")
    nz = wide // NX
    tiles = tile_values.shape[0]
    shape = (8, tiles, max(128, wide))
    what = jnp.where(
        lax.broadcasted_iota(jnp.int32, shape, 0) == 0,
        tile_block[None, :, None],
        lax.broadcasted_iota(jnp.int32, shape, 1),
    )
    owned = tile_owner[None, :, None] == lax.broadcasted_iota(jnp.int32, shape, 2)
    req = jnp.max(jnp.where(owned, what, -1), axis=1)
    return hand_over(
        layer(
            nz,
            nh,
            paper_features,
            cite_weight,
            self_weight,
            hot_embed,
            hot_ids.T,
            req,
            tile_values,
            cotangent,
            tile_rows,
            tile_target_block,
        )
    )


def solution(mesh):
    return jax.shard_map(
        on_device,
        mesh=mesh,
        in_specs=(
            P(("wide", "hot"), None),
            P(),
            P(),
            P("hot", None),
            P(("wide", "hot"), None),
            P(("wide", "hot"), None, None),
            P(("wide", "hot")),
            P(("wide", "hot")),
            P(("wide", "hot")),
            P(("wide", "hot")),
            P(("wide", "hot"), None),
        ),
        out_specs=(P(("wide", "hot"), None), P("wide", None), P("wide", None), P("hot", None)),
        check_vma=False,
    )
```
